32 devices in a mesh: dp: 4 (over y, x), blk: 8 (over z, core).
Axes of the slice: x: 2, y: 2, z: 4, core: 2. Of those that a mesh axis runs over, the one named last changes fastest.
Arguments:
- inputs: bfloat16 [8, 2048, 768], P('dp', 'blk'), may hold values from -6 to 6
- cotangent: bfloat16 [8, 2048, 768], P('dp', 'blk'), may hold values from -6 to 6
- lengths: int32 [8, 4], P('dp'), may hold values from 1 to 1920, 2048 in all within a row
- view_counts: int32 [8, 4], P('dp'), may hold values from 1 to 2
- padding: int32 [8, 2048], P('dp'), may hold values 0 or 1
- first_gain: float32 [768], replicated, may hold values from 0.5 to 1.5
- query_weight: bfloat16 [768, 768], replicated, may hold values from -0.4375 to 0.4375
- key_value_weight: bfloat16 [768, 1536], replicated, may hold values from -0.21875 to 0.21875
- output_weight: bfloat16 [768, 768], replicated, may hold values from -1.75 to 1.75
- second_gain: float32 [768], replicated, may hold values from 0.5 to 1.5
- expand_weight: bfloat16 [768, 3072], replicated, may hold values from -0.21875 to 0.21875
- contract_weight: bfloat16 [3072, 768], replicated, may hold values from -0.109375 to 0.109375
Outputs:
- result: bfloat16 [8, 2048, 768], P('dp', 'blk')
- grad_inputs: bfloat16 [8, 2048, 768], P('dp', 'blk')
- grad_first_gain: float32 [768], replicated
- grad_query_weight: float32 [768, 768], replicated
- grad_key_value_weight: float32 [768, 1536], replicated
- grad_output_weight: float32 [768, 768], replicated
- grad_second_gain: float32 [768], replicated
- grad_expand_weight: float32 [768, 3072], replicated
- grad_contract_weight: float32 [3072, 768], replicated
The draws below stay inside these ranges and needn't reach their ends.
Inputs may be any that keep to these rules, and one draw needn't show every extreme that they name: Each row's 4 item lengths add up to 2048, and its longest item has exactly 1920 tokens.
All inputs are finite; a program needn't handle non-finite values. No bound on the sum of `padding` on one device may be relied on, other than what follows from the above.
Results may differ from the reference program's by a relative error of at most 0.017.
Values may be sent and summed in bfloat16 or wider, within the bound.
A program may use at most 256 MiB of HBM per device.

```python
import math
import jax
import jax.numpy as jnp
import numpy as np
from jax import lax

D = 768
HEADS = 12
HEAD = 64
FF = 3072
ROWS = 256
ITEMS = 4
PATCHES = 64
SEQ = 2048
BATCH = 8


def with_ends(entries, stream_key, least, high):
    extent = entries.shape
    spot = [jax.random.randint(jax.random.fold_in(stream_key, axis), (), 0, extent[axis]) for axis in range(len(extent))]
    entries = entries.at[tuple(spot)].set(least)
    longest = extent.index(max(extent))
    spot[longest] = (spot[longest] + 1) % extent[longest]
    return entries.at[tuple(spot)].set(high)


def shard_levels(stream_key, extent, shards, smallest, top_value):
    def one(dim, shards_of):
        draws = jax.random.uniform(jax.random.fold_in(jax.random.fold_in(stream_key, 6), dim), (shards_of,), jnp.float32, smallest / len(shards), top_value / len(shards))
        return jnp.repeat(jnp.exp(draws), extent[dim] // shards_of).reshape((-1,) + (1,) * (len(extent) - dim - 1))

    factor_of = one(*shards[0])
    for cut in shards[1:]:
        factor_of = factor_of * one(*cut)
    return factor_of


def profile(count, total, reach, slope):
    loads = [(1 << 20) // math.isqrt(rank ** slope) + 1 for rank in range(2, count + 1)]
    spare, given = total - reach - (count - 1), [1] * (count - 1)
    while spare > 0:
        free = [i for i in range(count - 1) if given[i] < reach]
        pool, remaining = sum([loads[i] for i in free]), spare
        for i in free:
            addition = min(reach - given[i], max(1, remaining * loads[i] // pool), spare)
            given[i] = given[i] + addition
            spare = spare - addition
    return np.array([reach] + given)


def uneven(rng, number_of, total, reach, slope):
    if number_of == 2:
        one = jax.random.randint(rng, (), max(1, total - reach), min(reach, total - 1) + 1)
        return jnp.stack([one, total - one])
    sizes = jnp.asarray(profile(number_of, total, reach, slope), jnp.int32)
    couples = (number_of - 1) // 2
    giver, sink = sizes[1:1 + 2 * couples:2], sizes[2:2 + 2 * couples:2]
    margin = jnp.minimum(giver - 1, reach - sink)
    moved = jax.random.randint(jax.random.fold_in(rng, 1), (couples,), 0, 1 << 20) % (margin + 1)
    sizes = sizes.at[1:1 + 2 * couples:2].set(giver - moved).at[2:2 + 2 * couples:2].set(sink + moved)
    return sizes[jax.random.permutation(jax.random.fold_in(rng, 2), number_of)]


def scatter_about(own_key, dims, deviation, limit, shards=(), kind=jnp.bfloat16):
    result = jax.random.normal(own_key, dims, jnp.float32) * deviation
    if len(shards) > 0:
        result = shard_levels(own_key, dims, shards, -0.22, 0.18) * result
    return jnp.clip(result, min=-limit, max=limit).astype(kind)


def setup_inputs(seed: int = 0) -> dict:
    key_of = jax.random.split(jax.random.key(seed), 13)
    return {
        "inputs": scatter_about(key_of[0], (BATCH, SEQ, D), 1.0, 6.0, ((0, 4), (1, 8))),
        "cotangent": scatter_about(key_of[1], (BATCH, SEQ, D), 1.0, 6.0, ((0, 4), (1, 8))),
        "lengths": jax.vmap(lambda own: uneven(own, ITEMS, SEQ, SEQ - ROWS // 2, 2))(jax.random.split(key_of[2], BATCH)).reshape((BATCH, ITEMS)).astype(jnp.int32),
        "view_counts": with_ends(jax.random.randint(key_of[3], (BATCH, ITEMS), 1, 3), jax.random.fold_in(key_of[3], 1), 1, 2).astype(jnp.int32),
        "padding": with_ends((jax.random.randint(key_of[4], (BATCH, SEQ), 0, 8) < 7).astype(jnp.int32), jax.random.fold_in(key_of[4], 1), 0, 1),
        "first_gain": jnp.clip(1.0 + 0.1 * jax.random.normal(key_of[5], (D,), jnp.float32), 0.5, 1.5),
        "query_weight": scatter_about(key_of[6], (D, D), (D // 4) ** -0.5, 0.4375),
        "key_value_weight": scatter_about(key_of[7], (D, 2 * D), D ** -0.5, 0.21875),
        "output_weight": scatter_about(key_of[8], (D, D), (max(D // 64, 4)) ** -0.5, 1.75),
        "second_gain": jnp.clip(1.0 + 0.1 * jax.random.normal(key_of[9], (D,), jnp.float32), 0.5, 1.5),
        "expand_weight": scatter_about(key_of[10], (D, FF), D ** -0.5, 0.21875),
        "contract_weight": scatter_about(key_of[11], (FF, D), FF ** -0.5, 0.109375),
    }


@jax.custom_vjp
def low(v):
    return lax.optimization_barrier(v.astype(jnp.bfloat16)).astype(jnp.float32)

@jax.custom_vjp
def low_back(v):
    return v

def low_keep(v):
    return (low(v), None)

def low_pass(kept, grad):
    return (grad,)

def back_keep(v):
    return (v, None)

def back_low(kept, grad):
    return (low(grad),)
low.defvjp(low_keep, low_pass)
low_back.defvjp(back_keep, back_low)
epsilon = 1e-05
lowest = -1e+30
highest = lax.Precision.HIGHEST

def layer_norm(value, gain):
    mean = lax.optimization_barrier(jnp.mean(value, -1, keepdims=True))
    centred = value - mean
    spread = lax.optimization_barrier(jnp.mean(centred * centred, -1, keepdims=True))
    return centred * lax.rsqrt(spread + epsilon) * gain

def token_info(lengths, views, positions):
    ends = jnp.cumsum(lengths).astype(jnp.int32)
    starts = (ends - lengths).astype(jnp.int32)
    inside = (positions[:, None] >= starts[None, :]) & (positions[:, None] < ends[None, :])
    number = jnp.arange(lengths.shape[0], dtype=jnp.int32)
    item = lax.optimization_barrier(jnp.sum(jnp.where(inside, number[None, :], 0), 1)).astype(jnp.int32)
    first = lax.optimization_barrier(jnp.sum(jnp.where(inside, starts[None, :], 0), 1)).astype(jnp.int32)
    span = lax.optimization_barrier(jnp.sum(jnp.where(inside, views[None, :], 0), 1)).astype(jnp.int32) * PATCHES
    frame = ((positions - first) // span).astype(jnp.int32)
    return (item, frame)

def visible(query_pos, query_item, query_frame, key_pos, key_item, key_frame, key_pad):
    same = query_item[:, None] == key_item[None, :]
    order = key_frame[None, :] <= query_frame[:, None]
    usable = (key_pad[None, :] == 1) | (query_pos[:, None] == key_pos[None, :])
    return same & order & usable

def attend(query, keys, values, item, frame, padding):
    block_rows = min(512, SEQ)
    count = SEQ // block_rows
    positions = jnp.arange(SEQ, dtype=jnp.int32)
    key_heads = keys.reshape(SEQ, HEADS, HEAD)
    value_heads = values.reshape(SEQ, HEADS, HEAD)
    blocks = (query.reshape(count, block_rows, HEADS, HEAD), positions.reshape(count, block_rows), item.reshape(count, block_rows), frame.reshape(count, block_rows))

    @jax.checkpoint
    def one_block(args):
        block_query, block_pos, block_item, block_frame = args
        scores = jnp.einsum('qhd,khd->hqk', block_query, key_heads, precision=highest) * HEAD ** (-0.5)
        scores = low_back(scores)
        mask = visible(block_pos, block_item, block_frame, positions, item, frame, padding)[None]
        peak = lax.optimization_barrier(jnp.max(jnp.where(mask, scores, lowest), -1, keepdims=True))
        raised = jnp.where(mask, jnp.exp(scores - peak), 0.0)
        weights = low(raised / lax.optimization_barrier(jnp.sum(raised, -1, keepdims=True)))
        mixed = jnp.einsum('hqk,khd->qhd', weights, value_heads, precision=highest)
        return mixed.reshape(block_rows, D)
    return lax.map(one_block, blocks).reshape(SEQ, D)

def forward(row_input, weights, item, frame, padding):
    first_gain, query_weight, key_value_weight, output_weight, second_gain, expand_weight, contract_weight = weights
    normed = low(layer_norm(row_input, first_gain))
    query = low_back(low(jnp.dot(normed, query_weight, precision=highest)))
    pair = low_back(low(jnp.dot(normed, key_value_weight, precision=highest)))
    attended = attend(query, pair[:, :D], pair[:, D:], item, frame, padding)
    attended = low_back(low(attended))
    branch = low_back(jnp.dot(attended, output_weight, precision=highest))
    mixed = row_input + branch
    second = low(layer_norm(mixed, second_gain))
    hidden = low_back(jnp.dot(second, expand_weight, precision=highest))
    activated = low(jax.nn.gelu(hidden, approximate=True))
    return mixed + jnp.dot(activated, contract_weight, precision=highest)

def reference(inputs, cotangent, lengths, view_counts, padding, first_gain, query_weight, key_value_weight, output_weight, second_gain, expand_weight, contract_weight):
    params = tuple((array.astype(jnp.float32) for array in (first_gain, query_weight, key_value_weight, output_weight, second_gain, expand_weight, contract_weight)))
    positions = jnp.arange(SEQ, dtype=jnp.int32)

    def one_row(totals, row):
        row_input, row_cot, row_lengths, row_views, row_pad = row
        item, frame = token_info(row_lengths, row_views, positions)

        def run(values, *weights):
            return forward(values, weights, item, frame, row_pad)
        output, pull = jax.vjp(run, row_input.astype(jnp.float32), *params)
        grads = pull(row_cot.astype(jnp.float32))
        totals = tuple((total + grad for total, grad in zip(totals, grads[1:])))
        return (totals, (output.astype(jnp.bfloat16), grads[0].astype(jnp.bfloat16)))
    initial = tuple((jnp.zeros(array.shape, jnp.float32) for array in params))
    totals, (outputs, input_grads) = lax.scan(one_row, initial, (inputs, cotangent, lengths, view_counts, padding))
    return (outputs, input_grads, totals[0], totals[1], totals[2], totals[3], totals[4], totals[5], totals[6])
```

```python
from functools import partial

import jax
import jax.numpy as jnp
from jax import lax
from jax.experimental import pallas as pl
from jax.experimental.pallas import tpu as pltpu
from jax.sharding import PartitionSpec as P

HEAD = 64
PATCHES = 64
CODES = 40
BIG = 1e30
LANES = 128
MESH = pl.DeviceIdType.MESH
bf16 = jnp.bfloat16
f32 = jnp.float32

epsilon = 1e-05
lowest = -1e30


def dot_nn(a, b):
    return lax.dot_general(a, b, (((1,), (0,)), ((), ())), preferred_element_type=f32)


def dot_nt(a, b):
    return lax.dot_general(a, b, (((1,), (1,)), ((), ())), preferred_element_type=f32)


def dot_tn(a, b):
    return lax.dot_general(a, b, (((0,), (0,)), ((), ())), preferred_element_type=f32)


def chip_order(z, step):
    code = jnp.where(z == 0, 3210, jnp.where(z == 1, 3201, jnp.where(z == 2, 312, 123)))
    return lax.rem(code // jnp.where(step == 0, 1, jnp.where(step == 1, 10, jnp.where(step == 2, 100, 1000))), 10)


def far_order(z, step):
    return jnp.where(
        step == 0,
        lax.rem(z + 2, 4),
        jnp.where(step == 1, 3 - z, jnp.where(step == 2, z + 1 - 2 * lax.rem(z, 2), z)),
    )


def features(block, rows, lengths, views, row, padded):
    lane = lax.broadcasted_iota(jnp.int32, (rows, LANES), 1) - HEAD
    position = block * rows + lax.broadcasted_iota(jnp.int32, (rows, LANES), 0)
    code = jnp.zeros((rows, LANES), jnp.int32)
    base = jnp.zeros((rows, LANES), jnp.int32)
    start = jnp.int32(0)
    first = jnp.int32(0)
    for item in range(lengths.shape[1]):
        length = lengths[row, item]
        view = views[row, item]
        offset = position - start
        inside = (offset >= 0) & (offset < length)
        frame = (offset >> 6) * (2 - view) + (offset >> 7) * (view - 1)
        code = jnp.where(inside, first + frame, code)
        base = jnp.where(inside, first, base)
        first = first + ((length + 63) >> 6) * (2 - view) + ((length + 127) >> 7) * (view - 1)
        start = start + length
    coded = (lane >= 0) & (lane < CODES)
    key = jnp.where(coded & (lane == code), 1.0, 0.0)
    key = jnp.where((lane > CODES) & (lane < CODES + 4), 1.0, key)
    key = jnp.where(lane == CODES, padded, key)
    hidden = (coded & ((lane < base) | (lane > code))) | (lane == CODES)
    query = jnp.where(hidden, -BIG, 0.0)
    return key, query


def three_parts(value):
    high = value.astype(bf16).astype(f32)
    rest = value - high
    middle = rest.astype(bf16).astype(f32)
    low = (rest - middle).astype(bf16).astype(f32)
    return high, middle, low


def spread(value, first, lane):
    high, middle, low = three_parts(value)
    return jnp.where(
        lane == first, high, jnp.where(lane == first + 1, middle, jnp.where(lane == first + 2, low, 0.0))
    )


def pack_heads(heads):
    half = heads[2].shape[0] // 2
    wide = jnp.concatenate([heads[0], heads[1]], 1)
    narrow = jnp.concatenate([heads[2][:half], heads[2][half:]], 1)
    return wide, narrow


def greet_line(dp, me, count):
    barrier = pltpu.get_barrier_semaphore()
    for step in range(1, count):
        pl.semaphore_signal(
            barrier, inc=1, device_id=(dp, lax.rem(me + step, count)), device_id_type=MESH
        )
    pl.semaphore_wait(barrier, count - 1)


def forward_kernel(
    lengths, views, x_ref, gain_ref, pad_ref, wq_ref, wkv_ref,
    normed, qa, ka, va, o_ref, received,
    weight, stage, scores, tail, peak, acc, outgoing,
    sib_send, sib_recv, line_send, line_recv, out_send, out_recv,
):
    rows, width = x_ref.shape[1], x_ref.shape[2]
    blocks = normed.shape[0]
    heads = qa.shape[0]
    dp = lax.axis_index("dp")
    me = lax.axis_index("blk")
    z = me // 2
    core = lax.rem(me, 2)
    sibling = me + 1 - 2 * core
    lane = lax.broadcasted_iota(jnp.int32, (rows, LANES), 1)

    greet_line(dp, me, blocks)

    def norm(value):
        value = value.astype(f32)
        mean = jnp.mean(value, -1, keepdims=True)
        centred = value - mean
        var = jnp.mean(centred * centred, -1, keepdims=True)
        return (centred * lax.rsqrt(var + epsilon) * gain_ref[...]).astype(bf16)

    normed[me] = norm(x_ref[core])

    def line_copy(block, up):
        return pltpu.make_async_remote_copy(
            src_ref=normed.at[block],
            dst_ref=normed.at[block],
            send_sem=line_send.at[block, up],
            recv_sem=line_recv.at[block],
            device_id=(dp, me + (2 if up else -2)),
            device_id_type=MESH,
        )

    @pl.when(z < 3)
    def _():
        line_copy(me, 1).start()

    @pl.when(z > 0)
    def _():
        line_copy(me, 0).start()

    stage[...] = norm(x_ref[1 - core])
    sib_copy = pltpu.make_async_remote_copy(
        src_ref=stage,
        dst_ref=normed.at[me],
        send_sem=sib_send,
        recv_sem=sib_recv,
        device_id=(dp, sibling),
        device_id_type=MESH,
    )
    sib_copy.start()

    gap = jnp.zeros((width, LANES - HEAD), bf16)
    for chip in range(blocks // 2):

        @pl.when(z == chip)
        def _():
            for head in range(heads):
                at = (chip * heads + head) * HEAD
                for kind, piece in enumerate(
                    (
                        wq_ref[:, at : at + HEAD],
                        wkv_ref[:, at : at + HEAD],
                        wkv_ref[:, width + at : width + at + HEAD],
                    )
                ):
                    column = (head * 3 + kind) * LANES
                    weight[:, column : column + LANES] = jnp.concatenate([piece, gap], 1)

    ones = jnp.where((lane >= HEAD) & (lane < HEAD + 3), -1.0, 0.0)

    @pl.loop(0, blocks)
    def _(step):
        chip = chip_order(z, step // 2)
        block = 2 * chip + lax.rem(core + step, 2)

        @pl.when(step == 1)
        def _():
            pltpu.make_async_remote_copy(
                src_ref=stage,
                dst_ref=normed.at[sibling],
                send_sem=sib_send,
                recv_sem=sib_recv,
                device_id=(dp, sibling),
                device_id_type=MESH,
            ).wait_recv()

        @pl.when(step > 1)
        def _():
            pltpu.make_async_remote_copy(
                src_ref=normed.at[block],
                dst_ref=normed.at[block],
                send_sem=line_send.at[block, 0],
                recv_sem=line_recv.at[block],
                device_id=(dp, sibling),
                device_id_type=MESH,
            ).wait_recv()

        @pl.when((step > 0) & (chip <= z) & (z < 3))
        def _():
            line_copy(block, 1).start()

        @pl.when((step > 0) & (chip >= z) & (z > 0))
        def _():
            line_copy(block, 0).start()

        pad_row = 1.0 - pad_ref[core, pl.ds(block, 1), :].astype(f32)
        padded = jnp.transpose(jnp.broadcast_to(pad_row, (LANES, rows)))
        key, query = features(block, rows, lengths, views, core, padded)
        out = dot_nn(normed[block], weight[...]).astype(bf16).astype(f32)
        here = pl.ds(pl.multiple_of(block * rows, rows), rows)
        for head in range(heads):
            at = head * 3 * LANES
            qa[head, here, :] = (out[:, at : at + LANES] * (HEAD**-0.5) + query).astype(bf16)
            ka[head, here, :] = (out[:, at + LANES : at + 2 * LANES] + key).astype(bf16)
            va[head, here, :] = (out[:, at + 2 * LANES : at + 3 * LANES] + ones).astype(bf16)

    eye = lax.broadcasted_iota(jnp.int32, (rows, rows), 0) == lax.broadcasted_iota(
        jnp.int32, (rows, rows), 1
    )
    half = LANES

    def out_copy(block):
        return pltpu.make_async_remote_copy(
            src_ref=outgoing.at[block],
            dst_ref=received.at[me],
            send_sem=out_send.at[block],
            recv_sem=out_recv.at[me],
            device_id=(dp, block),
            device_id_type=MESH,
        )

    @pl.loop(0, blocks)
    def _(step):
        block = 2 * far_order(z, step // 2) + lax.rem(core + step, 2)
        here = pl.ds(pl.multiple_of(block * rows, rows), rows)
        last = block == blocks - 1
        beyond = jnp.where(last, blocks * rows - half, (block + 1) * rows)
        beyond = pl.ds(pl.multiple_of(beyond, half), half)
        shut = jnp.where(last, -BIG, 0.0)
        for head in range(heads):
            query = qa[head, here, :]
            s = dot_nt(query, ka[head, here, :])
            plain = dot_nt(query[:, :HEAD], ka[head, here, :HEAD])
            s = jnp.where(eye, plain, s)
            t = dot_nt(query, ka[head, beyond, :]) + shut
            scores[block, head] = s
            tail[head] = t
            peak[head] = jnp.maximum(jnp.maximum(s[:, :LANES], s[:, LANES:]), t)

        @pl.loop(0, block)
        def _(other):
            there = pl.ds(pl.multiple_of(other * rows, rows), rows)
            for head in range(heads):
                s = dot_nt(qa[head, here, :], ka[head, there, :])
                scores[other, head] = s
                peak[head] = jnp.maximum(peak[head], jnp.maximum(s[:, :LANES], s[:, LANES:]))

        for head in range(heads):
            top = jnp.max(peak[head], -1, keepdims=True)
            peak[head] = jnp.broadcast_to(top, (rows, LANES))
            p = jnp.exp(tail[head] - top).astype(bf16)
            acc[head] = dot_nn(p, va[head, beyond, :])

        @pl.loop(0, block + 1)
        def _(other):
            there = pl.ds(pl.multiple_of(other * rows, rows), rows)
            for head in range(heads):
                top = peak[head]
                s = scores[other, head]
                p = jnp.concatenate(
                    [jnp.exp(s[:, :LANES] - top), jnp.exp(s[:, LANES:] - top)], 1
                ).astype(bf16)
                acc[head] += dot_nn(p, va[head, there, :])

        results = []
        for head in range(heads):
            total = acc[head]
            mass = -total[:, HEAD : HEAD + 1]
            out = total / mass
            o_ref[head, here, :] = out
            results.append(out[:, :HEAD].astype(bf16))
            log_total = peak[head] + jnp.log(mass)
            qa[head, here, :] = (
                qa[head, here, :].astype(f32) - spread(log_total, HEAD + CODES + 1, lane)
            ).astype(bf16)
        wide, narrow = pack_heads(results)

        @pl.when(block == me)
        def _():
            received[me, :rows, :] = wide
            received[me, rows:, :] = narrow

        @pl.when(block != me)
        def _():
            outgoing[block, :rows, :] = wide
            outgoing[block, rows:, :] = narrow
            out_copy(block).start()

    sib_copy.wait_send()

    @pl.loop(0, blocks)
    def _(block):
        @pl.when((block // 2 <= z) & (z < 3))
        def _():
            line_copy(block, 1).wait_send()

        @pl.when((block // 2 >= z) & (z > 0))
        def _():
            line_copy(block, 0).wait_send()

        @pl.when(block != me)
        def _():
            out_copy(block).wait_send()
            pltpu.make_async_remote_copy(
                src_ref=outgoing.at[block],
                dst_ref=received.at[block],
                send_sem=out_send.at[block],
                recv_sem=out_recv.at[block],
                device_id=(dp, block),
                device_id_type=MESH,
            ).wait_recv()


def backward_kernel(
    grad_ref, normed, qa, ka, va, o_ref,
    got_query, got_pair, grad_weight,
    outgoing, received, doa, dq, dk, dv, mine, send_query, send_pair,
    out_send, out_recv, query_send, query_recv, pair_send, pair_recv,
):
    rows, width = grad_ref.shape[1], grad_ref.shape[2]
    blocks = normed.shape[0]
    heads = qa.shape[0]
    dp = lax.axis_index("dp")
    me = lax.axis_index("blk")
    z = me // 2
    core = lax.rem(me, 2)
    lane = lax.broadcasted_iota(jnp.int32, (rows, LANES), 1)
    greet_line(dp, me, blocks)

    def send(kind, block):
        src, dst, send_sem, recv_sem = {
            "grad": (outgoing, received, out_send, out_recv),
            "query": (send_query, got_query, query_send, query_recv),
            "pair": (send_pair, got_pair, pair_send, pair_recv),
        }[kind]
        return pltpu.make_async_remote_copy(
            src_ref=src.at[block],
            dst_ref=dst.at[me],
            send_sem=send_sem.at[block],
            recv_sem=recv_sem.at[me],
            device_id=(dp, block),
            device_id_type=MESH,
        )

    def arrive(kind, block):
        src, dst, send_sem, recv_sem = {
            "grad": (outgoing, received, out_send, out_recv),
            "query": (send_query, got_query, query_send, query_recv),
            "pair": (send_pair, got_pair, pair_send, pair_recv),
        }[kind]
        return pltpu.make_async_remote_copy(
            src_ref=src.at[block],
            dst_ref=dst.at[block],
            send_sem=send_sem.at[block],
            recv_sem=recv_sem.at[block],
            device_id=(dp, block),
            device_id_type=MESH,
        )

    for chip in range(blocks // 2):
        for row in range(2):
            at = chip * heads * HEAD
            wide, narrow = pack_heads(
                [grad_ref[row, :, at + h * HEAD : at + (h + 1) * HEAD] for h in range(heads)]
            )
            outgoing[2 * chip + row, :rows, :] = wide
            outgoing[2 * chip + row, rows:, :] = narrow

    for step in range(4):
        for row in range(2):
            block = 2 * far_order(z, jnp.int32(step)) + row

            @pl.when(block != me)
            def _():
                send("grad", block).start()

    received[me] = outgoing[me]

    @pl.loop(0, blocks)
    def _(step):
        block = 2 * chip_order(z, step // 2) + lax.rem(core + step, 2)

        @pl.when(block != me)
        def _():
            arrive("grad", block).wait_recv()

        here = pl.ds(pl.multiple_of(block * rows, rows), rows)
        wide = received[block, :rows, :].astype(f32)
        narrow = received[block, rows:, :].astype(f32)
        pieces = [
            wide[:, :HEAD],
            wide[:, HEAD:],
            jnp.concatenate([narrow[:, :HEAD], narrow[:, HEAD:]], 0),
        ]
        gap = jnp.zeros((rows, LANES - HEAD), f32)
        for head in range(heads):
            value = jnp.concatenate([pieces[head], gap], 1)
            delta = jnp.sum(value * o_ref[head, here, :], -1, keepdims=True)
            doa[head, here, :] = (value + spread(delta, HEAD, lane)).astype(bf16)
            dq[head, here, :] = jnp.zeros((rows, LANES), f32)

    eye = lax.broadcasted_iota(jnp.int32, (rows, rows), 0) == lax.broadcasted_iota(
        jnp.int32, (rows, rows), 1
    )
    bare = (lane < HEAD) | (lane > HEAD + CODES)
    half = LANES

    def pull(head, keys, queries, diagonal, first):
        k = ka[head, keys, :]
        q = qa[head, queries, :]
        g = doa[head, queries, :]
        s = dot_nt(k, q)
        if diagonal:
            s = jnp.where(eye, dot_nt(jnp.where(bare, k, 0.0).astype(bf16), q), s)
        p = jnp.exp(s)
        ds = (p * dot_nt(va[head, keys, :], g)).astype(bf16)
        p = p.astype(bf16)
        count = k.shape[0]
        if first:
            dv[head] = dot_nn(p, g)
            dk[head] = dot_nn(ds, q)
        else:
            dv[head, :count] += dot_nn(p, g)
            dk[head, :count] += dot_nn(ds, q)
        dq[head, queries, :] += dot_tn(ds, k)

    @pl.loop(0, blocks)
    def _(step):
        block = jnp.where(lax.rem(step, 2) == 0, step // 2, blocks - 1 - step // 2)
        here = pl.ds(pl.multiple_of(block * rows, rows), rows)
        for head in range(heads):
            pull(head, here, here, True, True)

        @pl.loop(block + 1, blocks)
        def _(other):
            there = pl.ds(pl.multiple_of(other * rows, rows), rows)
            for head in range(heads):
                pull(head, here, there, False, False)

        @pl.when(block > 0)
        def _():
            keys = pl.ds(pl.multiple_of(block * rows, rows), half)
            queries = pl.ds(pl.multiple_of(block * rows - half, half), half)
            for head in range(heads):
                pull(head, keys, queries, False, False)

        for head in range(heads):
            mine[head, here, :] = jnp.concatenate(
                [dk[head][:, :HEAD], dv[head][:, :HEAD]], 1
            ).astype(bf16)

        @pl.when(block == me)
        def _():
            for head in range(heads):
                got_pair[me, head * rows : (head + 1) * rows, :] = mine[head, here, :]

        @pl.when(block != me)
        def _():
            for head in range(heads):
                send_pair[block, head * rows : (head + 1) * rows, :] = mine[head, here, :]
            send("pair", block).start()

    @pl.loop(0, blocks)
    def _(step):
        block = 2 * far_order(z, step // 2) + lax.rem(core + step, 2)
        here = pl.ds(pl.multiple_of(block * rows, rows), rows)
        parts = [(dq[h, here, :][:, :HEAD] * (HEAD**-0.5)).astype(bf16) for h in range(heads)]
        wide, narrow = pack_heads(parts)
        mine[heads, here, :] = wide
        mine[heads + 1, here, :] = jnp.concatenate(
            [parts[2], jnp.zeros((rows, LANES - HEAD), bf16)], 1
        )

        @pl.when(block == me)
        def _():
            got_query[me, :rows, :] = wide
            got_query[me, rows:, :] = narrow

        @pl.when(block != me)
        def _():
            send_query[block, :rows, :] = wide
            send_query[block, rows:, :] = narrow
            send("query", block).start()

    for tile in range(heads + 2):
        grad_weight[:, tile * LANES : (tile + 1) * LANES] = jnp.zeros((width, LANES), f32)

    @pl.loop(0, blocks)
    def _(block):
        here = pl.ds(pl.multiple_of(block * rows, rows), rows)
        right = jnp.concatenate([mine[tile, here, :] for tile in range(heads + 2)], 1)
        grad_weight[...] += dot_tn(normed[block], right)

    @pl.loop(0, blocks)
    def _(block):
        @pl.when(block != me)
        def _():
            send("grad", block).wait_send()
            send("query", block).wait_send()
            send("pair", block).wait_send()
            arrive("query", block).wait_recv()
            arrive("pair", block).wait_recv()


VMEM = pl.BlockSpec(memory_space=pltpu.VMEM)
SMEM = pl.BlockSpec(memory_space=pltpu.SMEM)


def attention_forward(inputs, gain, lengths, views, padding, query_weight, pair_weight, blocks):
    micro, rows, width = inputs.shape
    total = rows * blocks
    heads = width // HEAD // (blocks // micro)
    packed = rows * heads // 2
    shape = jax.ShapeDtypeStruct
    dma = pltpu.SemaphoreType.DMA
    return pl.pallas_call(
        forward_kernel,
        out_shape=(
            shape((blocks, rows, width), bf16),
            shape((heads, total, LANES), bf16),
            shape((heads, total, LANES), bf16),
            shape((heads, total, LANES), bf16),
            shape((heads, total, LANES), f32),
            shape((blocks, packed, LANES), bf16),
        ),
        in_specs=[SMEM, SMEM] + [VMEM] * 5,
        out_specs=(VMEM,) * 6,
        scratch_shapes=[
            pltpu.VMEM((width, heads * 3 * LANES), bf16),
            pltpu.VMEM((rows, width), bf16),
            pltpu.VMEM((blocks, heads, rows, rows), f32),
            pltpu.VMEM((heads, rows, LANES), f32),
            pltpu.VMEM((heads, rows, LANES), f32),
            pltpu.VMEM((heads, rows, LANES), f32),
            pltpu.VMEM((blocks, packed, LANES), bf16),
            dma,
            dma,
            dma((blocks, 2)),
            dma((blocks,)),
            dma((blocks,)),
            dma((blocks,)),
        ],
        compiler_params=pltpu.CompilerParams(
            collective_id=0, has_side_effects=True, vmem_limit_bytes=60 << 20
        ),
        name="attention_forward",
    )(lengths, views, inputs, gain.reshape(1, width), padding.reshape(micro, blocks, rows), query_weight, pair_weight)


def attention_backward(grad, normed, qa, ka, va, out):
    micro, rows, width = grad.shape
    blocks = normed.shape[0]
    heads, total, _ = qa.shape
    packed = rows * heads // 2
    shape = jax.ShapeDtypeStruct
    dma = pltpu.SemaphoreType.DMA
    return pl.pallas_call(
        backward_kernel,
        out_shape=(
            shape((blocks, packed, LANES), bf16),
            shape((blocks, heads * rows, LANES), bf16),
            shape((width, (heads + 2) * LANES), f32),
        ),
        in_specs=[VMEM] * 6,
        out_specs=(VMEM,) * 3,
        scratch_shapes=[
            pltpu.VMEM((blocks, packed, LANES), bf16),
            pltpu.VMEM((blocks, packed, LANES), bf16),
            pltpu.VMEM((heads, total, LANES), bf16),
            pltpu.VMEM((heads, total, LANES), f32),
            pltpu.VMEM((heads, rows, LANES), f32),
            pltpu.VMEM((heads, rows, LANES), f32),
            pltpu.VMEM((heads + 2, total, LANES), bf16),
            pltpu.VMEM((blocks, packed, LANES), bf16),
            pltpu.VMEM((blocks, heads * rows, LANES), bf16),
            dma((blocks,)),
            dma((blocks,)),
            dma((blocks,)),
            dma((blocks,)),
            dma((blocks,)),
            dma((blocks,)),
        ],
        compiler_params=pltpu.CompilerParams(
            collective_id=1, has_side_effects=True, vmem_limit_bytes=60 << 20
        ),
        name="attention_backward",
    )(grad, normed, qa, ka, va, out)


def unpack_heads(packed, rows):
    wide = packed[..., :rows, :]
    narrow = packed[..., rows:, :]
    third = jnp.concatenate([narrow[..., :HEAD], narrow[..., HEAD:]], -2)
    return jnp.concatenate([wide, third], -1)


def by_token(received, rows):
    parts = unpack_heads(received, rows)
    chips = parts.shape[0] // 2
    parts = parts.reshape(chips, 2, rows, -1)
    return jnp.transpose(parts, (1, 2, 0, 3)).reshape(2 * rows, -1)


def layer_norm(value, gain):
    mean = jnp.mean(value, -1, keepdims=True)
    centred = value - mean
    spread = jnp.mean(centred * centred, -1, keepdims=True)
    return centred * lax.rsqrt(spread + epsilon) * gain


def token_info(lengths, views, positions):
    ends = jnp.cumsum(lengths)
    starts = ends - lengths
    inside = (positions[:, None] >= starts[None, :]) & (positions[:, None] < ends[None, :])
    number = jnp.arange(lengths.shape[0], dtype=jnp.int32)
    item = jnp.sum(jnp.where(inside, number[None, :], 0), 1)
    first = jnp.sum(jnp.where(inside, starts[None, :], 0), 1)
    span = jnp.sum(jnp.where(inside, views[None, :], 0), 1) * PATCHES
    frame = (positions - first) // span
    return (item, frame)


def visible(query_pos, query_item, query_frame, key_pos, key_item, key_frame, key_pad):
    same = query_item[:, None] == key_item[None, :]
    order = key_frame[None, :] <= query_frame[:, None]
    usable = (key_pad[None, :] == 1) | (query_pos[:, None] == key_pos[None, :])
    return same & order & usable


def in_blocks(update, carry, piece, block_rows):
    count = piece[0].shape[0]

    def advance(number, inner):
        begin = number * block_rows
        part = (
            lax.dynamic_slice_in_dim(piece[0], begin, block_rows),
            lax.dynamic_slice_in_dim(piece[1], begin, block_rows),
        )
        return update(inner, part, begin)

    return lax.fori_loop(0, count // block_rows, advance, carry)


def score_parts(query_heads, grad_heads, total, shift, key_heads, value_heads, mask, scale):
    scores = (
        jnp.einsum("qhd,khd->hqk", query_heads, key_heads, preferred_element_type=jnp.float32)
        * scale
    )
    chance = jnp.where(mask[None], jnp.exp(scores - total[..., None]), 0.0)
    chance_grad = jnp.einsum(
        "qhd,khd->hqk", grad_heads, value_heads, preferred_element_type=jnp.float32
    )
    score_grad = (chance * (chance_grad - shift[..., None])).astype(jnp.bfloat16)
    return (chance, score_grad)


def on_device(
    inputs,
    cotangent,
    lengths,
    view_counts,
    padding,
    first_gain,
    query_weight,
    key_value_weight,
    output_weight,
    second_gain,
    expand_weight,
    contract_weight,
):
    micro_count, row_count, width = inputs.shape
    head_count = width // HEAD
    scale = HEAD ** (-0.5)
    cycle_size = lax.axis_size("blk")
    own_start = lax.axis_index("blk") * row_count
    query_positions = own_start + jnp.arange(row_count, dtype=jnp.int32)
    gelu = partial(jax.nn.gelu, approximate=True)
    grads = tuple(
        (
            jnp.zeros(array.shape, jnp.float32)
            for array in (
                first_gain,
                query_weight,
                key_value_weight,
                output_weight,
                second_gain,
                expand_weight,
                contract_weight,
            )
        )
    )
    outputs = []
    input_grads = []
    for micro in range(micro_count):
        row_lengths = lengths[micro]
        row_views = view_counts[micro]
        row_pad = padding[micro]
        query_item, query_frame = token_info(row_lengths, row_views, query_positions)
        flat = inputs[micro].astype(jnp.float32)
        normed, first_pull = jax.vjp(layer_norm, flat, first_gain)
        normed_low = normed.astype(jnp.bfloat16)
        query = jnp.dot(normed_low, query_weight, preferred_element_type=jnp.float32).astype(
            jnp.bfloat16
        )
        pair = jnp.dot(normed_low, key_value_weight, preferred_element_type=jnp.float32).astype(
            jnp.bfloat16
        )
        keys = pair[:, :width]
        values = pair[:, width:]
        query_heads = query.reshape(row_count, head_count, HEAD)

        def mask_for(start, count):
            key_positions = start + jnp.arange(count, dtype=jnp.int32)
            key_item, key_frame = token_info(row_lengths, row_views, key_positions)
            key_pad = lax.dynamic_slice_in_dim(row_pad, start, count)
            return visible(
                query_positions,
                query_item,
                query_frame,
                key_positions,
                key_item,
                key_frame,
                key_pad,
            )

        def forward_block(carry, piece, start):
            count = piece[0].shape[0]
            mask = mask_for(start, count)

            def forward_work(state):
                peak, denominator, weighted = state
                key_heads = piece[0].reshape(count, head_count, HEAD)
                value_heads = piece[1].reshape(count, head_count, HEAD)
                scores = (
                    jnp.einsum(
                        "qhd,khd->hqk", query_heads, key_heads, preferred_element_type=jnp.float32
                    )
                    * scale
                )
                scores = jnp.where(mask[None], scores, lowest)
                new_peak = jnp.maximum(peak, jnp.max(scores, -1))
                raised = jnp.where(mask[None], jnp.exp(scores - new_peak[..., None]), 0.0)
                shrink = jnp.exp(peak - new_peak)
                denominator = denominator * shrink + jnp.sum(raised, -1)
                weighted = weighted * shrink[..., None] + jnp.einsum(
                    "hqk,khd->hqd",
                    raised.astype(jnp.bfloat16),
                    value_heads,
                    preferred_element_type=jnp.float32,
                )
                return (new_peak, denominator, weighted)

            return lax.cond(jnp.any(mask), forward_work, lambda state: state, carry)

        initial = (
            jnp.full((head_count, row_count), lowest, jnp.float32),
            jnp.zeros((head_count, row_count), jnp.float32),
            jnp.zeros((head_count, row_count, HEAD), jnp.float32),
        )
        peak, denominator, weighted = in_blocks(
            forward_block,
            initial,
            (
                lax.all_gather(keys, "blk", axis=0, tiled=True),
                lax.all_gather(values, "blk", axis=0, tiled=True),
            ),
            row_count,
        )
        attended_heads = weighted / denominator[..., None]
        log_total = peak + jnp.log(denominator)
        attended_low = (
            jnp.transpose(attended_heads, (1, 0, 2)).reshape(row_count, width).astype(jnp.bfloat16)
        )
        mixed = flat + jnp.dot(attended_low, output_weight, preferred_element_type=jnp.float32)
        second, second_pull = jax.vjp(layer_norm, mixed, second_gain)
        second_low = second.astype(jnp.bfloat16)
        hidden = jnp.dot(second_low, expand_weight, preferred_element_type=jnp.float32)
        activated, gelu_pull = jax.vjp(gelu, hidden)
        activated_low = activated.astype(jnp.bfloat16)
        output = mixed + jnp.dot(activated_low, contract_weight, preferred_element_type=jnp.float32)
        outputs.append(output.astype(jnp.bfloat16))
        upstream = cotangent[micro]
        grad_contract = jnp.einsum(
            "rf,rd->fd", activated_low, upstream, preferred_element_type=jnp.float32
        )
        activated_grad = jnp.einsum(
            "rd,fd->rf", upstream, contract_weight, preferred_element_type=jnp.float32
        )
        hidden_grad = gelu_pull(activated_grad)[0].astype(jnp.bfloat16)
        grad_expand = jnp.einsum(
            "rd,rf->df", second_low, hidden_grad, preferred_element_type=jnp.float32
        )
        second_grad = jnp.einsum(
            "rf,df->rd", hidden_grad, expand_weight, preferred_element_type=jnp.float32
        )
        mixed_part, grad_second = second_pull(second_grad)
        mixed_grad = upstream.astype(jnp.float32) + mixed_part
        branch_grad = mixed_grad.astype(jnp.bfloat16)
        grad_output = jnp.einsum(
            "rd,re->de", attended_low, branch_grad, preferred_element_type=jnp.float32
        )
        attended_grad = jnp.einsum(
            "re,de->rd", branch_grad, output_weight, preferred_element_type=jnp.float32
        ).astype(jnp.bfloat16)
        grad_heads = attended_grad.reshape(row_count, head_count, HEAD)
        delta = jnp.sum(
            jnp.transpose(grad_heads, (1, 0, 2)).astype(jnp.float32) * attended_heads, -1
        )

        def backward_block(carry, piece, start):
            count = piece[0].shape[0]
            mask = mask_for(start, count)

            def backward_work(state):
                query_sum, pair_terms = state
                key_heads = piece[0].reshape(count, head_count, HEAD)
                value_heads = piece[1].reshape(count, head_count, HEAD)
                chance, score_grad = score_parts(
                    query_heads, grad_heads, log_total, delta, key_heads, value_heads, mask, scale
                )
                value_term = jnp.einsum(
                    "hqk,qhd->khd",
                    chance.astype(jnp.bfloat16),
                    grad_heads,
                    preferred_element_type=jnp.float32,
                )
                query_sum = (
                    query_sum
                    + jnp.einsum(
                        "hqk,khd->qhd", score_grad, key_heads, preferred_element_type=jnp.float32
                    )
                    * scale
                )
                key_term = (
                    jnp.einsum(
                        "hqk,qhd->khd", score_grad, query_heads, preferred_element_type=jnp.float32
                    )
                    * scale
                )
                term = jnp.concatenate(
                    [key_term.reshape(count, width), value_term.reshape(count, width)], 1
                )
                previous = lax.dynamic_slice_in_dim(pair_terms, start, count)
                pair_terms = lax.dynamic_update_slice_in_dim(pair_terms, previous + term, start, 0)
                return (query_sum, pair_terms)

            return lax.cond(jnp.any(mask), backward_work, lambda state: state, carry)

        start_back = (
            jnp.zeros((row_count, head_count, HEAD), jnp.float32),
            jnp.zeros((row_count * cycle_size, 2 * width), jnp.float32),
        )
        back_state = in_blocks(
            backward_block,
            start_back,
            (
                lax.all_gather(keys, "blk", axis=0, tiled=True),
                lax.all_gather(values, "blk", axis=0, tiled=True),
            ),
            row_count,
        )
        query_sum, pair_terms = back_state
        pair_grad = lax.psum_scatter(
            pair_terms.astype(jnp.bfloat16), "blk", scatter_dimension=0, tiled=True
        )
        query_grad = query_sum.reshape(row_count, width).astype(jnp.bfloat16)
        grad_query = jnp.einsum(
            "rd,re->de", normed_low, query_grad, preferred_element_type=jnp.float32
        )
        grad_pair = jnp.einsum(
            "rd,re->de", normed_low, pair_grad, preferred_element_type=jnp.float32
        )
        normed_grad = jnp.einsum(
            "re,de->rd", query_grad, query_weight, preferred_element_type=jnp.float32
        )
        normed_grad = normed_grad + jnp.einsum(
            "re,de->rd", pair_grad, key_value_weight, preferred_element_type=jnp.float32
        )
        input_part, grad_first = first_pull(normed_grad)
        input_grads.append((mixed_grad + input_part).astype(jnp.bfloat16))
        terms = (
            grad_first,
            grad_query,
            grad_pair,
            grad_output,
            grad_second,
            grad_expand,
            grad_contract,
        )
        grads = tuple((total + term for total, term in zip(grads, terms)))
    summed = lax.psum(
        (grads[0], grads[1], grads[2], grads[3], grads[4], grads[5], grads[6]), ("dp", "blk")
    )
    return (
        jnp.stack(outputs),
        jnp.stack(input_grads),
        summed[0],
        summed[1],
        summed[2],
        summed[3],
        summed[4],
        summed[5],
        summed[6],
    )


def fast_on_device(
    inputs, cotangent, lengths, view_counts, padding, first_gain, query_weight, key_value_weight,
    output_weight, second_gain, expand_weight, contract_weight,
):
    micro, rows, width = inputs.shape
    blocks = lax.axis_size("blk")
    normed_all, qa, ka, va, out, received = attention_forward(
        inputs, first_gain, lengths, view_counts, padding, query_weight, key_value_weight, blocks
    )
    gelu = partial(jax.nn.gelu, approximate=True)
    flat = inputs.reshape(micro * rows, width).astype(f32)
    upstream = cotangent.reshape(micro * rows, width)
    _, first_pull = jax.vjp(layer_norm, flat, first_gain)
    attended = by_token(received, rows)
    mixed = flat + jnp.dot(attended, output_weight, preferred_element_type=f32)
    second, second_pull = jax.vjp(layer_norm, mixed, second_gain)
    second = second.astype(bf16)
    hidden = jnp.dot(second, expand_weight, preferred_element_type=f32)
    activated, gelu_pull = jax.vjp(gelu, hidden)
    activated = activated.astype(bf16)
    result = (mixed + jnp.dot(activated, contract_weight, preferred_element_type=f32)).astype(bf16)
    hidden_grad = gelu_pull(dot_nt(upstream, contract_weight))[0].astype(bf16)
    second_grad = dot_nt(hidden_grad, expand_weight)
    mixed_part, grad_second = second_pull(second_grad)
    mixed_grad = upstream.astype(f32) + mixed_part
    branch_grad = mixed_grad.astype(bf16)
    attended_grad = dot_nt(branch_grad, output_weight).astype(bf16)
    grad_contract = dot_tn(activated, upstream)
    grad_expand = dot_tn(second, hidden_grad)
    grad_output = dot_tn(attended, branch_grad)
    got_query, got_pair, unit_grad = attention_backward(
        attended_grad.reshape(micro, rows, width), normed_all, qa, ka, va, out
    )
    heads = qa.shape[0]
    chips = blocks // 2
    query_grad = by_token(got_query, rows)
    pair_grad = got_pair.reshape(chips, 2, heads, rows, 2, HEAD)
    pair_grad = jnp.transpose(pair_grad, (1, 3, 4, 0, 2, 5)).reshape(micro * rows, 2 * width)
    normed_grad = dot_nt(query_grad, query_weight) + dot_nt(pair_grad, key_value_weight)
    input_part, grad_first = first_pull(normed_grad)
    input_grad = (mixed_grad + input_part).astype(bf16)
    z = lax.axis_index("blk") // 2
    pair_part = unit_grad[:, : heads * LANES].reshape(width, heads, 2, HEAD)
    pair_part = jnp.transpose(pair_part, (0, 2, 1, 3)).reshape(width, 2, heads * HEAD)
    query_part = unit_grad[:, heads * LANES : heads * LANES + heads * HEAD]
    grad_pair = lax.dynamic_update_slice(
        jnp.zeros((width, 2, width), f32), pair_part, (0, 0, z * heads * HEAD)
    ).reshape(width, 2 * width)
    grad_query = lax.dynamic_update_slice(
        jnp.zeros((width, width), f32), query_part, (0, z * heads * HEAD)
    )
    wide = [g.astype(bf16) for g in (grad_query, grad_pair, grad_output, grad_expand, grad_contract)]
    wide = [g.astype(f32) for g in lax.psum(tuple(wide), ("dp", "blk"))]
    gains = lax.psum((grad_first, grad_second), ("dp", "blk"))
    return (
        result.reshape(micro, rows, width), input_grad.reshape(micro, rows, width),
        gains[0], wide[0], wide[1], wide[2], gains[1], wide[3], wide[4],
    )


def solution(mesh):
    placed = (
        P("dp", "blk", None),
        P("dp", "blk", None),
        P("dp", None),
        P("dp", None),
        P("dp", None),
    ) + (P(),) * 7

    def program(*arrays):
        inputs, lengths = arrays[0], arrays[2]
        dp, blk = mesh.shape["dp"], mesh.shape["blk"]
        rows, total, width = inputs.shape
        items = lengths.shape[1]
        chips = blk // 2
        fits = (
            (dp, blk) == (4, 8)
            and rows == 2 * dp
            and total % (blk * 2 * LANES) == 0
            and width % (LANES * HEAD // 64) == 0
            and width // HEAD == 3 * chips
            and total // PATCHES + items <= CODES
        )
        return jax.shard_map(
            fast_on_device if fits else on_device,
            mesh=mesh,
            in_specs=placed,
            out_specs=(P("dp", "blk", None), P("dp", "blk", None)) + (P(),) * 7,
            check_vma=False,
        )(*arrays)

    return program
```

```python
from functools import partial

import jax
import jax.numpy as jnp
from jax import lax
from jax.experimental import pallas as pl
from jax.experimental.pallas import tpu as pltpu
from jax.sharding import PartitionSpec as P

HEAD = 64
PATCHES = 64
CODES = 40
BIG = 1e30
EARLY = 6
OUT_AT = (0, 3, 6, 9, 12)
BACK_AT = (0, 3, 6, 9)
LATE = 13
GIVE = 4
PAIR_SLOTS = (10, 14, 18, 21, 23, 24, 22)
QUERY_SLOTS = (25, 27, 29, 31, 33, 34, 27)
UNIT_SLOTS = (1, 3, 5, 8, 11, 14, 16)
OUT = (1, 2, 3, 4, 5)
BACK = (6, 7, 8, 9)
LANES = 128
MESH = pl.DeviceIdType.MESH
bf16 = jnp.bfloat16
f32 = jnp.float32

epsilon = 1e-05
lowest = -1e30


def dot_nn(a, b):
    return lax.dot_general(a, b, (((1,), (0,)), ((), ())), preferred_element_type=f32)


def dot_nt(a, b):
    return lax.dot_general(a, b, (((1,), (1,)), ((), ())), preferred_element_type=f32)


def dot_tn(a, b):
    return lax.dot_general(a, b, (((0,), (0,)), ((), ())), preferred_element_type=f32)


def chip_order(z, step):
    code = jnp.where(z == 0, 3210, jnp.where(z == 1, 3201, jnp.where(z == 2, 312, 123)))
    return digit(code, step)


def digit(code, step):
    power = jnp.where(step == 0, 1, jnp.where(step == 1, 10, jnp.where(step == 2, 100, 1000)))
    return lax.rem(code // power, 10)


def chip_span(z, step):
    low = jnp.where(z == 0, 0, jnp.where(z == 1, 1, jnp.where(z == 2, 112, 123)))
    high = jnp.where(z == 0, 3210, jnp.where(z == 1, 3211, jnp.where(z == 2, 3322, 3333)))
    return digit(low, step), digit(high, step)


def far_order(z, step):
    return jnp.where(
        step == 0,
        lax.rem(z + 2, 4),
        jnp.where(step == 1, 3 - z, jnp.where(step == 2, z + 1 - 2 * lax.rem(z, 2), z)),
    )


def features(block, rows, lengths, views, row, padded):
    lane = lax.broadcasted_iota(jnp.int32, (rows, LANES), 1) - HEAD
    position = block * rows + lax.broadcasted_iota(jnp.int32, (rows, LANES), 0)
    code = jnp.zeros((rows, LANES), jnp.int32)
    base = jnp.zeros((rows, LANES), jnp.int32)
    start = jnp.int32(0)
    first = jnp.int32(0)
    for item in range(lengths.shape[1]):
        length = lengths[row, item]
        view = views[row, item]
        offset = position - start
        inside = (offset >= 0) & (offset < length)
        frame = (offset >> 6) * (2 - view) + (offset >> 7) * (view - 1)
        code = jnp.where(inside, first + frame, code)
        base = jnp.where(inside, first, base)
        first = first + ((length + 63) >> 6) * (2 - view) + ((length + 127) >> 7) * (view - 1)
        start = start + length
    coded = (lane >= 0) & (lane < CODES)
    key = jnp.where(coded & (lane == code), 1.0, 0.0)
    key = jnp.where((lane > CODES) & (lane < CODES + 4), 1.0, key)
    key = jnp.where(lane == CODES, padded, key)
    hidden = (coded & ((lane < base) | (lane > code))) | (lane == CODES)
    query = jnp.where(hidden, -BIG, 0.0)
    return key, query


def three_parts(value):
    high = value.astype(bf16).astype(f32)
    rest = value - high
    middle = rest.astype(bf16).astype(f32)
    low = (rest - middle).astype(bf16).astype(f32)
    return high, middle, low


def spread(value, first, lane):
    high, middle, low = three_parts(value)
    return jnp.where(
        lane == first, high, jnp.where(lane == first + 1, middle, jnp.where(lane == first + 2, low, 0.0))
    )


def pack_heads(heads):
    half = heads[2].shape[0] // 2
    wide = jnp.concatenate([heads[0], heads[1]], 1)
    narrow = jnp.concatenate([heads[2][:half], heads[2][half:]], 1)
    return wide, narrow


def greet(dp, me, count, others=()):
    barrier = pltpu.get_barrier_semaphore()
    for step in range(1, count):
        pl.semaphore_signal(
            barrier, inc=1, device_id=(dp, lax.rem(me + step, count)), device_id_type=MESH
        )
    for other in others:
        pl.semaphore_signal(barrier, inc=1, device_id=other, device_id_type=MESH)
    return lambda: pl.semaphore_wait(barrier, count - 1 + len(others))


def heads_of(wide, narrow):
    return [
        wide[:, :HEAD],
        wide[:, HEAD:],
        jnp.concatenate([narrow[:, :HEAD], narrow[:, HEAD:]], 0),
    ]


def columns_of(received, row, rows, blocks):
    pieces = []
    for chip in range(blocks // 2):
        block = 2 * chip + row
        pieces += heads_of(received[block, :rows, :], received[block, rows:, :])
    return jnp.concatenate(pieces, 1)


def normal(value):
    mean = jnp.mean(value, -1, keepdims=True)
    centred = value - mean
    scale = lax.rsqrt(jnp.mean(centred * centred, -1, keepdims=True) + epsilon)
    return centred * scale, scale


def normal_pull(grad, unit, scale):
    return scale * (
        grad - jnp.mean(grad, -1, keepdims=True) - unit * jnp.mean(grad * unit, -1, keepdims=True)
    )


def forward_kernel(
    lengths, views, x_ref, gain_ref, pad_ref, wq_ref, wkv_ref,
    normed_out, qa_out, ka_out, va_out, o_out, received,
    normed, qa, ka, va, o_ref, weight, stage, peak, outgoing,
    sib_send, sib_recv, line_send, line_recv, out_send, out_recv, store,
):
    rows, width = x_ref.shape[1], x_ref.shape[2]
    blocks = normed.shape[0]
    heads = qa.shape[0]
    dp = lax.axis_index("dp")
    me = lax.axis_index("blk")
    z = me // 2
    core = lax.rem(me, 2)
    sibling = me + 1 - 2 * core
    lane = lax.broadcasted_iota(jnp.int32, (rows, LANES), 1)

    arrived = greet(dp, me, blocks)
    gain = gain_ref[...].reshape(1, width)

    def norm(value):
        return (normal(value.astype(f32))[0] * gain).astype(bf16)

    normed[me] = norm(x_ref[core])
    arrived()

    def place(block):
        return pl.ds(pl.multiple_of(block * rows, rows), rows)

    def keep(block, number):
        here = place(block)
        src, dst = (
            (normed.at[block], normed_out.at[block // 2, pl.ds(pl.multiple_of(lax.rem(block, 2) * rows, rows), rows)]),
            (ka.at[:, here, :], ka_out.at[:, here, :]),
            (va.at[:, here, :], va_out.at[:, here, :]),
            (qa.at[:, here, :], qa_out.at[:, here, :]),
            (outgoing.at[block], o_out.at[block]),
        )[number]
        return pltpu.make_async_copy(src, dst, store.at[block, number])

    def line_copy(block, up):
        return pltpu.make_async_remote_copy(
            src_ref=normed.at[block],
            dst_ref=normed.at[block],
            send_sem=line_send.at[block, up],
            recv_sem=line_recv.at[block],
            device_id=(dp, me + (2 if up else -2)),
            device_id_type=MESH,
        )

    @pl.when(z < 3)
    def _():
        line_copy(me, 1).start()

    @pl.when(z > 0)
    def _():
        line_copy(me, 0).start()

    stage[...] = norm(x_ref[1 - core])
    sib_copy = pltpu.make_async_remote_copy(
        src_ref=stage,
        dst_ref=normed.at[me],
        send_sem=sib_send,
        recv_sem=sib_recv,
        device_id=(dp, sibling),
        device_id_type=MESH,
    )
    sib_copy.start()

    gap = jnp.zeros((width, LANES - HEAD), bf16)
    for chip in range(blocks // 2):

        @pl.when(z == chip)
        def _():
            for head in range(heads):
                at = (chip * heads + head) * HEAD
                for kind, piece in enumerate(
                    (
                        wq_ref[:, at : at + HEAD],
                        wkv_ref[:, at : at + HEAD],
                        wkv_ref[:, width + at : width + at + HEAD],
                    )
                ):
                    column = (head * 3 + kind) * LANES
                    weight[:, column : column + LANES] = jnp.concatenate([piece, gap], 1)

    ones = jnp.where((lane >= HEAD) & (lane < HEAD + 3), -1.0, 0.0)

    def bring(step, turn):
        chip = chip_order(z, step)
        block = 2 * chip + lax.rem(core + turn, 2)

        @pl.when((step == 0) & (turn == 1))
        def _():
            pltpu.make_async_remote_copy(
                src_ref=stage,
                dst_ref=normed.at[sibling],
                send_sem=sib_send,
                recv_sem=sib_recv,
                device_id=(dp, sibling),
                device_id_type=MESH,
            ).wait_recv()

        @pl.when(step > 0)
        def _():
            pltpu.make_async_remote_copy(
                src_ref=normed.at[block],
                dst_ref=normed.at[block],
                send_sem=line_send.at[block, 0],
                recv_sem=line_recv.at[block],
                device_id=(dp, sibling),
                device_id_type=MESH,
            ).wait_recv()

        @pl.when((step + turn > 0) & (chip <= z) & (z < 3))
        def _():
            line_copy(block, 1).start()

        @pl.when((step + turn > 0) & (chip >= z) & (z > 0))
        def _():
            line_copy(block, 0).start()

        keep(block, 0).start()
        pad_row = 1.0 - pad_ref[pl.ds(core, 1), place(block)].astype(f32)
        padded = jnp.transpose(jnp.broadcast_to(pad_row, (LANES, rows)))
        key, query = features(block, rows, lengths, views, core, padded)
        out = dot_nn(normed[block], weight[...]).astype(bf16).astype(f32)
        here = pl.ds(pl.multiple_of(block * rows, rows), rows)
        for head in range(heads):
            at = head * 3 * LANES
            qa[head, here, :] = (out[:, at : at + LANES] * (HEAD**-0.5) + query).astype(bf16)
            ka[head, here, :] = (out[:, at + LANES : at + 2 * LANES] + key).astype(bf16)
            va[head, here, :] = (out[:, at + 2 * LANES : at + 3 * LANES] + ones).astype(bf16)
            peak[head, here, :] = jnp.full((rows, LANES), -BIG, f32)
            o_ref[head, here, :] = jnp.zeros((rows, LANES), f32)
        keep(block, 1).start()
        keep(block, 2).start()

    wide = 2 * rows
    eye = lax.broadcasted_iota(jnp.int32, (wide, wide), 0) == lax.broadcasted_iota(
        jnp.int32, (wide, wide), 1
    )

    def attend(queries, keys, diagonal=False):
        found = []
        for head in range(heads):
            query = qa[head, queries, :]
            key = ka[head, keys, :]
            s = dot_nt(query, key)
            if diagonal:
                s = jnp.where(eye, dot_nt(query[:, :HEAD], key[:, :HEAD]), s)
            tiles = [s[:, i : i + LANES] for i in range(0, s.shape[1], LANES)]
            top = tiles[0]
            for tile in tiles[1:]:
                top = jnp.maximum(top, tile)
            old = peak[head, queries, :]
            new = jnp.maximum(old, jnp.max(top, -1, keepdims=True))
            p = jnp.concatenate([jnp.exp(tile - new).astype(bf16) for tile in tiles], 1)
            total = o_ref[head, queries, :] * jnp.exp(old - new) + dot_nn(p, va[head, keys, :])
            found.append((new, total))
        for head, (new, total) in enumerate(found):
            peak[head, queries, :] = new
            o_ref[head, queries, :] = total

    def out_copy(block):
        return pltpu.make_async_remote_copy(
            src_ref=outgoing.at[block],
            dst_ref=received.at[me],
            send_sem=out_send.at[block],
            recv_sem=out_recv.at[me],
            device_id=(dp, block),
            device_id_type=MESH,
        )

    def hand_back(chip):
        @pl.loop(0, 2)
        def _(turn):
            block = 2 * chip + lax.rem(core + turn, 2)
            here = pl.ds(pl.multiple_of(block * rows, rows), rows)
            results = []
            for head in range(heads):
                total = o_ref[head, here, :]
                mass = -total[:, HEAD : HEAD + 1]
                results.append((total / mass)[:, :HEAD].astype(bf16))
                log_total = peak[head, here, :] + jnp.log(mass)
                qa[head, here, :] = (
                    qa[head, here, :].astype(f32) - spread(log_total, HEAD + CODES + 1, lane)
                ).astype(bf16)
            both, third = pack_heads(results)
            outgoing[block, :rows, :] = both
            outgoing[block, rows:, :] = third

            @pl.when(block == me)
            def _():
                received[me, :rows, :] = both
                received[me, rows:, :] = third

            @pl.when(block != me)
            def _():
                out_copy(block).start()

            keep(block, 3).start()
            keep(block, 4).start()

    def span(chip):
        return pl.ds(pl.multiple_of(chip * wide, wide), wide)

    def across(chip):
        edge = (chip + 1) * wide
        attend(
            pl.ds(pl.multiple_of(edge - LANES, LANES), LANES),
            pl.ds(pl.multiple_of(edge, LANES), LANES),
        )

    @pl.loop(0, blocks // 2)
    def _(step):
        @pl.loop(0, 2)
        def _(turn):
            bring(step, turn)

        chip = chip_order(z, step)
        low, high = chip_span(z, step)

        @pl.when(chip > low)
        def _():
            across(chip - 1)

        @pl.when(chip < high)
        def _():
            across(chip)

        @pl.when((low == 0) & (chip == high) & (chip > 0))
        def _():
            hand_back(chip - 1)

        @pl.loop(low, high + 1)
        def _(other):
            top = jnp.maximum(chip, other)

            @pl.when(other == chip)
            def _():
                attend(span(chip), span(chip), True)

            @pl.when(other != chip)
            def _():
                attend(span(top), span(jnp.minimum(chip, other)))

            @pl.when((other >= chip) & (low == 0) & (high >= jnp.minimum(top + 1, blocks // 2 - 1)))
            def _():
                hand_back(top)

    sib_copy.wait_send()

    @pl.loop(0, blocks)
    def _(block):
        for number in range(5):
            keep(block, number).wait()

        @pl.when((block // 2 <= z) & (z < 3))
        def _():
            line_copy(block, 1).wait_send()

        @pl.when((block // 2 >= z) & (z > 0))
        def _():
            line_copy(block, 0).wait_send()

        @pl.when(block != me)
        def _():
            out_copy(block).wait_send()
            pltpu.make_async_remote_copy(
                src_ref=outgoing.at[block],
                dst_ref=received.at[block],
                send_sem=out_send.at[block],
                recv_sem=out_recv.at[block],
                device_id=(dp, block),
                device_id_type=MESH,
            ).wait_recv()


class Sums:
    def __init__(self, final, own, buffers, semaphores, local):
        self.final, self.own, self.local = final, own, local
        self.from_core, self.first, self.second, self.line, self.near, self.far = buffers
        self.sems = dict(zip(
            ("core", "first", "second", "inward", "across", "outward", "back", "wide", "twin"), semaphores
        ))
        self.count = own.shape[0]
        self.half, self.lanes = own.shape[1], own.shape[2]
        self.quarter = self.half // 4
        self.eighth = self.half // 8
        self.dp = lax.axis_index("dp")
        self.me = lax.axis_index("blk")
        self.core = lax.rem(self.me, 2)
        self.z = self.me // 2
        self.x = lax.rem(self.dp, 2)
        self.y = self.dp // 2
        self.along_x = (self.dp + 1 - 2 * self.x, self.me)
        self.along_y = (self.dp + 2 - 4 * self.y, self.me)
        self.twin = (self.dp, self.me + 1 - 2 * self.core)
        self.inner = (self.z == 1) | (self.z == 2)
        self.outer = (self.z == 0) | (self.z == 3)
        self.pair = (self.dp, self.me + 2 - 4 * lax.rem(self.z, 2))
        self.middle = (self.dp, jnp.where(self.z < 2, self.me + 2, self.me - 2))

    def copy(self, name, piece, src, dst, device, way=None):
        send, recv = self.sems[name]
        at = (piece,) if way is None else (piece, way)
        return pltpu.make_async_remote_copy(
            src_ref=src,
            dst_ref=dst,
            send_sem=send.at[at],
            recv_sem=recv.at[at],
            device_id=device,
            device_id_type=MESH,
        )

    def rows(self, start, count):
        return pl.ds(pl.multiple_of(start, 16), count)

    def place(self, ref, piece, start, count):
        cols = pl.ds(pl.multiple_of(lax.rem(piece, 2) * self.lanes, LANES), self.lanes)
        return ref.at[piece // 2, self.rows(start, count), cols]

    def to_core(self, piece, src=None):
        src = self.own.at[piece] if src is None else src
        return self.copy("core", piece, src, self.from_core.at[piece], self.twin)

    def to_first(self, piece):
        q = self.quarter
        return (
            self.copy("first", piece, self.own.at[piece, self.rows(q * (1 - self.x), q)], self.first.at[piece, 0], self.along_x, 0),
            self.copy("first", piece, self.own.at[piece, self.rows(2 * q + q * (1 - self.y), q)], self.first.at[piece, 1], self.along_y, 1),
        )

    def to_second(self, piece):
        q, e = self.quarter, self.eighth
        return (
            self.copy("second", piece, self.own.at[piece, self.rows(q * self.x + e * (1 - self.y), e)], self.second.at[piece, 0], self.along_y, 0),
            self.copy("second", piece, self.own.at[piece, self.rows(2 * q + q * self.y + e * (1 - self.x), e)], self.second.at[piece, 1], self.along_x, 1),
        )

    def inward(self, piece):
        return self.copy("inward", piece, self.line.at[piece], self.near.at[piece], self.pair)

    def across(self, piece):
        return self.copy("across", piece, self.line.at[piece], self.far.at[piece], self.middle)

    def outward(self, piece):
        return self.copy("outward", piece, self.far.at[piece], self.near.at[piece], self.pair)

    def mine(self):
        q, e = self.quarter, self.eighth
        base = self.core * self.half
        return base + q * self.x + e * self.y, base + 2 * q + q * self.y + e * self.x

    def keep(self, piece, total):
        e = self.eighth
        one, two = self.mine()
        return (
            pltpu.make_async_copy(total.at[piece, :e], self.place(self.final, piece, one, e), self.local.at[piece, 0]),
            pltpu.make_async_copy(total.at[piece, e:], self.place(self.final, piece, two, e), self.local.at[piece, 1]),
        )

    def back(self, piece, total):
        e = self.eighth
        one, two = self.mine()
        return (
            self.copy("back", piece, total.at[piece, :e], self.place(self.final, piece, one, e), self.along_y, 0),
            self.copy("back", piece, total.at[piece, e:], self.place(self.final, piece, two, e), self.along_x, 1),
        )

    def wide(self, piece):
        q = self.quarter
        base = self.core * self.half
        one = self.place(self.final, piece, base + q * self.x, q)
        two = self.place(self.final, piece, base + 2 * q + q * self.y, q)
        return (
            self.copy("wide", piece, one, one, self.along_x, 0),
            self.copy("wide", piece, two, two, self.along_y, 1),
        )

    def to_twin(self, piece):
        part = self.place(self.final, piece, self.core * self.half, self.half)
        return self.copy("twin", piece, part, part, self.twin)

    def step_1(self, piece):
        self.to_core(piece).wait_recv()
        self.own[piece] = self.own[piece] + self.from_core[piece]
        for copy in self.to_first(piece):
            copy.start()

    def step_2(self, piece):
        q = self.quarter
        one, two = self.to_first(piece)
        one.wait_recv()
        at = self.rows(q * self.x, q)
        self.own[piece, at, :] = self.own[piece, at, :] + self.first[piece, 0]
        two.wait_recv()
        at = self.rows(2 * q + q * self.y, q)
        self.own[piece, at, :] = self.own[piece, at, :] + self.first[piece, 1]
        for copy in self.to_second(piece):
            copy.start()

    def step_3(self, piece):
        q, e = self.quarter, self.eighth
        one, two = self.to_second(piece)
        one.wait_recv()
        at = self.rows(q * self.x + e * self.y, e)
        self.line[piece, :e, :] = self.own[piece, at, :] + self.second[piece, 0]
        two.wait_recv()
        at = self.rows(2 * q + q * self.y + e * self.x, e)
        self.line[piece, e:, :] = self.own[piece, at, :] + self.second[piece, 1]

        @pl.when(self.outer)
        def _():
            self.inward(piece).start()

    def step_4(self, piece):
        @pl.when(self.inner)
        def _():
            self.inward(piece).wait_recv()
            self.line[piece] = self.line[piece] + self.near[piece]
            self.across(piece).start()

    def step_5(self, piece):
        @pl.when(self.inner)
        def _():
            self.across(piece).wait_recv()
            self.far[piece] = self.line[piece] + self.far[piece]
            self.outward(piece).start()

    def step_6(self, piece):
        @pl.when(self.outer)
        def _():
            self.outward(piece).wait_recv()
            for copy in self.back(piece, self.near) + self.keep(piece, self.near):
                copy.start()

        @pl.when(self.inner)
        def _():
            for copy in self.back(piece, self.far) + self.keep(piece, self.far):
                copy.start()

    def step_7(self, piece):
        for copy in self.keep(piece, self.near):
            copy.wait()
        for copy in self.back(piece, self.near):
            copy.wait_recv()
        for copy in self.wide(piece):
            copy.start()

    def step_8(self, piece):
        for copy in self.wide(piece):
            copy.wait_recv()
        self.to_twin(piece).start()

    def step_9(self, piece):
        self.to_twin(piece).wait_recv()

    def tick(self, numbers, offsets, time, last):
        for place in reversed(range(len(numbers))):
            piece = time - offsets[place]

            @pl.when((piece >= 0) & (piece < last))
            def _():
                getattr(self, "step_" + str(numbers[place]))(piece)

    def finish(self, piece):
        for copies in (self.to_first(piece), self.to_second(piece), self.back(piece, self.near), self.wide(piece)):
            for copy in copies:
                copy.wait_send()
        self.to_twin(piece).wait_send()

        @pl.when(self.outer)
        def _():
            self.inward(piece).wait_send()

        @pl.when(self.inner)
        def _():
            self.across(piece).wait_send()
            self.outward(piece).wait_send()

    @staticmethod
    def scratch(count, half, lanes):
        def array(*shape):
            return pltpu.VMEM((count,) + shape + (lanes,), bf16)

        quarter, eighth = half // 4, half // 8
        dma = pltpu.SemaphoreType.DMA
        one, two = [dma((count,))] * 2, [dma((count, 2))] * 2
        return (
            [array(half)] * 2
            + [array(2, quarter), array(2, eighth)]
            + [array(quarter)] * 3
            + one + two + two + one + one + one + two + two + one
            + [dma((count, 2))]
        )

    @classmethod
    def gather(cls, final, refs):
        sems = refs[7:25]
        pairs = [(sems[2 * i], sems[2 * i + 1]) for i in range(9)]
        return cls(final, refs[0], refs[1:7], pairs, refs[25])


class UnitSum:
    def __init__(self, sums, final, refs):
        self.sums, self.final = sums, final
        (
            self.own, self.give, self.from_core, self.first, self.second, self.line,
            self.core_sems, self.first_sems, self.second_sems, self.line_send, self.line_recv,
            self.back_sems, self.wide_sems, self.twin_sems, self.local,
        ) = refs

    def copy(self, sems, at, src, dst, device):
        return pltpu.make_async_remote_copy(
            src_ref=src,
            dst_ref=dst,
            send_sem=sems.at[0, at],
            recv_sem=sems.at[1, at],
            device_id=device,
            device_id_type=MESH,
        )

    def to_core(self):
        return self.copy(self.core_sems, 0, self.give, self.from_core, self.sums.twin)

    def to_first(self):
        s, q = self.sums, self.sums.quarter
        return (
            self.copy(self.first_sems, 0, self.own.at[s.rows(q * (1 - s.x), q)], self.first.at[0], s.along_x),
            self.copy(self.first_sems, 1, self.own.at[s.rows(2 * q + q * (1 - s.y), q)], self.first.at[1], s.along_y),
        )

    def to_second(self):
        s, q, e = self.sums, self.sums.quarter, self.sums.eighth
        return (
            self.copy(self.second_sems, 0, self.own.at[s.rows(q * s.x + e * (1 - s.y), e)], self.second.at[0], s.along_y),
            self.copy(self.second_sems, 1, self.own.at[s.rows(2 * q + q * s.y + e * (1 - s.x), e)], self.second.at[1], s.along_x),
        )

    def along_line(self, chip):
        s = self.sums
        return pltpu.make_async_remote_copy(
            src_ref=self.line.at[s.z],
            dst_ref=self.line.at[s.z],
            send_sem=self.line_send.at[chip],
            recv_sem=self.line_recv.at[s.z],
            device_id=(s.dp, 2 * chip + s.core),
            device_id_type=MESH,
        )

    def from_line(self, chip):
        s = self.sums
        return pltpu.make_async_remote_copy(
            src_ref=self.line.at[chip],
            dst_ref=self.line.at[chip],
            send_sem=self.line_send.at[chip],
            recv_sem=self.line_recv.at[chip],
            device_id=(s.dp, 2 * chip + s.core),
            device_id_type=MESH,
        )

    def keep(self):
        s, e = self.sums, self.sums.eighth
        one, two = s.mine()
        return (
            pltpu.make_async_copy(self.line.at[:, :e], self.final.at[:, s.rows(one, e)], self.local.at[0]),
            pltpu.make_async_copy(self.line.at[:, e:], self.final.at[:, s.rows(two, e)], self.local.at[1]),
        )

    def back(self):
        s, e = self.sums, self.sums.eighth
        one, two = s.mine()
        return (
            self.copy(self.back_sems, 0, self.line.at[:, :e], self.final.at[:, s.rows(one, e)], s.along_y),
            self.copy(self.back_sems, 1, self.line.at[:, e:], self.final.at[:, s.rows(two, e)], s.along_x),
        )

    def wide(self):
        s, q = self.sums, self.sums.quarter
        base = s.core * s.half
        one = self.final.at[:, s.rows(base + q * s.x, q)]
        two = self.final.at[:, s.rows(base + 2 * q + q * s.y, q)]
        return (
            self.copy(self.wide_sems, 0, one, one, s.along_x),
            self.copy(self.wide_sems, 1, two, two, s.along_y),
        )

    def to_twin(self):
        s = self.sums
        part = self.final.at[:, s.rows(s.core * s.half, s.half)]
        return self.copy(self.twin_sems, 0, part, part, s.twin)

    def step(self, number):
        s, q, e = self.sums, self.sums.quarter, self.sums.eighth
        if number == 0:
            self.to_core().start()
        elif number == 1:
            self.to_core().wait_recv()
            self.own[...] = self.own[...] + self.from_core[...]
            for copy in self.to_first():
                copy.start()
        elif number == 2:
            for way, start in ((0, q * s.x), (1, 2 * q + q * s.y)):
                self.to_first()[way].wait_recv()
                at = s.rows(start, q)
                self.own[at, :] = self.own[at, :] + self.first[way]
            for copy in self.to_second():
                copy.start()
        elif number == 3:
            for way, start in ((0, q * s.x + e * s.y), (1, 2 * q + q * s.y + e * s.x)):
                self.to_second()[way].wait_recv()
                self.line[s.z, way * e : (way + 1) * e, :] = self.own[s.rows(start, e), :] + self.second[way]
            for ahead in (2, 1, 3):
                self.along_line(lax.rem(s.z + ahead, 4)).start()
        elif number == 4:
            for ahead in (1, 2, 3):
                self.from_line(lax.rem(s.z + ahead, 4)).wait_recv()
            for copy in self.back() + self.keep():
                copy.start()
        elif number == 5:
            for copy in self.keep():
                copy.wait()
            for copy in self.back():
                copy.wait_recv()
            for copy in self.wide():
                copy.start()
        elif number == 6:
            for copy in self.wide():
                copy.wait_recv()
            self.to_twin().start()
        else:
            self.to_twin().wait_recv()

    def finish(self):
        s = self.sums
        for copy in (self.to_core(), self.to_twin()) + self.to_first() + self.to_second() + self.back() + self.wide():
            copy.wait_send()
        for ahead in (1, 2, 3):
            self.along_line(lax.rem(s.z + ahead, 4)).wait_send()

    @staticmethod
    def scratch(chips, half, lanes):
        dma = pltpu.SemaphoreType.DMA
        quarter, eighth = half // 4, half // 8
        array = [pltpu.VMEM((half, lanes), bf16)]
        return (
            array * 3
            + [
                pltpu.VMEM((2, quarter, lanes), bf16),
                pltpu.VMEM((2, eighth, lanes), bf16),
                pltpu.VMEM((chips, quarter, lanes), bf16),
                dma((2, 1)),
                dma((2, 2)),
                dma((2, 2)),
                dma((chips,)),
                dma((chips,)),
                dma((2, 2)),
                dma((2, 2)),
                dma((2, 1)),
                dma((2,)),
            ]
        )


def backward_kernel(
    grad_ref, mixed_grad_ref, gain_ref, acts_in, normed_in, qa_in, ka_in, va_in, o_in, wq_in, wkv_in, x_in,
    input_grad, final, unit_final,
    acts, qa, ka, va, out, received, doa, right_key, key_turned, dqt, dvk, send_query, send_pair,
    got_query, got_pair, unit, give,
    load_acts, load_heads, load_late, out_send, out_recv, query_send, query_recv, pair_send, pair_recv,
    *sum_refs,
):
    blocks, packed = grad_ref.shape[0], grad_ref.shape[1]
    rows = 2 * packed // 3
    micro, _, width = input_grad.shape
    heads = qa.shape[0]
    chips = blocks // 2
    dp = lax.axis_index("dp")
    me = lax.axis_index("blk")
    z = me // 2
    core = lax.rem(me, 2)
    lane = lax.broadcasted_iota(jnp.int32, (rows, LANES), 1)
    sums = Sums.gather(final, sum_refs[:26])
    units = UnitSum(sums, unit_final, sum_refs[26:])
    count = sums.count
    arrived = greet(dp, me, blocks, (sums.along_x, sums.along_y))

    def load(block):
        return pltpu.make_async_copy(acts_in.at[block], acts.at[block], load_acts.at[block])

    def load_head(number):
        src = (qa_in, ka_in, va_in, o_in)[number]
        return pltpu.make_async_copy(src, (qa, ka, va, out)[number], load_heads.at[number])

    order = [9, 0, 1, 2, 3, 8, 4, 5, 6, 7, 10, 11]
    for block in order[:3]:
        load(block).start()
    arrived()

    kinds = {
        "grad": (grad_ref, received, out_send, out_recv),
        "query": (send_query, got_query, query_send, query_recv),
        "pair": (send_pair, got_pair, pair_send, pair_recv),
    }

    def send(kind, block):
        src, dst, send_sem, recv_sem = kinds[kind]
        return pltpu.make_async_remote_copy(
            src_ref=src.at[block],
            dst_ref=dst.at[me],
            send_sem=send_sem.at[block],
            recv_sem=recv_sem.at[me],
            device_id=(dp, block),
            device_id_type=MESH,
        )

    def arrive(kind, block):
        src, dst, send_sem, recv_sem = kinds[kind]
        return pltpu.make_async_remote_copy(
            src_ref=src.at[block],
            dst_ref=dst.at[block],
            send_sem=send_sem.at[block],
            recv_sem=recv_sem.at[block],
            device_id=(dp, block),
            device_id_type=MESH,
        )

    for step in range(4):
        for row in range(2):
            block = 2 * far_order(z, jnp.int32(step)) + row

            @pl.when(block != me)
            def _():
                send("grad", block).start()

    for block in order[3:]:
        load(block).start()
    for number in range(4):
        load_head(number).start()
    received[me] = grad_ref[me]

    def message(number):
        return 2 * far_order(z, number // 2) + lax.rem(core + number, 2)

    def slot(time):
        for kind, starts in (("pair", PAIR_SLOTS), ("query", QUERY_SLOTS)):
            for number, start in enumerate(starts):
                block = message(jnp.int32(2 * chips - 1 if number == 2 * chips - 2 else number))

                @pl.when(time == start)
                def _():
                    send(kind, block).start()

        sums.tick(OUT, OUT_AT, time, count)
        sums.tick(BACK, BACK_AT, time - LATE, count)

    parts = (count // 2 - 1) // 2
    side = sums.half

    def weigh(piece):
        whole = piece // 2
        left = jnp.where(whole < parts, whole, jnp.where(whole < 2 * parts, 2 * parts, 2 * parts + 2))
        right = jnp.where(whole < parts, 2 * parts + 1, jnp.where(whole < 2 * parts, whole, 2 * parts + 3))
        cols = pl.ds(pl.multiple_of(lax.rem(piece, 2) * side, LANES), side)
        turn = lax.rem(piece, GIVE)

        @pl.when(piece >= GIVE)
        def _():
            sums.to_core(piece - GIVE, give.at[turn]).wait_send()

        operand = acts[right, :, cols]
        theirs = pl.ds(pl.multiple_of((1 - core) * side, LANES), side)
        give[turn] = dot_tn(acts[left, :, theirs], operand).astype(bf16)
        sums.to_core(piece, give.at[turn]).start()
        ours = pl.ds(pl.multiple_of(core * side, LANES), side)
        sums.own[piece] = dot_tn(acts[left, :, ours], operand).astype(bf16)

    per_slot = count // EARLY
    for number in range(EARLY):
        if number == 0:
            for block in order[:5]:
                load(block).wait()
        if number == 2:
            for block in order[5:]:
                load(block).wait()

        @pl.loop(0, per_slot)
        def _(turn):
            weigh(number * per_slot + turn)

        slot(jnp.int32(number))

    squares = [(wq_in, 0), (wkv_in, 0), (wkv_in, width)]
    tall = acts.shape[1]

    def late():
        copies = [
            pltpu.make_async_copy(normed_in.at[chip], acts.at[chip], load_late.at[chip]) for chip in range(chips)
        ]
        for number, (src, start) in enumerate(squares):
            cols = pl.ds(start, width)
            copies.append(
                pltpu.make_async_copy(
                    src.at[pl.ds(0, tall), cols], acts.at[chips + 2 * number], load_late.at[chips + 2 * number]
                )
            )
            copies.append(
                pltpu.make_async_copy(
                    src.at[pl.ds(tall, width - tall), cols],
                    acts.at[chips + 2 * number + 1, pl.ds(0, width - tall)],
                    load_late.at[chips + 2 * number + 1],
                )
            )
        for row in range(micro):
            copies.append(
                pltpu.make_async_copy(
                    x_in.at[row],
                    acts.at[chips + 6, pl.ds(row * rows, rows)],
                    load_late.at[chips + 6 + row],
                )
            )
        return copies

    for copy in late():
        copy.start()

    dqt[...] = jnp.zeros_like(dqt)
    for number in range(4):
        load_head(number).wait()

    @pl.loop(0, blocks)
    def _(block):
        here = pl.ds(pl.multiple_of(block * rows, rows), rows)
        for head in range(heads):
            key = ka[head, here, :][:, :HEAD].astype(f32)
            key_turned[head, :, here] = jnp.transpose(key).astype(bf16)
            query = qa[head, here, :][:, :HEAD]
            right_key[head, here, :] = jnp.concatenate([jnp.zeros_like(query), query], 1)

    @pl.loop(0, blocks)
    def _(step):
        block = 2 * chip_order(z, step // 2) + lax.rem(core + step, 2)

        @pl.when(block != me)
        def _():
            arrive("grad", block).wait_recv()

        here = pl.ds(pl.multiple_of(block * rows, rows), rows)
        wide = received[block, :rows, :].astype(f32)
        narrow = received[block, rows:, :].astype(f32)
        shares = heads_of(wide * out[block, :rows, :].astype(f32), narrow * out[block, rows:, :].astype(f32))
        gap = jnp.zeros((rows, LANES - HEAD), f32)
        for head, piece in enumerate(heads_of(wide, narrow)):
            delta = jnp.sum(shares[head], -1, keepdims=True)
            value = jnp.concatenate([piece, gap], 1)
            doa[head, here, :] = (value + spread(delta, HEAD, lane)).astype(bf16)

    wide_rows = 2 * rows
    eye = lax.broadcasted_iota(jnp.int32, (wide_rows, wide_rows), 0) == lax.broadcasted_iota(
        jnp.int32, (wide_rows, wide_rows), 1
    )
    half = LANES

    def pull(keys, queries, diagonal=False):
        found = []
        for head in range(heads):
            k = ka[head, keys, :]
            q = qa[head, queries, :]
            g = doa[head, queries, :]
            at = lax.broadcasted_iota(jnp.int32, k.shape, 1)
            s = dot_nt(k, q)
            if diagonal:
                bare = (at < HEAD) | (at > HEAD + CODES)
                s = jnp.where(eye, dot_nt(jnp.where(bare, k, 0.0).astype(bf16), q), s)
            p = jnp.exp(s)
            ds = (p * dot_nt(va[head, keys, :], g)).astype(bf16)
            left = jnp.concatenate([p.astype(bf16), ds], 1)
            at = lax.broadcasted_iota(jnp.int32, g.shape, 1)
            value = jnp.where(at < HEAD, g, 0.0).astype(bf16)
            right = jnp.concatenate([value, right_key[head, queries, :]], 0)
            found.append((dot_nn(left, right), dot_nn(key_turned[head, :, keys], ds)))
        return found

    @pl.loop(0, chips)
    def _(step):
        chip = far_order(z, step)
        here = pl.ds(pl.multiple_of(chip * wide_rows, wide_rows), wide_rows)
        for head, (pair, query) in enumerate(pull(here, here, True)):
            dvk[head] = pair
            dqt[head, :, here] += query
        time = EARLY
        for earlier in range(chips - 1):
            done = far_order(z, earlier)
            bodies = chips - done + jnp.where(done > 0, 1, 0)
            time = time + jnp.where(earlier < step, bodies, 0)
        slot(time)

        @pl.loop(chip + 1, chips)
        def _(other):
            there = pl.ds(pl.multiple_of(other * wide_rows, wide_rows), wide_rows)
            for head, (pair, query) in enumerate(pull(here, there)):
                dvk[head] += pair
                dqt[head, :, there] += query
            slot(time + other - chip)

        @pl.when(chip > 0)
        def _():
            edge = chip * wide_rows
            keys = pl.ds(pl.multiple_of(edge, half), half)
            queries = pl.ds(pl.multiple_of(edge - half, half), half)
            for head, (pair, query) in enumerate(pull(keys, queries)):
                dvk[head, :half] += pair
                dqt[head, :, queries] += query
            slot(time + chips - chip)

        for turn in range(2):
            block = 2 * chip + turn
            for head in range(heads):
                send_pair[block, head * rows : (head + 1) * rows, :] = dvk[
                    head, turn * rows : (turn + 1) * rows
                ].astype(bf16)

            @pl.when(block == me)
            def _():
                got_pair[me] = send_pair[me]

    @pl.loop(0, blocks)
    def _(step):
        block = step
        here = pl.ds(pl.multiple_of(block * rows, rows), rows)
        wide, narrow = pack_heads(
            [(jnp.transpose(dqt[h, :, here]) * (HEAD**-0.5)).astype(bf16) for h in range(heads)]
        )
        send_query[block, :rows, :] = wide
        send_query[block, rows:, :] = narrow

        @pl.when(block == me)
        def _():
            got_query[me] = send_query[me]

    for copy in late():
        copy.wait()

    for turn in range(2):
        which = 1 - core if turn == 0 else core
        cols = pl.ds(pl.multiple_of(which * side, LANES), side)
        unit[...] = jnp.zeros_like(unit)

        @pl.loop(0, chips)
        def _(chip):
            tiles = []
            for block in (2 * chip, 2 * chip + 1):
                query = heads_of(send_query[block, :rows, :], send_query[block, rows:, :])
                tile = [send_pair[block, head * rows : (head + 1) * rows, :] for head in range(heads)]
                tile += query + [jnp.zeros((rows, LANES - HEAD), bf16)]
                tiles.append(jnp.concatenate(tile, 1))
            unit[...] += dot_tn(acts[chip, :, cols], jnp.concatenate(tiles, 0))

        if turn == 0:
            units.give[...] = unit[...].astype(bf16)
            units.step(0)
        else:
            units.own[...] = unit[...].astype(bf16)
        slot(jnp.int32(EARLY + 13 + turn))

    ready = EARLY + 15
    end = LATE + count + BACK_AT[-1]
    spots = [int(ready + place) for place in UNIT_SLOTS]

    def last(row):
        query = columns_of(got_query, row, rows, blocks)
        keys, values = [], []
        for chip in range(chips):
            for head in range(heads):
                both = got_pair[2 * chip + row, head * rows : (head + 1) * rows, :]
                keys.append(both[:, HEAD:])
                values.append(both[:, :HEAD])
        grad = []
        for part in range(2):
            height = tall if part == 0 else width - tall
            total = jnp.zeros((rows, height), f32)
            for number, operand in enumerate(
                (query, jnp.concatenate(keys, 1), jnp.concatenate(values, 1))
            ):
                total = total + dot_nt(operand, acts[chips + 2 * number + part, :height])
            grad.append(total)
        grad = jnp.concatenate(grad, 1)
        unit_, scale = normal(acts[chips + 6, row * rows : (row + 1) * rows, :].astype(f32))
        gain = gain_ref[...].reshape(1, width)
        input_grad[row] = (mixed_grad_ref[row] + normal_pull(grad * gain, unit_, scale)).astype(bf16)

    @pl.loop(ready, max(end, spots[-1] + 1, QUERY_SLOTS[-1] + 1))
    def _(time):
        for number, spot in enumerate(spots):

            @pl.when(time == spot)
            def _():
                units.step(number + 1)

        slot(time)

    @pl.loop(0, blocks)
    def _(block):
        @pl.when(block != me)
        def _():
            arrive("query", block).wait_recv()
            arrive("pair", block).wait_recv()

    for row in range(micro):
        last(row)

    @pl.loop(0, blocks)
    def _(block):
        @pl.when(block != me)
        def _():
            send("grad", block).wait_send()
            send("query", block).wait_send()
            send("pair", block).wait_send()

    for piece in range(count - GIVE, count):
        sums.to_core(piece, give.at[piece % GIVE]).wait_send()

    @pl.loop(0, count)
    def _(piece):
        sums.finish(piece)

    units.finish()


def dense_kernel(
    received, x_ref, up_ref, gain_ref, wo_in, we_in, wc_in,
    result_ref, mixed_grad_ref, attended_grad_ref, acts_out,
    wo, we, wc, acts, mixed, result_acc, second_acc, load, store,
):
    micro, rows, width = x_ref.shape
    blocks = received.shape[0]
    parts = we.shape[0]
    chips = blocks // 2
    heads = width // HEAD // chips
    fetch = [pltpu.make_async_copy(wo_in, wo, load.at[0])]
    for part in range(parts):
        cols = pl.ds(part * width, width)
        fetch.append(pltpu.make_async_copy(we_in.at[:, cols], we.at[part], load.at[1 + 2 * part]))
        fetch.append(pltpu.make_async_copy(wc_in.at[cols, :], wc.at[part], load.at[2 + 2 * part]))
    for copy in fetch:
        copy.start()

    def keep(block):
        return pltpu.make_async_copy(acts.at[block], acts_out.at[block], store.at[block])

    gain = gain_ref[...].reshape(1, width)
    low, up, attended, branch = 2 * parts, 2 * parts + 1, 2 * parts + 2, 2 * parts + 3
    for row in range(micro):
        at = slice(row * rows, (row + 1) * rows)
        acts[attended, at, :] = columns_of(received, row, rows, blocks)
        acts[up, at, :] = up_ref[row]
    fetch[0].wait()
    mixed[...] = dot_nn(acts[attended], wo[...])
    for row in range(micro):
        at = slice(row * rows, (row + 1) * rows)
        mixed[at, :] += x_ref[row].astype(f32)
        unit, _ = normal(mixed[at, :])
        acts[low, at, :] = (unit * gain).astype(bf16)
    result_acc[...] = mixed[...]
    second_acc[...] = jnp.zeros_like(second_acc)
    for block in (up, attended, low):
        keep(block).start()

    for part in range(parts):
        fetch[1 + 2 * part].wait()
        fetch[2 + 2 * part].wait()

        @pl.loop(0, micro)
        def _(row):
            at = pl.ds(pl.multiple_of(row * rows, rows), rows)
            hidden = dot_nn(acts[low, at, :], we[part])
            active_grad = dot_nt(acts[up, at, :], wc[part])
            square = hidden * hidden
            c = 0.7978845608028654
            bend = jnp.tanh(hidden * (c + 0.044715 * c * square))
            gate = 0.5 + 0.5 * bend
            slope = gate + 0.5 * hidden * (1.0 - bend * bend) * (c + 3.0 * 0.044715 * c * square)
            active = (hidden * gate).astype(bf16)
            grad = (active_grad * slope).astype(bf16)
            acts[part, at, :] = active
            acts[parts + part, at, :] = grad
            result_acc[at, :] += dot_nn(active, wc[part])
            second_acc[at, :] += dot_nt(grad, we[part])

        keep(part).start()
        keep(parts + part).start()

    for row in range(micro):
        at = slice(row * rows, (row + 1) * rows)
        unit, scale = normal(mixed[at, :])
        grad = acts[up, at, :].astype(f32) + normal_pull(second_acc[at, :] * gain, unit, scale)
        mixed_grad_ref[row] = grad
        acts[branch, at, :] = grad.astype(bf16)
    keep(branch).start()
    back = dot_nt(acts[branch], wo[...]).astype(bf16)
    for row in range(micro):
        at = slice(row * rows, (row + 1) * rows)
        result_ref[row] = result_acc[at, :].astype(bf16)
        for chip in range(chips):
            start = chip * heads * HEAD
            wide, narrow = pack_heads(
                [back[at, start + h * HEAD : start + (h + 1) * HEAD] for h in range(heads)]
            )
            attended_grad_ref[2 * chip + row, :rows, :] = wide
            attended_grad_ref[2 * chip + row, rows:, :] = narrow
    for block in range(2 * parts + 4):
        keep(block).wait()


def final_kernel(
    final, we_ref, unit_ref, first_gain, second_gain, wq_ref, wkv_ref,
    first_ref, query_ref, pair_ref, output_ref, second_ref, expand_ref, contract_ref,
    first_acc, second_acc,
):
    step = pl.program_id(0)
    width = wq_ref.shape[0]
    chips = unit_ref.shape[0]
    heads = width // HEAD // chips
    parts = (pl.num_programs(0) - 4) // 2

    def fold(array):
        return sum(array[:, i : i + LANES] for i in range(0, width, LANES))

    @pl.when(step == 0)
    def _():
        first_acc[...] = jnp.zeros_like(first_acc)
        second_acc[...] = jnp.zeros_like(second_acc)

    @pl.when(step < parts)
    def _():
        contract_ref[...] = final[0].astype(f32)

    @pl.when((step >= parts) & (step < 2 * parts))
    def _():
        value = final[0].astype(f32)
        expand_ref[...] = value
        second_acc[...] += fold(value * we_ref[...].astype(f32))

    @pl.when(step == 2 * parts)
    def _():
        output_ref[...] = final[0].astype(f32)

    def columns(place):
        return jnp.concatenate(
            [unit_ref[chip][:, place(head) : place(head) + HEAD] for chip in range(chips) for head in range(heads)], 1
        ).astype(f32)

    @pl.when(step == 2 * parts + 1)
    def _():
        value = columns(lambda head: heads * LANES + head * HEAD)
        query_ref[...] = value
        first_acc[...] += fold(value * wq_ref[...].astype(f32))

    for side in range(2):

        @pl.when(step == 2 * parts + 2 + side)
        def _():
            value = columns(lambda head: head * LANES + (HEAD if side == 0 else 0))
            pair_ref[...] = value
            first_acc[...] += fold(value * wkv_ref[:, side * width : (side + 1) * width].astype(f32))

    @pl.when(step == pl.num_programs(0) - 1)
    def _():
        first_ref[...] = jnp.sum(jnp.transpose(first_acc[...]), 0) / first_gain[...]
        second_ref[...] = jnp.sum(jnp.transpose(second_acc[...]), 0) / second_gain[...]


VMEM = pl.BlockSpec(memory_space=pltpu.VMEM)
SMEM = pl.BlockSpec(memory_space=pltpu.SMEM)
ANY = pl.BlockSpec(memory_space=pl.ANY)


def attention_forward(inputs, gain, lengths, views, padding, query_weight, pair_weight, blocks):
    micro, rows, width = inputs.shape
    total = rows * blocks
    heads = width // HEAD // (blocks // micro)
    packed = rows * heads // 2
    shape = jax.ShapeDtypeStruct
    dma = pltpu.SemaphoreType.DMA
    unit = (heads, total, LANES)
    return pl.pallas_call(
        forward_kernel,
        out_shape=(
            shape((blocks // 2, 2 * rows, width), bf16),
            shape(unit, bf16),
            shape(unit, bf16),
            shape(unit, bf16),
            shape((blocks, packed, LANES), bf16),
            shape((blocks, packed, LANES), bf16),
        ),
        in_specs=[SMEM, SMEM] + [VMEM] * 5,
        out_specs=(ANY,) * 5 + (VMEM,),
        scratch_shapes=[
            pltpu.VMEM((blocks, rows, width), bf16),
            pltpu.VMEM(unit, bf16),
            pltpu.VMEM(unit, bf16),
            pltpu.VMEM(unit, bf16),
            pltpu.VMEM(unit, f32),
            pltpu.VMEM((width, heads * 3 * LANES), bf16),
            pltpu.VMEM((rows, width), bf16),
            pltpu.VMEM(unit, f32),
            pltpu.VMEM((blocks, packed, LANES), bf16),
            dma,
            dma,
            dma((blocks, 2)),
            dma((blocks,)),
            dma((blocks,)),
            dma((blocks,)),
            dma((blocks, 5)),
        ],
        compiler_params=pltpu.CompilerParams(
            collective_id=0, has_side_effects=True, vmem_limit_bytes=50 << 20
        ),
        name="attention_forward",
    )(lengths, views, inputs, gain, padding, query_weight, pair_weight)


def attention_backward(grad, mixed_grad, gain, acts, normed, qa, ka, va, out, query_weight, pair_weight, inputs):
    micro, rows, width = inputs.shape
    blocks, packed, _ = grad.shape
    heads, total, _ = qa.shape
    chips = blocks // 2
    pieces = acts.shape[0] - 3
    count = 2 * pieces
    unit_lanes = (heads + 2) * LANES
    side = width // 2
    shape = jax.ShapeDtypeStruct
    dma = pltpu.SemaphoreType.DMA
    unit = pltpu.VMEM((heads, total, LANES), bf16)
    message = pltpu.VMEM((blocks, packed, LANES), bf16)
    pair = pltpu.VMEM((blocks, heads * rows, LANES), bf16)
    return pl.pallas_call(
        backward_kernel,
        out_shape=(
            shape(inputs.shape, bf16),
            shape((pieces, width, width), bf16),
            shape((chips, width, unit_lanes), bf16),
        ),
        in_specs=[VMEM] * 3 + [ANY] * 9,
        out_specs=(VMEM, ANY, ANY),
        scratch_shapes=[
            pltpu.VMEM(acts.shape, bf16),
            unit,
            unit,
            unit,
            message,
            message,
            unit,
            unit,
            pltpu.VMEM((heads, HEAD, total), bf16),
            pltpu.VMEM((heads, HEAD, total), f32),
            pltpu.VMEM((heads, 2 * rows, LANES), f32),
            message,
            pair,
            message,
            pair,
            pltpu.VMEM((side, unit_lanes), f32),
            pltpu.VMEM((GIVE, side, side), bf16),
            dma((acts.shape[0],)),
            dma((4,)),
            dma((chips + 6 + micro,)),
        ]
        + [dma((blocks,))] * 6
        + Sums.scratch(count, side, side)
        + UnitSum.scratch(chips, side, unit_lanes),
        compiler_params=pltpu.CompilerParams(
            collective_id=1, has_side_effects=True, vmem_limit_bytes=62 << 20
        ),
        name="attention_backward",
    )(grad, mixed_grad, gain, acts, normed, qa, ka, va, out, query_weight, pair_weight, inputs)


def dense(received, inputs, cotangent, gain, output_weight, expand_weight, contract_weight):
    micro, rows, width = inputs.shape
    tokens = micro * rows
    parts = expand_weight.shape[1] // width
    shape = jax.ShapeDtypeStruct
    dma = pltpu.SemaphoreType.DMA
    acts = (2 * parts + 4, tokens, width)
    return pl.pallas_call(
        dense_kernel,
        out_shape=(
            shape((micro, rows, width), bf16),
            shape((micro, rows, width), f32),
            shape(received.shape, bf16),
            shape(acts, bf16),
        ),
        in_specs=[VMEM] * 4 + [ANY] * 3,
        out_specs=(VMEM,) * 3 + (ANY,),
        scratch_shapes=[
            pltpu.VMEM((width, width), bf16),
            pltpu.VMEM((parts, width, width), bf16),
            pltpu.VMEM((parts, width, width), bf16),
            pltpu.VMEM(acts, bf16),
            pltpu.VMEM((tokens, width), f32),
            pltpu.VMEM((tokens, width), f32),
            pltpu.VMEM((tokens, width), f32),
            dma((1 + 2 * parts,)),
            dma((acts[0],)),
        ],
        compiler_params=pltpu.CompilerParams(vmem_limit_bytes=56 << 20),
        name="dense",
    )(received, inputs, cotangent, gain, output_weight, expand_weight, contract_weight)


def finish(final, unit_final, first_gain, second_gain, query_weight, pair_weight, expand_weight):
    pieces, width, _ = final.shape
    steps = pieces + 3
    parts = (pieces - 1) // 2
    shape = jax.ShapeDtypeStruct
    square = (width, width)

    def whole(array):
        return pl.BlockSpec(array.shape, lambda p: (0,) * array.ndim)

    def clip(p, start, count):
        return jnp.clip(p - start, 0, count - 1)

    fixed = (unit_final, first_gain, second_gain, query_weight, pair_weight)
    row = pl.BlockSpec((width,), lambda p: (0,))
    return pl.pallas_call(
        final_kernel,
        grid=(steps,),
        out_shape=(
            shape((width,), f32),
            shape(square, f32),
            shape((width, 2 * width), f32),
            shape(square, f32),
            shape((width,), f32),
            shape((width, parts * width), f32),
            shape((parts * width, width), f32),
        ),
        in_specs=[
            pl.BlockSpec((1,) + square, lambda p: (clip(p, 0, pieces), 0, 0)),
            pl.BlockSpec(square, lambda p: (0, clip(p, parts, parts))),
        ]
        + [whole(array) for array in fixed],
        out_specs=(
            row,
            pl.BlockSpec(square, lambda p: (0, 0)),
            pl.BlockSpec(square, lambda p: (0, clip(p, 2 * parts + 2, 2))),
            pl.BlockSpec(square, lambda p: (0, 0)),
            row,
            pl.BlockSpec(square, lambda p: (0, clip(p, parts, parts))),
            pl.BlockSpec(square, lambda p: (clip(p, 0, parts), 0)),
        ),
        scratch_shapes=[pltpu.VMEM((width, LANES), f32), pltpu.VMEM((width, LANES), f32)],
        compiler_params=pltpu.CompilerParams(vmem_limit_bytes=56 << 20),
        name="finish",
    )(final, expand_weight, *fixed)


def layer_norm(value, gain):
    mean = jnp.mean(value, -1, keepdims=True)
    centred = value - mean
    spread = jnp.mean(centred * centred, -1, keepdims=True)
    return centred * lax.rsqrt(spread + epsilon) * gain


def token_info(lengths, views, positions):
    ends = jnp.cumsum(lengths)
    starts = ends - lengths
    inside = (positions[:, None] >= starts[None, :]) & (positions[:, None] < ends[None, :])
    number = jnp.arange(lengths.shape[0], dtype=jnp.int32)
    item = jnp.sum(jnp.where(inside, number[None, :], 0), 1)
    first = jnp.sum(jnp.where(inside, starts[None, :], 0), 1)
    span = jnp.sum(jnp.where(inside, views[None, :], 0), 1) * PATCHES
    frame = (positions - first) // span
    return (item, frame)


def visible(query_pos, query_item, query_frame, key_pos, key_item, key_frame, key_pad):
    same = query_item[:, None] == key_item[None, :]
    order = key_frame[None, :] <= query_frame[:, None]
    usable = (key_pad[None, :] == 1) | (query_pos[:, None] == key_pos[None, :])
    return same & order & usable


def in_blocks(update, carry, piece, block_rows):
    count = piece[0].shape[0]

    def advance(number, inner):
        begin = number * block_rows
        part = (
            lax.dynamic_slice_in_dim(piece[0], begin, block_rows),
            lax.dynamic_slice_in_dim(piece[1], begin, block_rows),
        )
        return update(inner, part, begin)

    return lax.fori_loop(0, count // block_rows, advance, carry)


def score_parts(query_heads, grad_heads, total, shift, key_heads, value_heads, mask, scale):
    scores = (
        jnp.einsum("qhd,khd->hqk", query_heads, key_heads, preferred_element_type=jnp.float32)
        * scale
    )
    chance = jnp.where(mask[None], jnp.exp(scores - total[..., None]), 0.0)
    chance_grad = jnp.einsum(
        "qhd,khd->hqk", grad_heads, value_heads, preferred_element_type=jnp.float32
    )
    score_grad = (chance * (chance_grad - shift[..., None])).astype(jnp.bfloat16)
    return (chance, score_grad)


def on_device(
    inputs,
    cotangent,
    lengths,
    view_counts,
    padding,
    first_gain,
    query_weight,
    key_value_weight,
    output_weight,
    second_gain,
    expand_weight,
    contract_weight,
):
    micro_count, row_count, width = inputs.shape
    head_count = width // HEAD
    scale = HEAD ** (-0.5)
    cycle_size = lax.axis_size("blk")
    own_start = lax.axis_index("blk") * row_count
    query_positions = own_start + jnp.arange(row_count, dtype=jnp.int32)
    gelu = partial(jax.nn.gelu, approximate=True)
    grads = tuple(
        (
            jnp.zeros(array.shape, jnp.float32)
            for array in (
                first_gain,
                query_weight,
                key_value_weight,
                output_weight,
                second_gain,
                expand_weight,
                contract_weight,
            )
        )
    )
    outputs = []
    input_grads = []
    for micro in range(micro_count):
        row_lengths = lengths[micro]
        row_views = view_counts[micro]
        row_pad = padding[micro]
        query_item, query_frame = token_info(row_lengths, row_views, query_positions)
        flat = inputs[micro].astype(jnp.float32)
        normed, first_pull = jax.vjp(layer_norm, flat, first_gain)
        normed_low = normed.astype(jnp.bfloat16)
        query = jnp.dot(normed_low, query_weight, preferred_element_type=jnp.float32).astype(
            jnp.bfloat16
        )
        pair = jnp.dot(normed_low, key_value_weight, preferred_element_type=jnp.float32).astype(
            jnp.bfloat16
        )
        keys = pair[:, :width]
        values = pair[:, width:]
        query_heads = query.reshape(row_count, head_count, HEAD)

        def mask_for(start, count):
            key_positions = start + jnp.arange(count, dtype=jnp.int32)
            key_item, key_frame = token_info(row_lengths, row_views, key_positions)
            key_pad = lax.dynamic_slice_in_dim(row_pad, start, count)
            return visible(
                query_positions,
                query_item,
                query_frame,
                key_positions,
                key_item,
                key_frame,
                key_pad,
            )

        def forward_block(carry, piece, start):
            count = piece[0].shape[0]
            mask = mask_for(start, count)

            def forward_work(state):
                peak, denominator, weighted = state
                key_heads = piece[0].reshape(count, head_count, HEAD)
                value_heads = piece[1].reshape(count, head_count, HEAD)
                scores = (
                    jnp.einsum(
                        "qhd,khd->hqk", query_heads, key_heads, preferred_element_type=jnp.float32
                    )
                    * scale
                )
                scores = jnp.where(mask[None], scores, lowest)
                new_peak = jnp.maximum(peak, jnp.max(scores, -1))
                raised = jnp.where(mask[None], jnp.exp(scores - new_peak[..., None]), 0.0)
                shrink = jnp.exp(peak - new_peak)
                denominator = denominator * shrink + jnp.sum(raised, -1)
                weighted = weighted * shrink[..., None] + jnp.einsum(
                    "hqk,khd->hqd",
                    raised.astype(jnp.bfloat16),
                    value_heads,
                    preferred_element_type=jnp.float32,
                )
                return (new_peak, denominator, weighted)

            return lax.cond(jnp.any(mask), forward_work, lambda state: state, carry)

        initial = (
            jnp.full((head_count, row_count), lowest, jnp.float32),
            jnp.zeros((head_count, row_count), jnp.float32),
            jnp.zeros((head_count, row_count, HEAD), jnp.float32),
        )
        peak, denominator, weighted = in_blocks(
            forward_block,
            initial,
            (
                lax.all_gather(keys, "blk", axis=0, tiled=True),
                lax.all_gather(values, "blk", axis=0, tiled=True),
            ),
            row_count,
        )
        attended_heads = weighted / denominator[..., None]
        log_total = peak + jnp.log(denominator)
        attended_low = (
            jnp.transpose(attended_heads, (1, 0, 2)).reshape(row_count, width).astype(jnp.bfloat16)
        )
        mixed = flat + jnp.dot(attended_low, output_weight, preferred_element_type=jnp.float32)
        second, second_pull = jax.vjp(layer_norm, mixed, second_gain)
        second_low = second.astype(jnp.bfloat16)
        hidden = jnp.dot(second_low, expand_weight, preferred_element_type=jnp.float32)
        activated, gelu_pull = jax.vjp(gelu, hidden)
        activated_low = activated.astype(jnp.bfloat16)
        output = mixed + jnp.dot(activated_low, contract_weight, preferred_element_type=jnp.float32)
        outputs.append(output.astype(jnp.bfloat16))
        upstream = cotangent[micro]
        grad_contract = jnp.einsum(
            "rf,rd->fd", activated_low, upstream, preferred_element_type=jnp.float32
        )
        activated_grad = jnp.einsum(
            "rd,fd->rf", upstream, contract_weight, preferred_element_type=jnp.float32
        )
        hidden_grad = gelu_pull(activated_grad)[0].astype(jnp.bfloat16)
        grad_expand = jnp.einsum(
            "rd,rf->df", second_low, hidden_grad, preferred_element_type=jnp.float32
        )
        second_grad = jnp.einsum(
            "rf,df->rd", hidden_grad, expand_weight, preferred_element_type=jnp.float32
        )
        mixed_part, grad_second = second_pull(second_grad)
        mixed_grad = upstream.astype(jnp.float32) + mixed_part
        branch_grad = mixed_grad.astype(jnp.bfloat16)
        grad_output = jnp.einsum(
            "rd,re->de", attended_low, branch_grad, preferred_element_type=jnp.float32
        )
        attended_grad = jnp.einsum(
            "re,de->rd", branch_grad, output_weight, preferred_element_type=jnp.float32
        ).astype(jnp.bfloat16)
        grad_heads = attended_grad.reshape(row_count, head_count, HEAD)
        delta = jnp.sum(
            jnp.transpose(grad_heads, (1, 0, 2)).astype(jnp.float32) * attended_heads, -1
        )

        def backward_block(carry, piece, start):
            count = piece[0].shape[0]
            mask = mask_for(start, count)

            def backward_work(state):
                query_sum, pair_terms = state
                key_heads = piece[0].reshape(count, head_count, HEAD)
                value_heads = piece[1].reshape(count, head_count, HEAD)
                chance, score_grad = score_parts(
                    query_heads, grad_heads, log_total, delta, key_heads, value_heads, mask, scale
                )
                value_term = jnp.einsum(
                    "hqk,qhd->khd",
                    chance.astype(jnp.bfloat16),
                    grad_heads,
                    preferred_element_type=jnp.float32,
                )
                query_sum = (
                    query_sum
                    + jnp.einsum(
                        "hqk,khd->qhd", score_grad, key_heads, preferred_element_type=jnp.float32
                    )
                    * scale
                )
                key_term = (
                    jnp.einsum(
                        "hqk,qhd->khd", score_grad, query_heads, preferred_element_type=jnp.float32
                    )
                    * scale
                )
                term = jnp.concatenate(
                    [key_term.reshape(count, width), value_term.reshape(count, width)], 1
                )
                previous = lax.dynamic_slice_in_dim(pair_terms, start, count)
                pair_terms = lax.dynamic_update_slice_in_dim(pair_terms, previous + term, start, 0)
                return (query_sum, pair_terms)

            return lax.cond(jnp.any(mask), backward_work, lambda state: state, carry)

        start_back = (
            jnp.zeros((row_count, head_count, HEAD), jnp.float32),
            jnp.zeros((row_count * cycle_size, 2 * width), jnp.float32),
        )
        back_state = in_blocks(
            backward_block,
            start_back,
            (
                lax.all_gather(keys, "blk", axis=0, tiled=True),
                lax.all_gather(values, "blk", axis=0, tiled=True),
            ),
            row_count,
        )
        query_sum, pair_terms = back_state
        pair_grad = lax.psum_scatter(
            pair_terms.astype(jnp.bfloat16), "blk", scatter_dimension=0, tiled=True
        )
        query_grad = query_sum.reshape(row_count, width).astype(jnp.bfloat16)
        grad_query = jnp.einsum(
            "rd,re->de", normed_low, query_grad, preferred_element_type=jnp.float32
        )
        grad_pair = jnp.einsum(
            "rd,re->de", normed_low, pair_grad, preferred_element_type=jnp.float32
        )
        normed_grad = jnp.einsum(
            "re,de->rd", query_grad, query_weight, preferred_element_type=jnp.float32
        )
        normed_grad = normed_grad + jnp.einsum(
            "re,de->rd", pair_grad, key_value_weight, preferred_element_type=jnp.float32
        )
        input_part, grad_first = first_pull(normed_grad)
        input_grads.append((mixed_grad + input_part).astype(jnp.bfloat16))
        terms = (
            grad_first,
            grad_query,
            grad_pair,
            grad_output,
            grad_second,
            grad_expand,
            grad_contract,
        )
        grads = tuple((total + term for total, term in zip(grads, terms)))
    summed = lax.psum(
        (grads[0], grads[1], grads[2], grads[3], grads[4], grads[5], grads[6]), ("dp", "blk")
    )
    return (
        jnp.stack(outputs),
        jnp.stack(input_grads),
        summed[0],
        summed[1],
        summed[2],
        summed[3],
        summed[4],
        summed[5],
        summed[6],
    )


def fast_on_device(
    inputs, cotangent, lengths, view_counts, padding, first_gain, query_weight, key_value_weight,
    output_weight, second_gain, expand_weight, contract_weight,
):
    normed, qa, ka, va, out, received = attention_forward(
        inputs, first_gain, lengths, view_counts, padding, query_weight, key_value_weight, lax.axis_size("blk")
    )
    result, mixed_grad, attended_grad, acts = dense(
        received, inputs, cotangent, second_gain, output_weight, expand_weight, contract_weight
    )
    input_grad, final, unit_final = attention_backward(
        attended_grad, mixed_grad, first_gain, acts, normed, qa, ka, va, out, query_weight, key_value_weight, inputs
    )
    first, query, pair, output, second, expand, contract = finish(
        final, unit_final, first_gain, second_gain, query_weight, key_value_weight, expand_weight
    )
    return result, input_grad, first, query, pair, output, second, expand, contract


def solution(mesh):
    placed = (
        P("dp", "blk", None),
        P("dp", "blk", None),
        P("dp", None),
        P("dp", None),
        P("dp", None),
    ) + (P(),) * 7

    def program(*arrays):
        inputs, lengths = arrays[0], arrays[2]
        dp, blk = mesh.shape["dp"], mesh.shape["blk"]
        rows, total, width = inputs.shape
        items = lengths.shape[1]
        chips = blk // 2
        fits = (
            (dp, blk) == (4, 8)
            and rows == 2 * dp
            and total % (blk * 2 * LANES) == 0
            and width % (LANES * HEAD // 64) == 0
            and width // HEAD == 3 * chips
            and total // PATCHES + items <= CODES
        )
        return jax.shard_map(
            fast_on_device if fits else on_device,
            mesh=mesh,
            in_specs=placed,
            out_specs=(P("dp", "blk", None), P("dp", "blk", None)) + (P(),) * 7,
            check_vma=False,
        )(*arrays)

    return program
```

```python
from functools import partial

import jax
import jax.numpy as jnp
from jax import lax
from jax.experimental import pallas as pl
from jax.experimental.pallas import tpu as pltpu
from jax.sharding import PartitionSpec as P

HEAD = 64
PATCHES = 64
CODES = 40
BIG = 1e30
EARLY = 12
OUT_AT = (0, 3, 6, 9, 12)
BACK_AT = (0, 3, 6, 9)
LATE = 13
GIVE = 3
PAIR_SLOTS = (18, 23, 28, 31, 34, 35, 28)
QUERY_SLOTS = (36, 37, 38, 39, 40, 40, 31)
PAIR_SUM_SLOTS = (0, 2, 4, 6, 9, 11, 14)
QUERY_SUM_SLOTS = (1, 3, 5, 8, 10, 12, 15)
PAIR_DONE = 40
OUT = (1, 2, 3, 4, 5)
BACK = (6, 7, 8, 9)
LANES = 128
MESH = pl.DeviceIdType.MESH
bf16 = jnp.bfloat16
f32 = jnp.float32

epsilon = 1e-05
lowest = -1e30


def dot_nn(a, b):
    return lax.dot_general(a, b, (((1,), (0,)), ((), ())), preferred_element_type=f32)


def dot_nt(a, b):
    return lax.dot_general(a, b, (((1,), (1,)), ((), ())), preferred_element_type=f32)


def dot_tn(a, b):
    return lax.dot_general(a, b, (((0,), (0,)), ((), ())), preferred_element_type=f32)


def chip_order(z, step):
    code = jnp.where(z == 0, 3210, jnp.where(z == 1, 3201, jnp.where(z == 2, 312, 123)))
    return digit(code, step)


def digit(code, step):
    power = jnp.where(step == 0, 1, jnp.where(step == 1, 10, jnp.where(step == 2, 100, 1000)))
    return lax.rem(code // power, 10)


def chip_span(z, step):
    low = jnp.where(z == 0, 0, jnp.where(z == 1, 1, jnp.where(z == 2, 112, 123)))
    high = jnp.where(z == 0, 3210, jnp.where(z == 1, 3211, jnp.where(z == 2, 3322, 3333)))
    return digit(low, step), digit(high, step)


def far_order(z, step):
    return jnp.where(
        step == 0,
        lax.rem(z + 2, 4),
        jnp.where(step == 1, 3 - z, jnp.where(step == 2, z + 1 - 2 * lax.rem(z, 2), z)),
    )


def features(block, rows, lengths, views, row, padded):
    lane = lax.broadcasted_iota(jnp.int32, (rows, LANES), 1) - HEAD
    position = block * rows + lax.broadcasted_iota(jnp.int32, (rows, LANES), 0)
    code = jnp.zeros((rows, LANES), jnp.int32)
    base = jnp.zeros((rows, LANES), jnp.int32)
    start = jnp.int32(0)
    first = jnp.int32(0)
    for item in range(lengths.shape[1]):
        length = lengths[row, item]
        view = views[row, item]
        offset = position - start
        inside = (offset >= 0) & (offset < length)
        frame = (offset >> 6) * (2 - view) + (offset >> 7) * (view - 1)
        code = jnp.where(inside, first + frame, code)
        base = jnp.where(inside, first, base)
        first = first + ((length + 63) >> 6) * (2 - view) + ((length + 127) >> 7) * (view - 1)
        start = start + length
    coded = (lane >= 0) & (lane < CODES)
    key = jnp.where(coded & (lane == code), 1.0, 0.0)
    key = jnp.where((lane > CODES) & (lane < CODES + 4), 1.0, key)
    key = jnp.where(lane == CODES, padded, key)
    hidden = (coded & ((lane < base) | (lane > code))) | (lane == CODES)
    query = jnp.where(hidden, -BIG, 0.0)
    return key, query


def three_parts(value):
    high = value.astype(bf16).astype(f32)
    rest = value - high
    middle = rest.astype(bf16).astype(f32)
    low = (rest - middle).astype(bf16).astype(f32)
    return high, middle, low


def spread(value, first, lane):
    high, middle, low = three_parts(value)
    return jnp.where(
        lane == first, high, jnp.where(lane == first + 1, middle, jnp.where(lane == first + 2, low, 0.0))
    )


def pack_heads(heads):
    half = heads[2].shape[0] // 2
    wide = jnp.concatenate([heads[0], heads[1]], 1)
    narrow = jnp.concatenate([heads[2][:half], heads[2][half:]], 1)
    return wide, narrow


def greet(dp, me, count, others=()):
    barrier = pltpu.get_barrier_semaphore()
    for step in range(1, count):
        pl.semaphore_signal(
            barrier, inc=1, device_id=(dp, lax.rem(me + step, count)), device_id_type=MESH
        )
    for other in others:
        pl.semaphore_signal(barrier, inc=1, device_id=other, device_id_type=MESH)
    return lambda: pl.semaphore_wait(barrier, count - 1 + len(others))


def heads_of(wide, narrow):
    return [
        wide[:, :HEAD],
        wide[:, HEAD:],
        jnp.concatenate([narrow[:, :HEAD], narrow[:, HEAD:]], 0),
    ]


def columns_of(received, row, rows, blocks):
    pieces = []
    for chip in range(blocks // 2):
        block = 2 * chip + row
        pieces += heads_of(received[block, :rows, :], received[block, rows:, :])
    return jnp.concatenate(pieces, 1)


def normal(value):
    mean = jnp.mean(value, -1, keepdims=True)
    centred = value - mean
    scale = lax.rsqrt(jnp.mean(centred * centred, -1, keepdims=True) + epsilon)
    return centred * scale, scale


def normal_pull(grad, unit, scale):
    return scale * (
        grad - jnp.mean(grad, -1, keepdims=True) - unit * jnp.mean(grad * unit, -1, keepdims=True)
    )


def forward_kernel(
    lengths, views, x_ref, gain_ref, pad_ref, wq_in, wkv_in,
    normed_out, qa_out, ka_out, va_out, o_out, received,
    normed, qa, ka, va, o_ref, weight, wq_ref, wkv_ref, stage, peak, outgoing,
    fetch, sib_send, sib_recv, line_send, line_recv, out_send, out_recv, store,
):
    rows, width = x_ref.shape[1], x_ref.shape[2]
    blocks = normed.shape[0]
    heads = qa.shape[0]
    dp = lax.axis_index("dp")
    me = lax.axis_index("blk")
    z = me // 2
    core = lax.rem(me, 2)
    sibling = me + 1 - 2 * core
    lane = lax.broadcasted_iota(jnp.int32, (rows, LANES), 1)

    arrived = greet(dp, me, blocks)
    loads = [
        pltpu.make_async_copy(wq_in, wq_ref, fetch.at[0]),
        pltpu.make_async_copy(wkv_in, wkv_ref, fetch.at[1]),
    ]
    for copy in loads:
        copy.start()
    gain = gain_ref[...].reshape(1, width)

    def norm(value):
        return (normal(value.astype(f32))[0] * gain).astype(bf16)

    normed[me] = norm(x_ref[core])
    arrived()

    def place(block):
        return pl.ds(pl.multiple_of(block * rows, rows), rows)

    def keep(block, number):
        here = place(block)
        src, dst = (
            (normed.at[block], normed_out.at[block // 2, pl.ds(pl.multiple_of(lax.rem(block, 2) * rows, rows), rows)]),
            (ka.at[:, here, :], ka_out.at[:, here, :]),
            (va.at[:, here, :], va_out.at[:, here, :]),
            (qa.at[:, here, :], qa_out.at[:, here, :]),
            (outgoing.at[block], o_out.at[block]),
        )[number]
        return pltpu.make_async_copy(src, dst, store.at[block, number])

    def line_copy(block, up):
        return pltpu.make_async_remote_copy(
            src_ref=normed.at[block],
            dst_ref=normed.at[block],
            send_sem=line_send.at[block, up],
            recv_sem=line_recv.at[block],
            device_id=(dp, me + (2 if up else -2)),
            device_id_type=MESH,
        )

    @pl.when(z < 3)
    def _():
        line_copy(me, 1).start()

    @pl.when(z > 0)
    def _():
        line_copy(me, 0).start()

    stage[...] = norm(x_ref[1 - core])
    sib_copy = pltpu.make_async_remote_copy(
        src_ref=stage,
        dst_ref=normed.at[me],
        send_sem=sib_send,
        recv_sem=sib_recv,
        device_id=(dp, sibling),
        device_id_type=MESH,
    )
    sib_copy.start()

    for copy in loads:
        copy.wait()
    gap = jnp.zeros((width, LANES - HEAD), bf16)
    for chip in range(blocks // 2):

        @pl.when(z == chip)
        def _():
            for head in range(heads):
                at = (chip * heads + head) * HEAD
                for kind, piece in enumerate(
                    (
                        wq_ref[:, at : at + HEAD],
                        wkv_ref[:, at : at + HEAD],
                        wkv_ref[:, width + at : width + at + HEAD],
                    )
                ):
                    column = (head * 3 + kind) * LANES
                    weight[:, column : column + LANES] = jnp.concatenate([piece, gap], 1)

    ones = jnp.where((lane >= HEAD) & (lane < HEAD + 3), -1.0, 0.0)

    def bring(step, turn):
        chip = chip_order(z, step)
        block = 2 * chip + lax.rem(core + turn, 2)

        @pl.when((step == 0) & (turn == 1))
        def _():
            pltpu.make_async_remote_copy(
                src_ref=stage,
                dst_ref=normed.at[sibling],
                send_sem=sib_send,
                recv_sem=sib_recv,
                device_id=(dp, sibling),
                device_id_type=MESH,
            ).wait_recv()

        @pl.when(step > 0)
        def _():
            pltpu.make_async_remote_copy(
                src_ref=normed.at[block],
                dst_ref=normed.at[block],
                send_sem=line_send.at[block, 0],
                recv_sem=line_recv.at[block],
                device_id=(dp, sibling),
                device_id_type=MESH,
            ).wait_recv()

        @pl.when((step + turn > 0) & (chip <= z) & (z < 3))
        def _():
            line_copy(block, 1).start()

        @pl.when((step + turn > 0) & (chip >= z) & (z > 0))
        def _():
            line_copy(block, 0).start()

        keep(block, 0).start()
        pad_row = 1.0 - pad_ref[pl.ds(core, 1), place(block)].astype(f32)
        padded = jnp.transpose(jnp.broadcast_to(pad_row, (LANES, rows)))
        key, query = features(block, rows, lengths, views, core, padded)
        out = dot_nn(normed[block], weight[...]).astype(bf16).astype(f32)
        here = pl.ds(pl.multiple_of(block * rows, rows), rows)
        for head in range(heads):
            at = head * 3 * LANES
            qa[head, here, :] = (out[:, at : at + LANES] * (HEAD**-0.5) + query).astype(bf16)
            ka[head, here, :] = (out[:, at + LANES : at + 2 * LANES] + key).astype(bf16)
            va[head, here, :] = (out[:, at + 2 * LANES : at + 3 * LANES] + ones).astype(bf16)
            peak[head, here, :] = jnp.full((rows, LANES), -BIG, f32)
            o_ref[head, here, :] = jnp.zeros((rows, LANES), f32)
        keep(block, 1).start()
        keep(block, 2).start()

    wide = 2 * rows
    eye = lax.broadcasted_iota(jnp.int32, (wide, wide), 0) == lax.broadcasted_iota(
        jnp.int32, (wide, wide), 1
    )

    def attend(queries, keys, diagonal=False):
        found = []
        for head in range(heads):
            query = qa[head, queries, :]
            key = ka[head, keys, :]
            s = dot_nt(query, key)
            if diagonal:
                s = jnp.where(eye, dot_nt(query[:, :HEAD], key[:, :HEAD]), s)
            tiles = [s[:, i : i + LANES] for i in range(0, s.shape[1], LANES)]
            top = tiles[0]
            for tile in tiles[1:]:
                top = jnp.maximum(top, tile)
            old = peak[head, queries, :]
            new = jnp.maximum(old, jnp.max(top, -1, keepdims=True))
            p = jnp.concatenate([jnp.exp(tile - new).astype(bf16) for tile in tiles], 1)
            total = o_ref[head, queries, :] * jnp.exp(old - new) + dot_nn(p, va[head, keys, :])
            found.append((new, total))
        for head, (new, total) in enumerate(found):
            peak[head, queries, :] = new
            o_ref[head, queries, :] = total

    def out_copy(block):
        return pltpu.make_async_remote_copy(
            src_ref=outgoing.at[block],
            dst_ref=received.at[me],
            send_sem=out_send.at[block],
            recv_sem=out_recv.at[me],
            device_id=(dp, block),
            device_id_type=MESH,
        )

    def hand_back(chip):
        @pl.loop(0, 2)
        def _(turn):
            block = 2 * chip + lax.rem(core + turn, 2)
            here = pl.ds(pl.multiple_of(block * rows, rows), rows)
            results = []
            for head in range(heads):
                total = o_ref[head, here, :]
                mass = -total[:, HEAD : HEAD + 1]
                results.append((total / mass)[:, :HEAD].astype(bf16))
                log_total = peak[head, here, :] + jnp.log(mass)
                qa[head, here, :] = (
                    qa[head, here, :].astype(f32) - spread(log_total, HEAD + CODES + 1, lane)
                ).astype(bf16)
            both, third = pack_heads(results)
            outgoing[block, :rows, :] = both
            outgoing[block, rows:, :] = third

            @pl.when(block == me)
            def _():
                received[me, :rows, :] = both
                received[me, rows:, :] = third

            @pl.when(block != me)
            def _():
                out_copy(block).start()

            keep(block, 3).start()
            keep(block, 4).start()

    def span(chip):
        return pl.ds(pl.multiple_of(chip * wide, wide), wide)

    def across(chip):
        edge = (chip + 1) * wide
        attend(
            pl.ds(pl.multiple_of(edge - LANES, LANES), LANES),
            pl.ds(pl.multiple_of(edge, LANES), LANES),
        )

    @pl.loop(0, blocks // 2)
    def _(step):
        @pl.loop(0, 2)
        def _(turn):
            bring(step, turn)

        chip = chip_order(z, step)
        low, high = chip_span(z, step)

        @pl.when(chip > low)
        def _():
            across(chip - 1)

        @pl.when(chip < high)
        def _():
            across(chip)

        @pl.when((low == 0) & (chip == high) & (chip > 0))
        def _():
            hand_back(chip - 1)

        @pl.loop(low, high + 1)
        def _(other):
            top = jnp.maximum(chip, other)

            @pl.when(other == chip)
            def _():
                attend(span(chip), span(chip), True)

            @pl.when(other != chip)
            def _():
                attend(span(top), span(jnp.minimum(chip, other)))

            @pl.when((other >= chip) & (low == 0) & (high >= jnp.minimum(top + 1, blocks // 2 - 1)))
            def _():
                hand_back(top)

    sib_copy.wait_send()

    @pl.loop(0, blocks)
    def _(block):
        for number in range(5):
            keep(block, number).wait()

        @pl.when((block // 2 <= z) & (z < 3))
        def _():
            line_copy(block, 1).wait_send()

        @pl.when((block // 2 >= z) & (z > 0))
        def _():
            line_copy(block, 0).wait_send()

        @pl.when(block != me)
        def _():
            out_copy(block).wait_send()
            pltpu.make_async_remote_copy(
                src_ref=outgoing.at[block],
                dst_ref=received.at[block],
                send_sem=out_send.at[block],
                recv_sem=out_recv.at[block],
                device_id=(dp, block),
                device_id_type=MESH,
            ).wait_recv()


class Sums:
    def __init__(self, final, own, buffers, semaphores, local):
        self.final, self.own, self.local = final, own, local
        self.from_core, self.first, self.second, self.line, self.near, self.far = buffers
        self.sems = dict(zip(
            ("core", "first", "second", "inward", "across", "outward", "back", "wide", "twin"), semaphores
        ))
        self.count = own.shape[0]
        self.half, self.lanes = own.shape[1], own.shape[2]
        self.quarter = self.half // 4
        self.eighth = self.half // 8
        self.dp = lax.axis_index("dp")
        self.me = lax.axis_index("blk")
        self.core = lax.rem(self.me, 2)
        self.z = self.me // 2
        self.x = lax.rem(self.dp, 2)
        self.y = self.dp // 2
        self.along_x = (self.dp + 1 - 2 * self.x, self.me)
        self.along_y = (self.dp + 2 - 4 * self.y, self.me)
        self.twin = (self.dp, self.me + 1 - 2 * self.core)
        self.inner = (self.z == 1) | (self.z == 2)
        self.outer = (self.z == 0) | (self.z == 3)
        self.pair = (self.dp, self.me + 2 - 4 * lax.rem(self.z, 2))
        self.middle = (self.dp, jnp.where(self.z < 2, self.me + 2, self.me - 2))

    def copy(self, name, piece, src, dst, device, way=None):
        send, recv = self.sems[name]
        at = (piece,) if way is None else (piece, way)
        return pltpu.make_async_remote_copy(
            src_ref=src,
            dst_ref=dst,
            send_sem=send.at[at],
            recv_sem=recv.at[at],
            device_id=device,
            device_id_type=MESH,
        )

    def rows(self, start, count):
        return pl.ds(pl.multiple_of(start, 16), count)

    def place(self, ref, piece, start, count):
        cols = pl.ds(pl.multiple_of(lax.rem(piece, 2) * self.lanes, LANES), self.lanes)
        return ref.at[piece // 2, self.rows(start, count), cols]

    def to_core(self, piece, src=None):
        src = self.own.at[piece] if src is None else src
        return self.copy("core", piece, src, self.from_core.at[piece], self.twin)

    def to_first(self, piece):
        q = self.quarter
        return (
            self.copy("first", piece, self.own.at[piece, self.rows(q * (1 - self.x), q)], self.first.at[piece, 0], self.along_x, 0),
            self.copy("first", piece, self.own.at[piece, self.rows(2 * q + q * (1 - self.y), q)], self.first.at[piece, 1], self.along_y, 1),
        )

    def to_second(self, piece):
        q, e = self.quarter, self.eighth
        return (
            self.copy("second", piece, self.own.at[piece, self.rows(q * self.x + e * (1 - self.y), e)], self.second.at[piece, 0], self.along_y, 0),
            self.copy("second", piece, self.own.at[piece, self.rows(2 * q + q * self.y + e * (1 - self.x), e)], self.second.at[piece, 1], self.along_x, 1),
        )

    def inward(self, piece):
        return self.copy("inward", piece, self.line.at[piece], self.near.at[piece], self.pair)

    def across(self, piece):
        return self.copy("across", piece, self.line.at[piece], self.far.at[piece], self.middle)

    def outward(self, piece):
        return self.copy("outward", piece, self.far.at[piece], self.near.at[piece], self.pair)

    def mine(self):
        q, e = self.quarter, self.eighth
        base = self.core * self.half
        return base + q * self.x + e * self.y, base + 2 * q + q * self.y + e * self.x

    def keep(self, piece, total):
        e = self.eighth
        one, two = self.mine()
        return (
            pltpu.make_async_copy(total.at[piece, :e], self.place(self.final, piece, one, e), self.local.at[piece, 0]),
            pltpu.make_async_copy(total.at[piece, e:], self.place(self.final, piece, two, e), self.local.at[piece, 1]),
        )

    def back(self, piece, total):
        e = self.eighth
        one, two = self.mine()
        return (
            self.copy("back", piece, total.at[piece, :e], self.place(self.final, piece, one, e), self.along_y, 0),
            self.copy("back", piece, total.at[piece, e:], self.place(self.final, piece, two, e), self.along_x, 1),
        )

    def wide(self, piece):
        q = self.quarter
        base = self.core * self.half
        one = self.place(self.final, piece, base + q * self.x, q)
        two = self.place(self.final, piece, base + 2 * q + q * self.y, q)
        return (
            self.copy("wide", piece, one, one, self.along_x, 0),
            self.copy("wide", piece, two, two, self.along_y, 1),
        )

    def to_twin(self, piece):
        part = self.place(self.final, piece, self.core * self.half, self.half)
        return self.copy("twin", piece, part, part, self.twin)

    def step_1(self, piece):
        self.to_core(piece).wait_recv()
        self.own[piece] = self.own[piece] + self.from_core[piece]
        for copy in self.to_first(piece):
            copy.start()

    def step_2(self, piece):
        q = self.quarter
        one, two = self.to_first(piece)
        one.wait_recv()
        at = self.rows(q * self.x, q)
        self.own[piece, at, :] = self.own[piece, at, :] + self.first[piece, 0]
        two.wait_recv()
        at = self.rows(2 * q + q * self.y, q)
        self.own[piece, at, :] = self.own[piece, at, :] + self.first[piece, 1]
        for copy in self.to_second(piece):
            copy.start()

    def step_3(self, piece):
        q, e = self.quarter, self.eighth
        one, two = self.to_second(piece)
        one.wait_recv()
        at = self.rows(q * self.x + e * self.y, e)
        self.line[piece, :e, :] = self.own[piece, at, :] + self.second[piece, 0]
        two.wait_recv()
        at = self.rows(2 * q + q * self.y + e * self.x, e)
        self.line[piece, e:, :] = self.own[piece, at, :] + self.second[piece, 1]

        @pl.when(self.outer)
        def _():
            self.inward(piece).start()

    def step_4(self, piece):
        @pl.when(self.inner)
        def _():
            self.inward(piece).wait_recv()
            self.line[piece] = self.line[piece] + self.near[piece]
            self.across(piece).start()

    def step_5(self, piece):
        @pl.when(self.inner)
        def _():
            self.across(piece).wait_recv()
            self.far[piece] = self.line[piece] + self.far[piece]
            self.outward(piece).start()

    def step_6(self, piece):
        @pl.when(self.outer)
        def _():
            self.outward(piece).wait_recv()
            for copy in self.back(piece, self.near) + self.keep(piece, self.near):
                copy.start()

        @pl.when(self.inner)
        def _():
            for copy in self.back(piece, self.far) + self.keep(piece, self.far):
                copy.start()

    def step_7(self, piece):
        for copy in self.keep(piece, self.near):
            copy.wait()
        for copy in self.back(piece, self.near):
            copy.wait_recv()
        for copy in self.wide(piece):
            copy.start()

    def step_8(self, piece):
        for copy in self.wide(piece):
            copy.wait_recv()
        self.to_twin(piece).start()

    def step_9(self, piece):
        self.to_twin(piece).wait_recv()

    def tick(self, numbers, offsets, time, last):
        for place in reversed(range(len(numbers))):
            piece = time - offsets[place]

            @pl.when((piece >= 0) & (piece < last))
            def _():
                getattr(self, "step_" + str(numbers[place]))(piece)

    def finish(self, piece):
        for copies in (self.to_first(piece), self.to_second(piece), self.back(piece, self.near), self.wide(piece)):
            for copy in copies:
                copy.wait_send()
        self.to_twin(piece).wait_send()

        @pl.when(self.outer)
        def _():
            self.inward(piece).wait_send()

        @pl.when(self.inner)
        def _():
            self.across(piece).wait_send()
            self.outward(piece).wait_send()

    @staticmethod
    def scratch(count, half, lanes):
        def array(*shape):
            return pltpu.VMEM((count,) + shape + (lanes,), bf16)

        quarter, eighth = half // 4, half // 8
        dma = pltpu.SemaphoreType.DMA
        one, two = [dma((count,))] * 2, [dma((count, 2))] * 2
        return (
            [array(half)] * 2
            + [array(2, quarter), array(2, eighth)]
            + [array(quarter)] * 3
            + one + two + two + one + one + one + two + two + one
            + [dma((count, 2))]
        )

    @classmethod
    def gather(cls, final, refs):
        sems = refs[7:25]
        pairs = [(sems[2 * i], sems[2 * i + 1]) for i in range(9)]
        return cls(final, refs[0], refs[1:7], pairs, refs[25])


class UnitSum:
    def __init__(self, sums, final, refs):
        self.sums, self.final = sums, final
        (
            self.own, self.give, self.from_core, self.first, self.second, self.line,
            self.core_sems, self.first_sems, self.second_sems, self.line_send, self.line_recv,
            self.back_sems, self.wide_sems, self.twin_sems, self.local,
        ) = refs

    def copy(self, sems, at, src, dst, device):
        return pltpu.make_async_remote_copy(
            src_ref=src,
            dst_ref=dst,
            send_sem=sems.at[0, at],
            recv_sem=sems.at[1, at],
            device_id=device,
            device_id_type=MESH,
        )

    def to_core(self):
        return self.copy(self.core_sems, 0, self.give, self.from_core, self.sums.twin)

    def to_first(self):
        s, q = self.sums, self.sums.quarter
        return (
            self.copy(self.first_sems, 0, self.own.at[s.rows(q * (1 - s.x), q)], self.first.at[0], s.along_x),
            self.copy(self.first_sems, 1, self.own.at[s.rows(2 * q + q * (1 - s.y), q)], self.first.at[1], s.along_y),
        )

    def to_second(self):
        s, q, e = self.sums, self.sums.quarter, self.sums.eighth
        return (
            self.copy(self.second_sems, 0, self.own.at[s.rows(q * s.x + e * (1 - s.y), e)], self.second.at[0], s.along_y),
            self.copy(self.second_sems, 1, self.own.at[s.rows(2 * q + q * s.y + e * (1 - s.x), e)], self.second.at[1], s.along_x),
        )

    def along_line(self, chip):
        s = self.sums
        return pltpu.make_async_remote_copy(
            src_ref=self.line.at[s.z],
            dst_ref=self.line.at[s.z],
            send_sem=self.line_send.at[chip],
            recv_sem=self.line_recv.at[s.z],
            device_id=(s.dp, 2 * chip + s.core),
            device_id_type=MESH,
        )

    def from_line(self, chip):
        s = self.sums
        return pltpu.make_async_remote_copy(
            src_ref=self.line.at[chip],
            dst_ref=self.line.at[chip],
            send_sem=self.line_send.at[chip],
            recv_sem=self.line_recv.at[chip],
            device_id=(s.dp, 2 * chip + s.core),
            device_id_type=MESH,
        )

    def keep(self):
        s, e = self.sums, self.sums.eighth
        one, two = s.mine()
        return (
            pltpu.make_async_copy(self.line.at[:, :e], self.final.at[:, s.rows(one, e)], self.local.at[0]),
            pltpu.make_async_copy(self.line.at[:, e:], self.final.at[:, s.rows(two, e)], self.local.at[1]),
        )

    def back(self):
        s, e = self.sums, self.sums.eighth
        one, two = s.mine()
        return (
            self.copy(self.back_sems, 0, self.line.at[:, :e], self.final.at[:, s.rows(one, e)], s.along_y),
            self.copy(self.back_sems, 1, self.line.at[:, e:], self.final.at[:, s.rows(two, e)], s.along_x),
        )

    def wide(self):
        s, q = self.sums, self.sums.quarter
        base = s.core * s.half
        one = self.final.at[:, s.rows(base + q * s.x, q)]
        two = self.final.at[:, s.rows(base + 2 * q + q * s.y, q)]
        return (
            self.copy(self.wide_sems, 0, one, one, s.along_x),
            self.copy(self.wide_sems, 1, two, two, s.along_y),
        )

    def to_twin(self):
        s = self.sums
        part = self.final.at[:, s.rows(s.core * s.half, s.half)]
        return self.copy(self.twin_sems, 0, part, part, s.twin)

    def step(self, number):
        s, q, e = self.sums, self.sums.quarter, self.sums.eighth
        if number == 0:
            self.to_core().start()
        elif number == 1:
            self.to_core().wait_recv()
            self.own[...] = self.own[...] + self.from_core[...]
            for copy in self.to_first():
                copy.start()
        elif number == 2:
            for way, start in ((0, q * s.x), (1, 2 * q + q * s.y)):
                self.to_first()[way].wait_recv()
                at = s.rows(start, q)
                self.own[at, :] = self.own[at, :] + self.first[way]
            for copy in self.to_second():
                copy.start()
        elif number == 3:
            for way, start in ((0, q * s.x + e * s.y), (1, 2 * q + q * s.y + e * s.x)):
                self.to_second()[way].wait_recv()
                self.line[s.z, way * e : (way + 1) * e, :] = self.own[s.rows(start, e), :] + self.second[way]
            for ahead in (2, 1, 3):
                self.along_line(lax.rem(s.z + ahead, 4)).start()
        elif number == 4:
            for ahead in (1, 2, 3):
                self.from_line(lax.rem(s.z + ahead, 4)).wait_recv()
            for copy in self.back() + self.keep():
                copy.start()
        elif number == 5:
            for copy in self.keep():
                copy.wait()
            for copy in self.back():
                copy.wait_recv()
            for copy in self.wide():
                copy.start()
        elif number == 6:
            for copy in self.wide():
                copy.wait_recv()
            self.to_twin().start()
        else:
            self.to_twin().wait_recv()

    def finish(self):
        s = self.sums
        for copy in (self.to_core(), self.to_twin()) + self.to_first() + self.to_second() + self.back() + self.wide():
            copy.wait_send()
        for ahead in (1, 2, 3):
            self.along_line(lax.rem(s.z + ahead, 4)).wait_send()

    @staticmethod
    def scratch(chips, half, lanes):
        dma = pltpu.SemaphoreType.DMA
        quarter, eighth = half // 4, half // 8
        array = [pltpu.VMEM((half, lanes), bf16)]
        return (
            array * 3
            + [
                pltpu.VMEM((2, quarter, lanes), bf16),
                pltpu.VMEM((2, eighth, lanes), bf16),
                pltpu.VMEM((chips, quarter, lanes), bf16),
                dma((2, 1)),
                dma((2, 2)),
                dma((2, 2)),
                dma((chips,)),
                dma((chips,)),
                dma((2, 2)),
                dma((2, 2)),
                dma((2, 1)),
                dma((2,)),
            ]
        )


def backward_kernel(
    first_gain, second_gain, received_in, x_in, up_in, normed_in, qa_in, ka_in, va_in, o_in,
    wq_in, wkv_in, wo_in, we_in, wc_in,
    result_ref, input_grad, final, pair_final, query_final,
    acts, pool, result_acc, second_acc, out, grad_out, received, key_turned, dqt, dvk, send_query, send_pair,
    got_query, give,
    load_tiles, load_first, load_heads, load_late, out_send, out_recv, query_send, query_recv, pair_send, pair_recv,
    save, *sum_refs,
):
    blocks, packed = grad_out.shape[0], grad_out.shape[1]
    rows = 2 * packed // 3
    micro, _, width = input_grad.shape
    heads, _, total = key_turned.shape
    chips = blocks // 2
    tall = acts.shape[1]
    tiles = width // LANES
    dp = lax.axis_index("dp")
    me = lax.axis_index("blk")
    z = me // 2
    core = lax.rem(me, 2)
    lane = lax.broadcasted_iota(jnp.int32, (rows, LANES), 1)
    sums = Sums.gather(final, sum_refs[:26])
    pair_sum = UnitSum(sums, pair_final, sum_refs[26:41])
    query_sum = UnitSum(sums, query_final, sum_refs[41:])
    count = sums.count
    parts = (count // 2 - 1) // 2
    low, up, attended, branch = 2 * parts, 2 * parts + 1, 2 * parts + 2, 2 * parts + 3
    arrived = greet(dp, me, blocks, (sums.along_x, sums.along_y))

    at_query, at_key, at_value, at_grad, at_right, at_pair = (number * heads * total for number in range(6))

    def in_pool(base, head, start, size):
        return pl.ds(pl.multiple_of(base + head * total + start, LANES), size)

    def pair_rows(block):
        size = heads * rows
        return pl.ds(pl.multiple_of(at_pair + block * size, size), size)

    def fetch(number):
        part = number % parts
        copies = []
        for tile in range(tiles):
            if number < parts:
                src = we_in.at[:, pl.ds(part * width + tile * LANES, LANES)]
            else:
                src = wc_in.at[pl.ds(part * width, width), pl.ds(tile * LANES, LANES)]
            place = number * tiles + tile
            copies.append(
                pltpu.make_async_copy(src, pool.at[pl.ds(place * width, width)], load_tiles.at[place])
            )
        return copies

    def weight(number):
        return jnp.concatenate(
            [pool[(number * tiles + tile) * width : (number * tiles + tile + 1) * width, :] for tile in range(tiles)], 1
        )

    def fetch_output():
        return [
            pltpu.make_async_copy(
                wo_in.at[:, pl.ds(tile * LANES, LANES)], pool.at[pl.ds(tile * width, width)], load_tiles.at[tile]
            )
            for tile in range(tiles)
        ]

    def openers():
        copies = [
            pltpu.make_async_copy(received_in, send_query, load_first.at[0]),
            pltpu.make_async_copy(wo_in.at[pl.ds(0, tall)], acts.at[parts], load_first.at[1]),
            pltpu.make_async_copy(
                wo_in.at[pl.ds(tall, width - tall)], acts.at[parts + 1, pl.ds(0, width - tall)], load_first.at[2]
            ),
        ]
        for row in range(micro):
            here = pl.ds(row * rows, rows)
            copies.append(pltpu.make_async_copy(x_in.at[row], acts.at[branch, here], load_first.at[3 + 2 * row]))
            copies.append(pltpu.make_async_copy(up_in.at[row], acts.at[up, here], load_first.at[4 + 2 * row]))
        return copies

    def load_head(number):
        src = (qa_in, ka_in, va_in, o_in)[number]
        base = (at_query, at_key, at_value)
        dst = out if number == 3 else pool.at[pl.ds(base[number], heads * total)]
        return pltpu.make_async_copy(src, dst, load_heads.at[number])

    for copy in openers():
        copy.start()
    for part in range(parts):
        for copy in fetch(part) + fetch(parts + part):
            copy.start()

    kinds = {
        "grad": (grad_out, received, out_send, out_recv),
        "query": (send_query, got_query, query_send, query_recv),
        "pair": (send_pair, pool, pair_send, pair_recv),
    }

    def send(kind, block):
        src, dst, send_sem, recv_sem = kinds[kind]
        return pltpu.make_async_remote_copy(
            src_ref=src.at[block],
            dst_ref=dst.at[pair_rows(me) if kind == "pair" else me],
            send_sem=send_sem.at[block],
            recv_sem=recv_sem.at[me],
            device_id=(dp, block),
            device_id_type=MESH,
        )

    def arrive(kind, block):
        src, dst, send_sem, recv_sem = kinds[kind]
        return pltpu.make_async_remote_copy(
            src_ref=src.at[block],
            dst_ref=dst.at[pair_rows(block) if kind == "pair" else block],
            send_sem=send_sem.at[block],
            recv_sem=recv_sem.at[block],
            device_id=(dp, block),
            device_id_type=MESH,
        )

    def message(number):
        return 2 * far_order(z, number // 2) + lax.rem(core + number, 2)

    def slot(time):
        for kind, starts in (("pair", PAIR_SLOTS), ("query", QUERY_SLOTS)):
            for number, start in enumerate(starts):
                block = message(jnp.int32(2 * chips - 1 if number == 2 * chips - 2 else number))

                @pl.when(time == start)
                def _():
                    send(kind, block).start()

        sums.tick(OUT, OUT_AT, time, count)
        sums.tick(BACK, BACK_AT, time - LATE, count)

    side = sums.half

    def weigh(piece):
        whole = piece // 2
        left = jnp.where(whole < parts, whole, jnp.where(whole < 2 * parts, low, attended))
        right = jnp.where(whole < parts, up, jnp.where(whole < 2 * parts, whole, branch))
        cols = pl.ds(pl.multiple_of(lax.rem(piece, 2) * side, LANES), side)
        turn = lax.rem(piece, GIVE)

        theirs = pl.ds(pl.multiple_of((1 - core) * side, 16), side)
        ours = pl.ds(pl.multiple_of(core * side, 16), side)

        @pl.when(piece >= GIVE)
        def _():
            sums.to_core(piece - GIVE, give.at[turn, theirs]).wait_send()

        give[turn] = dot_tn(acts[left], acts[right, :, cols]).astype(bf16)
        sums.to_core(piece, give.at[turn, theirs]).start()
        sums.own[piece] = give[turn, ours, :]

    opening = openers()
    gain = second_gain[...].reshape(1, width)
    opening[0].wait()
    for row in range(micro):
        acts[attended, row * rows : (row + 1) * rows, :] = columns_of(send_query, row, rows, blocks)
    for copy in opening[1:]:
        copy.wait()
    for row in range(micro):
        at = slice(row * rows, (row + 1) * rows)
        value = acts[branch, at, :].astype(f32) + dot_nn(acts[attended, at, :tall], acts[parts])
        value += dot_nn(acts[attended, at, tall:], acts[parts + 1, : width - tall])
        result_acc[at, :] = value
        acts[low, at, :] = (normal(value)[0] * gain).astype(bf16)
    second_acc[...] = jnp.zeros_like(second_acc)

    for part in range(parts):
        for copy in fetch(part) + fetch(parts + part):
            copy.wait()

        @pl.loop(0, micro)
        def _(row):
            at = pl.ds(pl.multiple_of(row * rows, rows), rows)
            widen, narrow = weight(part), weight(parts + part)
            hidden = dot_nn(acts[low, at, :], widen)
            active_grad = dot_nt(acts[up, at, :], narrow)
            square = hidden * hidden
            c = 0.7978845608028654
            bend = jnp.tanh(hidden * (c + 0.044715 * c * square))
            gate = 0.5 + 0.5 * bend
            slope = gate + 0.5 * hidden * (1.0 - bend * bend) * (c + 3.0 * 0.044715 * c * square)
            active = (hidden * gate).astype(bf16)
            grad = (active_grad * slope).astype(bf16)
            acts[part, at, :] = active
            acts[parts + part, at, :] = grad
            result_acc[at, :] += dot_nn(active, narrow)
            second_acc[at, :] += dot_nt(grad, widen)

        if part == 0:
            arrived()
            for copy in fetch_output():
                copy.start()

        @pl.loop(0, 2)
        def _(turn):
            weigh(2 * part + turn)
            if part > 0:
                slot(2 * part - 2 + turn)

    for copy in fetch_output():
        copy.wait()
    project = weight(0)
    for row in range(micro):
        at = slice(row * rows, (row + 1) * rows)
        result_ref[row] = result_acc[at, :].astype(bf16)
        value = acts[branch, at, :].astype(f32) + dot_nn(acts[attended, at, :], project)
        unit_, scale = normal(value)
        grad = acts[up, at, :].astype(f32) + normal_pull(second_acc[at, :] * gain, unit_, scale)
        second_acc[at, :] = grad
        acts[branch, at, :] = grad.astype(bf16)
        back = dot_nt(acts[branch, at, :], project).astype(bf16)
        for chip in range(chips):
            start = chip * heads * HEAD
            wide, narrow = pack_heads(
                [back[:, start + h * HEAD : start + (h + 1) * HEAD] for h in range(heads)]
            )
            grad_out[2 * chip + row, :rows, :] = wide
            grad_out[2 * chip + row, rows:, :] = narrow

    for step in range(4):
        for row in range(2):
            block = 2 * far_order(z, jnp.int32(step)) + row

            @pl.when(block != me)
            def _():
                send("grad", block).start()

    received[me] = grad_out[me]
    for number in range(4):
        load_head(number).start()

    for number in range(2 * parts - 2, 2 * parts):
        slot(jnp.int32(number))

    @pl.loop(2 * parts, count)
    def _(piece):
        weigh(piece)

        @pl.when((lax.rem(piece, 2) == 1) & (piece > 2 * parts + 1))
        def _():
            slot(2 * parts + (piece - 2 * parts - 3) // 2)

    squares = [(wq_in, 0), (wkv_in, 0), (wkv_in, width)]

    def late():
        copies = [
            pltpu.make_async_copy(normed_in.at[chip], acts.at[chip], load_late.at[chip]) for chip in range(chips)
        ]
        for number, (src, start) in enumerate(squares):
            cols = pl.ds(start, width)
            copies.append(
                pltpu.make_async_copy(
                    src.at[pl.ds(0, tall), cols], acts.at[chips + 2 * number], load_late.at[chips + 2 * number]
                )
            )
            copies.append(
                pltpu.make_async_copy(
                    src.at[pl.ds(tall, width - tall), cols],
                    acts.at[chips + 2 * number + 1, pl.ds(0, width - tall)],
                    load_late.at[chips + 2 * number + 1],
                )
            )
        for row in range(micro):
            copies.append(
                pltpu.make_async_copy(
                    x_in.at[row],
                    acts.at[chips + 6, pl.ds(row * rows, rows)],
                    load_late.at[chips + 6 + row],
                )
            )
        return copies

    for copy in late():
        copy.start()

    dqt[...] = jnp.zeros_like(dqt)
    for number in range(4):
        load_head(number).wait()

    @pl.loop(0, blocks)
    def _(block):
        here = pl.ds(pl.multiple_of(block * rows, rows), rows)
        for head in range(heads):
            key = pool[in_pool(at_key, head, block * rows, rows), :][:, :HEAD].astype(f32)
            key_turned[head, :, here] = jnp.transpose(key).astype(bf16)
            query = pool[in_pool(at_query, head, block * rows, rows), :][:, :HEAD]
            pool[in_pool(at_right, head, block * rows, rows), :] = jnp.concatenate([jnp.zeros_like(query), query], 1)

    @pl.loop(0, blocks)
    def _(step):
        block = 2 * chip_order(z, step // 2) + lax.rem(core + step, 2)

        @pl.when(block != me)
        def _():
            arrive("grad", block).wait_recv()

        wide = received[block, :rows, :].astype(f32)
        narrow = received[block, rows:, :].astype(f32)
        shares = heads_of(wide * out[block, :rows, :].astype(f32), narrow * out[block, rows:, :].astype(f32))
        gap = jnp.zeros((rows, LANES - HEAD), f32)
        for head, piece in enumerate(heads_of(wide, narrow)):
            delta = jnp.sum(shares[head], -1, keepdims=True)
            value = jnp.concatenate([piece, gap], 1)
            pool[in_pool(at_grad, head, block * rows, rows), :] = (value + spread(delta, HEAD, lane)).astype(bf16)

    wide_rows = 2 * rows
    eye = lax.broadcasted_iota(jnp.int32, (wide_rows, wide_rows), 0) == lax.broadcasted_iota(
        jnp.int32, (wide_rows, wide_rows), 1
    )
    half = LANES

    def pull(keys, queries, diagonal=False):
        found = []
        for head in range(heads):
            k = pool[in_pool(at_key, head, *keys), :]
            q = pool[in_pool(at_query, head, *queries), :]
            g = pool[in_pool(at_grad, head, *queries), :]
            at = lax.broadcasted_iota(jnp.int32, k.shape, 1)
            s = dot_nt(k, q)
            if diagonal:
                bare = (at < HEAD) | (at > HEAD + CODES)
                s = jnp.where(eye, dot_nt(jnp.where(bare, k, 0.0).astype(bf16), q), s)
            p = jnp.exp(s)
            ds = (p * dot_nt(pool[in_pool(at_value, head, *keys), :], g)).astype(bf16)
            left = jnp.concatenate([p.astype(bf16), ds], 1)
            at = lax.broadcasted_iota(jnp.int32, g.shape, 1)
            value = jnp.where(at < HEAD, g, 0.0).astype(bf16)
            right = jnp.concatenate([value, pool[in_pool(at_right, head, *queries), :]], 0)
            turned = key_turned[head, :, pl.ds(pl.multiple_of(keys[0], LANES), keys[1])]
            found.append((dot_nn(left, right), dot_nn(turned, ds)))
        return found

    @pl.loop(0, chips)
    def _(step):
        chip = far_order(z, step)
        span = (chip * wide_rows, wide_rows)
        here = pl.ds(pl.multiple_of(chip * wide_rows, wide_rows), wide_rows)
        for head, (pair, query) in enumerate(pull(span, span, True)):
            dvk[head] = pair
            dqt[head, :, here] += query
        time = EARLY
        for earlier in range(chips - 1):
            done = far_order(z, earlier)
            bodies = chips - done + jnp.where(done > 0, 1, 0)
            time = time + jnp.where(earlier < step, bodies, 0)
        slot(time)

        @pl.loop(chip + 1, chips)
        def _(other):
            there = pl.ds(pl.multiple_of(other * wide_rows, wide_rows), wide_rows)
            for head, (pair, query) in enumerate(pull(span, (other * wide_rows, wide_rows))):
                dvk[head] += pair
                dqt[head, :, there] += query
            slot(time + other - chip)

        @pl.when(chip > 0)
        def _():
            edge = chip * wide_rows
            queries = pl.ds(pl.multiple_of(edge - half, half), half)
            for head, (pair, query) in enumerate(pull((edge, half), (edge - half, half))):
                dvk[head, :half] += pair
                dqt[head, :, queries] += query
            slot(time + chips - chip)

        for turn in range(2):
            block = 2 * chip + turn
            for head in range(heads):
                send_pair[block, head * rows : (head + 1) * rows, :] = dvk[
                    head, turn * rows : (turn + 1) * rows
                ].astype(bf16)

            @pl.when(block == me)
            def _():
                pool[pair_rows(me), :] = send_pair[me]

    for copy in late():
        copy.wait()

    def columns(tile):
        right = jnp.concatenate([jnp.concatenate(tile(block), 1) for block in range(blocks)], 0)
        for unit, which in (("give", 1 - core), ("own", core)):
            cols = pl.ds(pl.multiple_of(which * side, LANES), side)
            left = acts[:chips, :, cols].reshape(total, side)
            yield unit, dot_tn(left, right).astype(bf16)

    for unit, value in columns(
        lambda block: [send_pair[block, head * rows : (head + 1) * rows, :] for head in range(heads)]
    ):
        getattr(pair_sum, unit)[...] = value
        if unit == "give":
            pair_sum.step(0)
    slot(jnp.int32(EARLY + 13))

    @pl.loop(0, blocks)
    def _(block):
        here = pl.ds(pl.multiple_of(block * rows, rows), rows)
        wide, narrow = pack_heads(
            [(jnp.transpose(dqt[h, :, here]) * (HEAD**-0.5)).astype(bf16) for h in range(heads)]
        )
        send_query[block, :rows, :] = wide
        send_query[block, rows:, :] = narrow

        @pl.when(block == me)
        def _():
            got_query[me] = send_query[me]

    gap = jnp.zeros((rows, LANES - HEAD), bf16)
    for unit, value in columns(
        lambda block: heads_of(send_query[block, :rows, :], send_query[block, rows:, :]) + [gap]
    ):
        getattr(query_sum, unit)[...] = value
        if unit == "give":
            query_sum.step(0)
    slot(jnp.int32(EARLY + 14))

    ready = EARLY + 15
    end = LATE + count + BACK_AT[-1]

    def normed_part(row, operands, first):
        grad = []
        for part in range(2):
            height = tall if part == 0 else width - tall
            total_ = jnp.zeros((rows, height), f32)
            for number, operand in enumerate(operands):
                total_ = total_ + dot_nt(operand, acts[chips + 2 * (first + number) + part, :height])
            grad.append(total_)
        return jnp.concatenate(grad, 1)

    def pair_part(row):
        keys, values = [], []
        for chip in range(chips):
            for head in range(heads):
                start = at_pair + ((2 * chip + row) * heads + head) * rows
                both = pool[start : start + rows, :]
                keys.append(both[:, HEAD:])
                values.append(both[:, :HEAD])
        operands = [jnp.concatenate(keys, 1), jnp.concatenate(values, 1)]
        result_acc[row * rows : (row + 1) * rows, :] = normed_part(row, operands, 1)

    def last(row):
        at = slice(row * rows, (row + 1) * rows)
        grad = result_acc[at, :] + normed_part(row, [columns_of(got_query, row, rows, blocks)], 0)
        unit_, scale = normal(acts[chips + 6, at, :].astype(f32))
        pulled = normal_pull(grad * first_gain[...].reshape(1, width), unit_, scale)
        acts[chips + 7, at, :] = (second_acc[at, :] + pulled).astype(bf16)
        return pltpu.make_async_copy(acts.at[chips + 7, pl.ds(row * rows, rows)], input_grad.at[row], save.at[row])

    def wait_for(kind):
        @pl.loop(0, blocks)
        def _(block):
            @pl.when(block != me)
            def _():
                arrive(kind, block).wait_recv()

    @pl.loop(ready, max(end, ready + max(PAIR_SUM_SLOTS + QUERY_SUM_SLOTS) + 1))
    def _(time):
        for unit, places in ((pair_sum, PAIR_SUM_SLOTS), (query_sum, QUERY_SUM_SLOTS)):
            for number, place in enumerate(places):

                @pl.when(time == ready + place)
                def _():
                    unit.step(number + 1)

        slot(time)

        @pl.when(time == PAIR_DONE)
        def _():
            wait_for("pair")
            for row in range(micro):
                pair_part(row)

    wait_for("query")
    saves = [last(row) for row in range(micro)]
    for copy in saves:
        copy.start()

    @pl.loop(0, blocks)
    def _(block):
        @pl.when(block != me)
        def _():
            send("grad", block).wait_send()
            send("query", block).wait_send()
            send("pair", block).wait_send()

    theirs = pl.ds(pl.multiple_of((1 - core) * side, 16), side)
    for piece in range(count - GIVE, count):
        sums.to_core(piece, give.at[piece % GIVE, theirs]).wait_send()

    @pl.loop(0, count)
    def _(piece):
        sums.finish(piece)

    pair_sum.finish()
    query_sum.finish()
    for copy in saves:
        copy.wait()


def final_kernel(
    final, we_ref, first_gain, second_gain, pair_in, query_in, wq_in, wkv_in,
    first_ref, query_ref, pair_ref, output_ref, second_ref, expand_ref, contract_ref,
    first_acc, second_acc, pair_unit, query_unit, wq_ref, wkv_ref, fetch,
):
    step = pl.program_id(0)
    width = wq_ref.shape[0]
    chips = pair_in.shape[0]
    heads = width // HEAD // chips
    parts = (pl.num_programs(0) - 4) // 2

    def fold(array):
        return sum(array[:, i : i + LANES] for i in range(0, width, LANES))

    def loads():
        pairs = ((pair_in, pair_unit), (query_in, query_unit), (wq_in, wq_ref), (wkv_in, wkv_ref))
        return [pltpu.make_async_copy(src, dst, fetch.at[i]) for i, (src, dst) in enumerate(pairs)]

    @pl.when(step == 0)
    def _():
        for copy in loads():
            copy.start()
        first_acc[...] = jnp.zeros_like(first_acc)
        second_acc[...] = jnp.zeros_like(second_acc)

    @pl.when(step < parts)
    def _():
        contract_ref[...] = final[0].astype(f32)

    @pl.when((step >= parts) & (step < 2 * parts))
    def _():
        value = final[0].astype(f32)
        expand_ref[...] = value
        second_acc[...] += fold(value * we_ref[...].astype(f32))

    @pl.when(step == 2 * parts)
    def _():
        output_ref[...] = final[0].astype(f32)

    def columns(unit, place):
        return jnp.concatenate(
            [unit[chip][:, place(head) : place(head) + HEAD] for chip in range(chips) for head in range(heads)], 1
        ).astype(f32)

    @pl.when(step == 2 * parts + 1)
    def _():
        for copy in loads():
            copy.wait()
        value = columns(query_unit, lambda head: head * HEAD)
        query_ref[...] = value
        first_acc[...] += fold(value * wq_ref[...].astype(f32))

    for side in range(2):

        @pl.when(step == 2 * parts + 2 + side)
        def _():
            value = columns(pair_unit, lambda head: head * LANES + (HEAD if side == 0 else 0))
            pair_ref[...] = value
            first_acc[...] += fold(value * wkv_ref[:, side * width : (side + 1) * width].astype(f32))

    @pl.when(step == pl.num_programs(0) - 1)
    def _():
        first_ref[...] = jnp.sum(jnp.transpose(first_acc[...]), 0) / first_gain[...]
        second_ref[...] = jnp.sum(jnp.transpose(second_acc[...]), 0) / second_gain[...]


VMEM = pl.BlockSpec(memory_space=pltpu.VMEM)
SMEM = pl.BlockSpec(memory_space=pltpu.SMEM)
ANY = pl.BlockSpec(memory_space=pl.ANY)


def attention_forward(inputs, gain, lengths, views, padding, query_weight, pair_weight, blocks):
    micro, rows, width = inputs.shape
    total = rows * blocks
    heads = width // HEAD // (blocks // micro)
    packed = rows * heads // 2
    shape = jax.ShapeDtypeStruct
    dma = pltpu.SemaphoreType.DMA
    unit = (heads, total, LANES)
    return pl.pallas_call(
        forward_kernel,
        out_shape=(
            shape((blocks // 2, 2 * rows, width), bf16),
            shape(unit, bf16),
            shape(unit, bf16),
            shape(unit, bf16),
            shape((blocks, packed, LANES), bf16),
            shape((blocks, packed, LANES), bf16),
        ),
        in_specs=[SMEM, SMEM] + [VMEM] * 3 + [ANY] * 2,
        out_specs=(ANY,) * 5 + (VMEM,),
        scratch_shapes=[
            pltpu.VMEM((blocks, rows, width), bf16),
            pltpu.VMEM(unit, bf16),
            pltpu.VMEM(unit, bf16),
            pltpu.VMEM(unit, bf16),
            pltpu.VMEM(unit, f32),
            pltpu.VMEM((width, heads * 3 * LANES), bf16),
            pltpu.VMEM(query_weight.shape, bf16),
            pltpu.VMEM(pair_weight.shape, bf16),
            pltpu.VMEM((rows, width), bf16),
            pltpu.VMEM(unit, f32),
            pltpu.VMEM((blocks, packed, LANES), bf16),
            dma((2,)),
            dma,
            dma,
            dma((blocks, 2)),
            dma((blocks,)),
            dma((blocks,)),
            dma((blocks,)),
            dma((blocks, 5)),
        ],
        compiler_params=pltpu.CompilerParams(
            collective_id=0, has_side_effects=True, vmem_limit_bytes=63 << 20
        ),
        name="attention_forward",
    )(lengths, views, inputs, gain, padding, query_weight, pair_weight)


def attention_backward(
    first_gain, second_gain, received, inputs, cotangent, normed, qa, ka, va, out,
    query_weight, pair_weight, output_weight, expand_weight, contract_weight,
):
    micro, rows, width = inputs.shape
    blocks, packed, _ = received.shape
    heads, total, _ = qa.shape
    chips = blocks // 2
    tokens = micro * rows
    parts = expand_weight.shape[1] // width
    pieces = 2 * parts + 1
    count = 2 * pieces
    side = width // 2
    flat = (heads * total, LANES)
    shape = jax.ShapeDtypeStruct
    dma = pltpu.SemaphoreType.DMA
    message = pltpu.VMEM((blocks, packed, LANES), bf16)
    return pl.pallas_call(
        backward_kernel,
        out_shape=(
            shape(inputs.shape, bf16),
            shape(inputs.shape, bf16),
            shape((pieces, width, width), bf16),
            shape((chips, width, heads * LANES), bf16),
            shape((chips, width, 2 * LANES), bf16),
        ),
        in_specs=[VMEM] * 2 + [ANY] * 13,
        out_specs=(VMEM, ANY, ANY, ANY, ANY),
        scratch_shapes=[
            pltpu.VMEM((2 * parts + 4, tokens, width), bf16),
            pltpu.VMEM((2 * parts * width // LANES * width, LANES), bf16),
            pltpu.VMEM((tokens, width), f32),
            pltpu.VMEM((tokens, width), f32),
            message,
            message,
            message,
            pltpu.VMEM((heads, HEAD, total), bf16),
            pltpu.VMEM((heads, HEAD, total), f32),
            pltpu.VMEM((heads, 2 * rows, LANES), f32),
            message,
            pltpu.VMEM((blocks, heads * rows, LANES), bf16),
            message,
            pltpu.VMEM((GIVE, width, side), bf16),
            dma((2 * parts * width // LANES,)),
            dma((3 + 2 * micro,)),
            dma((4,)),
            dma((chips + 6 + micro,)),
        ]
        + [dma((blocks,))] * 6
        + [dma((micro,))]
        + Sums.scratch(count, side, side)
        + UnitSum.scratch(chips, side, heads * LANES)
        + UnitSum.scratch(chips, side, 2 * LANES),
        compiler_params=pltpu.CompilerParams(
            collective_id=1, has_side_effects=True, vmem_limit_bytes=63 << 20
        ),
        name="backward",
    )(
        first_gain, second_gain, received, inputs, cotangent, normed,
        qa.reshape(flat), ka.reshape(flat), va.reshape(flat), out,
        query_weight, pair_weight, output_weight, expand_weight, contract_weight,
    )


def finish(final, pair_final, query_final, first_gain, second_gain, query_weight, pair_weight, expand_weight):
    pieces, width, _ = final.shape
    steps = pieces + 3
    parts = (pieces - 1) // 2
    shape = jax.ShapeDtypeStruct
    square = (width, width)

    def whole(array):
        return pl.BlockSpec(array.shape, lambda p: (0,) * array.ndim)

    def clip(p, start, count):
        return jnp.clip(p - start, 0, count - 1)

    fixed = (first_gain, second_gain)
    later = (pair_final, query_final, query_weight, pair_weight)
    row = pl.BlockSpec((width,), lambda p: (0,))
    return pl.pallas_call(
        final_kernel,
        grid=(steps,),
        out_shape=(
            shape((width,), f32),
            shape(square, f32),
            shape((width, 2 * width), f32),
            shape(square, f32),
            shape((width,), f32),
            shape((width, parts * width), f32),
            shape((parts * width, width), f32),
        ),
        in_specs=[
            pl.BlockSpec((1,) + square, lambda p: (clip(p, 0, pieces), 0, 0)),
            pl.BlockSpec(square, lambda p: (0, clip(p, parts, parts))),
        ]
        + [whole(array) for array in fixed]
        + [ANY] * 4,
        out_specs=(
            row,
            pl.BlockSpec(square, lambda p: (0, 0)),
            pl.BlockSpec(square, lambda p: (0, clip(p, 2 * parts + 2, 2))),
            pl.BlockSpec(square, lambda p: (0, 0)),
            row,
            pl.BlockSpec(square, lambda p: (0, clip(p, parts, parts))),
            pl.BlockSpec(square, lambda p: (clip(p, 0, parts), 0)),
        ),
        scratch_shapes=[pltpu.VMEM((width, LANES), f32), pltpu.VMEM((width, LANES), f32)]
        + [pltpu.VMEM(array.shape, bf16) for array in later]
        + [pltpu.SemaphoreType.DMA((4,))],
        compiler_params=pltpu.CompilerParams(vmem_limit_bytes=63 << 20),
        name="finish",
    )(final, expand_weight, *fixed, *later)


def layer_norm(value, gain):
    mean = jnp.mean(value, -1, keepdims=True)
    centred = value - mean
    spread = jnp.mean(centred * centred, -1, keepdims=True)
    return centred * lax.rsqrt(spread + epsilon) * gain


def token_info(lengths, views, positions):
    ends = jnp.cumsum(lengths)
    starts = ends - lengths
    inside = (positions[:, None] >= starts[None, :]) & (positions[:, None] < ends[None, :])
    number = jnp.arange(lengths.shape[0], dtype=jnp.int32)
    item = jnp.sum(jnp.where(inside, number[None, :], 0), 1)
    first = jnp.sum(jnp.where(inside, starts[None, :], 0), 1)
    span = jnp.sum(jnp.where(inside, views[None, :], 0), 1) * PATCHES
    frame = (positions - first) // span
    return (item, frame)


def visible(query_pos, query_item, query_frame, key_pos, key_item, key_frame, key_pad):
    same = query_item[:, None] == key_item[None, :]
    order = key_frame[None, :] <= query_frame[:, None]
    usable = (key_pad[None, :] == 1) | (query_pos[:, None] == key_pos[None, :])
    return same & order & usable


def in_blocks(update, carry, piece, block_rows):
    count = piece[0].shape[0]

    def advance(number, inner):
        begin = number * block_rows
        part = (
            lax.dynamic_slice_in_dim(piece[0], begin, block_rows),
            lax.dynamic_slice_in_dim(piece[1], begin, block_rows),
        )
        return update(inner, part, begin)

    return lax.fori_loop(0, count // block_rows, advance, carry)


def score_parts(query_heads, grad_heads, total, shift, key_heads, value_heads, mask, scale):
    scores = (
        jnp.einsum("qhd,khd->hqk", query_heads, key_heads, preferred_element_type=jnp.float32)
        * scale
    )
    chance = jnp.where(mask[None], jnp.exp(scores - total[..., None]), 0.0)
    chance_grad = jnp.einsum(
        "qhd,khd->hqk", grad_heads, value_heads, preferred_element_type=jnp.float32
    )
    score_grad = (chance * (chance_grad - shift[..., None])).astype(jnp.bfloat16)
    return (chance, score_grad)


def on_device(
    inputs,
    cotangent,
    lengths,
    view_counts,
    padding,
    first_gain,
    query_weight,
    key_value_weight,
    output_weight,
    second_gain,
    expand_weight,
    contract_weight,
):
    micro_count, row_count, width = inputs.shape
    head_count = width // HEAD
    scale = HEAD ** (-0.5)
    cycle_size = lax.axis_size("blk")
    own_start = lax.axis_index("blk") * row_count
    query_positions = own_start + jnp.arange(row_count, dtype=jnp.int32)
    gelu = partial(jax.nn.gelu, approximate=True)
    grads = tuple(
        (
            jnp.zeros(array.shape, jnp.float32)
            for array in (
                first_gain,
                query_weight,
                key_value_weight,
                output_weight,
                second_gain,
                expand_weight,
                contract_weight,
            )
        )
    )
    outputs = []
    input_grads = []
    for micro in range(micro_count):
        row_lengths = lengths[micro]
        row_views = view_counts[micro]
        row_pad = padding[micro]
        query_item, query_frame = token_info(row_lengths, row_views, query_positions)
        flat = inputs[micro].astype(jnp.float32)
        normed, first_pull = jax.vjp(layer_norm, flat, first_gain)
        normed_low = normed.astype(jnp.bfloat16)
        query = jnp.dot(normed_low, query_weight, preferred_element_type=jnp.float32).astype(
            jnp.bfloat16
        )
        pair = jnp.dot(normed_low, key_value_weight, preferred_element_type=jnp.float32).astype(
            jnp.bfloat16
        )
        keys = pair[:, :width]
        values = pair[:, width:]
        query_heads = query.reshape(row_count, head_count, HEAD)

        def mask_for(start, count):
            key_positions = start + jnp.arange(count, dtype=jnp.int32)
            key_item, key_frame = token_info(row_lengths, row_views, key_positions)
            key_pad = lax.dynamic_slice_in_dim(row_pad, start, count)
            return visible(
                query_positions,
                query_item,
                query_frame,
                key_positions,
                key_item,
                key_frame,
                key_pad,
            )

        def forward_block(carry, piece, start):
            count = piece[0].shape[0]
            mask = mask_for(start, count)

            def forward_work(state):
                peak, denominator, weighted = state
                key_heads = piece[0].reshape(count, head_count, HEAD)
                value_heads = piece[1].reshape(count, head_count, HEAD)
                scores = (
                    jnp.einsum(
                        "qhd,khd->hqk", query_heads, key_heads, preferred_element_type=jnp.float32
                    )
                    * scale
                )
                scores = jnp.where(mask[None], scores, lowest)
                new_peak = jnp.maximum(peak, jnp.max(scores, -1))
                raised = jnp.where(mask[None], jnp.exp(scores - new_peak[..., None]), 0.0)
                shrink = jnp.exp(peak - new_peak)
                denominator = denominator * shrink + jnp.sum(raised, -1)
                weighted = weighted * shrink[..., None] + jnp.einsum(
                    "hqk,khd->hqd",
                    raised.astype(jnp.bfloat16),
                    value_heads,
                    preferred_element_type=jnp.float32,
                )
                return (new_peak, denominator, weighted)

            return lax.cond(jnp.any(mask), forward_work, lambda state: state, carry)

        initial = (
            jnp.full((head_count, row_count), lowest, jnp.float32),
            jnp.zeros((head_count, row_count), jnp.float32),
            jnp.zeros((head_count, row_count, HEAD), jnp.float32),
        )
        peak, denominator, weighted = in_blocks(
            forward_block,
            initial,
            (
                lax.all_gather(keys, "blk", axis=0, tiled=True),
                lax.all_gather(values, "blk", axis=0, tiled=True),
            ),
            row_count,
        )
        attended_heads = weighted / denominator[..., None]
        log_total = peak + jnp.log(denominator)
        attended_low = (
            jnp.transpose(attended_heads, (1, 0, 2)).reshape(row_count, width).astype(jnp.bfloat16)
        )
        mixed = flat + jnp.dot(attended_low, output_weight, preferred_element_type=jnp.float32)
        second, second_pull = jax.vjp(layer_norm, mixed, second_gain)
        second_low = second.astype(jnp.bfloat16)
        hidden = jnp.dot(second_low, expand_weight, preferred_element_type=jnp.float32)
        activated, gelu_pull = jax.vjp(gelu, hidden)
        activated_low = activated.astype(jnp.bfloat16)
        output = mixed + jnp.dot(activated_low, contract_weight, preferred_element_type=jnp.float32)
        outputs.append(output.astype(jnp.bfloat16))
        upstream = cotangent[micro]
        grad_contract = jnp.einsum(
            "rf,rd->fd", activated_low, upstream, preferred_element_type=jnp.float32
        )
        activated_grad = jnp.einsum(
            "rd,fd->rf", upstream, contract_weight, preferred_element_type=jnp.float32
        )
        hidden_grad = gelu_pull(activated_grad)[0].astype(jnp.bfloat16)
        grad_expand = jnp.einsum(
            "rd,rf->df", second_low, hidden_grad, preferred_element_type=jnp.float32
        )
        second_grad = jnp.einsum(
            "rf,df->rd", hidden_grad, expand_weight, preferred_element_type=jnp.float32
        )
        mixed_part, grad_second = second_pull(second_grad)
        mixed_grad = upstream.astype(jnp.float32) + mixed_part
        branch_grad = mixed_grad.astype(jnp.bfloat16)
        grad_output = jnp.einsum(
            "rd,re->de", attended_low, branch_grad, preferred_element_type=jnp.float32
        )
        attended_grad = jnp.einsum(
            "re,de->rd", branch_grad, output_weight, preferred_element_type=jnp.float32
        ).astype(jnp.bfloat16)
        grad_heads = attended_grad.reshape(row_count, head_count, HEAD)
        delta = jnp.sum(
            jnp.transpose(grad_heads, (1, 0, 2)).astype(jnp.float32) * attended_heads, -1
        )

        def backward_block(carry, piece, start):
            count = piece[0].shape[0]
            mask = mask_for(start, count)

            def backward_work(state):
                query_sum, pair_terms = state
                key_heads = piece[0].reshape(count, head_count, HEAD)
                value_heads = piece[1].reshape(count, head_count, HEAD)
                chance, score_grad = score_parts(
                    query_heads, grad_heads, log_total, delta, key_heads, value_heads, mask, scale
                )
                value_term = jnp.einsum(
                    "hqk,qhd->khd",
                    chance.astype(jnp.bfloat16),
                    grad_heads,
                    preferred_element_type=jnp.float32,
                )
                query_sum = (
                    query_sum
                    + jnp.einsum(
                        "hqk,khd->qhd", score_grad, key_heads, preferred_element_type=jnp.float32
                    )
                    * scale
                )
                key_term = (
                    jnp.einsum(
                        "hqk,qhd->khd", score_grad, query_heads, preferred_element_type=jnp.float32
                    )
                    * scale
                )
                term = jnp.concatenate(
                    [key_term.reshape(count, width), value_term.reshape(count, width)], 1
                )
                previous = lax.dynamic_slice_in_dim(pair_terms, start, count)
                pair_terms = lax.dynamic_update_slice_in_dim(pair_terms, previous + term, start, 0)
                return (query_sum, pair_terms)

            return lax.cond(jnp.any(mask), backward_work, lambda state: state, carry)

        start_back = (
            jnp.zeros((row_count, head_count, HEAD), jnp.float32),
            jnp.zeros((row_count * cycle_size, 2 * width), jnp.float32),
        )
        back_state = in_blocks(
            backward_block,
            start_back,
            (
                lax.all_gather(keys, "blk", axis=0, tiled=True),
                lax.all_gather(values, "blk", axis=0, tiled=True),
            ),
            row_count,
        )
        query_sum, pair_terms = back_state
        pair_grad = lax.psum_scatter(
            pair_terms.astype(jnp.bfloat16), "blk", scatter_dimension=0, tiled=True
        )
        query_grad = query_sum.reshape(row_count, width).astype(jnp.bfloat16)
        grad_query = jnp.einsum(
            "rd,re->de", normed_low, query_grad, preferred_element_type=jnp.float32
        )
        grad_pair = jnp.einsum(
            "rd,re->de", normed_low, pair_grad, preferred_element_type=jnp.float32
        )
        normed_grad = jnp.einsum(
            "re,de->rd", query_grad, query_weight, preferred_element_type=jnp.float32
        )
        normed_grad = normed_grad + jnp.einsum(
            "re,de->rd", pair_grad, key_value_weight, preferred_element_type=jnp.float32
        )
        input_part, grad_first = first_pull(normed_grad)
        input_grads.append((mixed_grad + input_part).astype(jnp.bfloat16))
        terms = (
            grad_first,
            grad_query,
            grad_pair,
            grad_output,
            grad_second,
            grad_expand,
            grad_contract,
        )
        grads = tuple((total + term for total, term in zip(grads, terms)))
    summed = lax.psum(
        (grads[0], grads[1], grads[2], grads[3], grads[4], grads[5], grads[6]), ("dp", "blk")
    )
    return (
        jnp.stack(outputs),
        jnp.stack(input_grads),
        summed[0],
        summed[1],
        summed[2],
        summed[3],
        summed[4],
        summed[5],
        summed[6],
    )


def fast_on_device(
    inputs, cotangent, lengths, view_counts, padding, first_gain, query_weight, key_value_weight,
    output_weight, second_gain, expand_weight, contract_weight,
):
    normed, qa, ka, va, out, received = attention_forward(
        inputs, first_gain, lengths, view_counts, padding, query_weight, key_value_weight, lax.axis_size("blk")
    )
    result, input_grad, final, pair_final, query_final = attention_backward(
        first_gain, second_gain, received, inputs, cotangent, normed, qa, ka, va, out,
        query_weight, key_value_weight, output_weight, expand_weight, contract_weight,
    )
    first, query, pair, output, second, expand, contract = finish(
        final, pair_final, query_final, first_gain, second_gain, query_weight, key_value_weight, expand_weight
    )
    return result, input_grad, first, query, pair, output, second, expand, contract


def solution(mesh):
    placed = (
        P("dp", "blk", None),
        P("dp", "blk", None),
        P("dp", None),
        P("dp", None),
        P("dp", None),
    ) + (P(),) * 7

    def program(*arrays):
        inputs, lengths = arrays[0], arrays[2]
        dp, blk = mesh.shape["dp"], mesh.shape["blk"]
        rows, total, width = inputs.shape
        items = lengths.shape[1]
        chips = blk // 2
        fits = (
            (dp, blk) == (4, 8)
            and rows == 2 * dp
            and total % (blk * 2 * LANES) == 0
            and width % (LANES * HEAD // 64) == 0
            and width // HEAD == 3 * chips
            and total // PATCHES + items <= CODES
        )
        return jax.shard_map(
            fast_on_device if fits else on_device,
            mesh=mesh,
            in_specs=placed,
            out_specs=(P("dp", "blk", None), P("dp", "blk", None)) + (P(),) * 7,
            check_vma=False,
        )(*arrays)

    return program
```

```python
from functools import partial

import jax
import jax.numpy as jnp
from jax import lax
from jax.experimental import pallas as pl
from jax.experimental.pallas import tpu as pltpu
from jax.sharding import PartitionSpec as P

HEAD = 64
PATCHES = 64
CODES = 40
BIG = 1e30
EARLY = 12
OUT_AT = (0, 3, 6, 9, 12)
BACK_AT = (0, 3, 6, 9)
LATE = 13
GIVE = 2
PAIR_SLOTS = (18, 23, 28, 31, 34, 35, 28)
QUERY_SLOTS = (36, 37, 38, 39, 40, 40, 31)
PAIR_SUM_SLOTS = (1, 3, 6, 9, 11, 13, 15)
QUERY_SUM_SLOTS = (2, 4, 7, 10, 12, 14, 16)
PAIR_DONE = 40
OUT = (1, 2, 3, 4, 5)
BACK = (6, 7, 8, 9)
LANES = 128
MESH = pl.DeviceIdType.MESH
bf16 = jnp.bfloat16
f32 = jnp.float32

epsilon = 1e-05
lowest = -1e30


def dot_nn(a, b):
    return lax.dot_general(a, b, (((1,), (0,)), ((), ())), preferred_element_type=f32)


def dot_nt(a, b):
    return lax.dot_general(a, b, (((1,), (1,)), ((), ())), preferred_element_type=f32)


def dot_tn(a, b):
    return lax.dot_general(a, b, (((0,), (0,)), ((), ())), preferred_element_type=f32)


def chip_order(z, step):
    code = jnp.where(z == 0, 3210, jnp.where(z == 1, 3201, jnp.where(z == 2, 312, 123)))
    return digit(code, step)


def digit(code, step):
    power = jnp.where(step == 0, 1, jnp.where(step == 1, 10, jnp.where(step == 2, 100, 1000)))
    return lax.rem(code // power, 10)


def chip_span(z, step):
    low = jnp.where(z == 0, 0, jnp.where(z == 1, 1, jnp.where(z == 2, 112, 123)))
    high = jnp.where(z == 0, 3210, jnp.where(z == 1, 3211, jnp.where(z == 2, 3322, 3333)))
    return digit(low, step), digit(high, step)


def far_order(z, step):
    return jnp.where(
        step == 0,
        lax.rem(z + 2, 4),
        jnp.where(step == 1, 3 - z, jnp.where(step == 2, z + 1 - 2 * lax.rem(z, 2), z)),
    )


def features(block, rows, lengths, views, row, padded):
    lane = lax.broadcasted_iota(jnp.int32, (rows, LANES), 1) - HEAD
    position = block * rows + lax.broadcasted_iota(jnp.int32, (rows, LANES), 0)
    code = jnp.zeros((rows, LANES), jnp.int32)
    base = jnp.zeros((rows, LANES), jnp.int32)
    start = jnp.int32(0)
    first = jnp.int32(0)
    for item in range(lengths.shape[1]):
        length = lengths[row, item]
        view = views[row, item]
        offset = position - start
        inside = (offset >= 0) & (offset < length)
        frame = (offset >> 6) * (2 - view) + (offset >> 7) * (view - 1)
        code = jnp.where(inside, first + frame, code)
        base = jnp.where(inside, first, base)
        first = first + ((length + 63) >> 6) * (2 - view) + ((length + 127) >> 7) * (view - 1)
        start = start + length
    coded = (lane >= 0) & (lane < CODES)
    key = jnp.where(coded & (lane == code), 1.0, 0.0)
    key = jnp.where((lane > CODES) & (lane < CODES + 4), 1.0, key)
    key = jnp.where(lane == CODES, padded, key)
    hidden = (coded & ((lane < base) | (lane > code))) | (lane == CODES)
    query = jnp.where(hidden, -BIG, 0.0)
    return key, query


def three_parts(value):
    high = value.astype(bf16).astype(f32)
    rest = value - high
    middle = rest.astype(bf16).astype(f32)
    low = (rest - middle).astype(bf16).astype(f32)
    return high, middle, low


def spread(value, first, lane):
    high, middle, low = three_parts(value)
    return jnp.where(
        lane == first, high, jnp.where(lane == first + 1, middle, jnp.where(lane == first + 2, low, 0.0))
    )


def pack_heads(heads):
    half = heads[2].shape[0] // 2
    wide = jnp.concatenate([heads[0], heads[1]], 1)
    narrow = jnp.concatenate([heads[2][:half], heads[2][half:]], 1)
    return wide, narrow


def greet(dp, me, count, others=()):
    barrier = pltpu.get_barrier_semaphore()
    for step in range(1, count):
        pl.semaphore_signal(
            barrier, inc=1, device_id=(dp, lax.rem(me + step, count)), device_id_type=MESH
        )
    for other in others:
        pl.semaphore_signal(barrier, inc=1, device_id=other, device_id_type=MESH)
    return lambda: pl.semaphore_wait(barrier, count - 1 + len(others))


def heads_of(wide, narrow):
    return [
        wide[:, :HEAD],
        wide[:, HEAD:],
        jnp.concatenate([narrow[:, :HEAD], narrow[:, HEAD:]], 0),
    ]


def columns_of(received, row, rows, blocks):
    pieces = []
    for chip in range(blocks // 2):
        block = 2 * chip + row
        pieces += heads_of(received[block, :rows, :], received[block, rows:, :])
    return jnp.concatenate(pieces, 1)


def normal(value):
    mean = jnp.mean(value, -1, keepdims=True)
    centred = value - mean
    scale = lax.rsqrt(jnp.mean(centred * centred, -1, keepdims=True) + epsilon)
    return centred * scale, scale


def normal_pull(grad, unit, scale):
    return scale * (
        grad - jnp.mean(grad, -1, keepdims=True) - unit * jnp.mean(grad * unit, -1, keepdims=True)
    )


def forward_kernel(
    lengths, views, x_ref, gain_ref, pad_ref, wq_in, wkv_in,
    normed_out, qa_out, ka_out, va_out, o_out, received,
    normed, qa, ka, va, o_ref, weight, wq_ref, wkv_ref, stage, peak, outgoing,
    fetch, sib_send, sib_recv, line_send, line_recv, out_send, out_recv, store,
):
    rows, width = x_ref.shape[1], x_ref.shape[2]
    blocks = normed.shape[0]
    heads = qa.shape[0]
    dp = lax.axis_index("dp")
    me = lax.axis_index("blk")
    z = me // 2
    core = lax.rem(me, 2)
    sibling = me + 1 - 2 * core
    lane = lax.broadcasted_iota(jnp.int32, (rows, LANES), 1)

    arrived = greet(dp, me, blocks)
    loads = [
        pltpu.make_async_copy(wq_in, wq_ref, fetch.at[0]),
        pltpu.make_async_copy(wkv_in, wkv_ref, fetch.at[1]),
    ]
    for copy in loads:
        copy.start()
    gain = gain_ref[...].reshape(1, width)

    def norm(value):
        return (normal(value.astype(f32))[0] * gain).astype(bf16)

    normed[me] = norm(x_ref[core])
    arrived()

    def place(block):
        return pl.ds(pl.multiple_of(block * rows, rows), rows)

    def keep(block, number):
        here = place(block)
        src, dst = (
            (normed.at[block], normed_out.at[block // 2, pl.ds(pl.multiple_of(lax.rem(block, 2) * rows, rows), rows)]),
            (ka.at[:, here, :], ka_out.at[:, here, :]),
            (va.at[:, here, :], va_out.at[:, here, :]),
            (qa.at[:, here, :], qa_out.at[:, here, :]),
            (outgoing.at[block], o_out.at[block]),
        )[number]
        return pltpu.make_async_copy(src, dst, store.at[block, number])

    def line_copy(block, up):
        return pltpu.make_async_remote_copy(
            src_ref=normed.at[block],
            dst_ref=normed.at[block],
            send_sem=line_send.at[block, up],
            recv_sem=line_recv.at[block],
            device_id=(dp, me + (2 if up else -2)),
            device_id_type=MESH,
        )

    @pl.when(z < 3)
    def _():
        line_copy(me, 1).start()

    @pl.when(z > 0)
    def _():
        line_copy(me, 0).start()

    stage[...] = norm(x_ref[1 - core])
    sib_copy = pltpu.make_async_remote_copy(
        src_ref=stage,
        dst_ref=normed.at[me],
        send_sem=sib_send,
        recv_sem=sib_recv,
        device_id=(dp, sibling),
        device_id_type=MESH,
    )
    sib_copy.start()

    for copy in loads:
        copy.wait()
    gap = jnp.zeros((width, LANES - HEAD), bf16)
    for chip in range(blocks // 2):

        @pl.when(z == chip)
        def _():
            for head in range(heads):
                at = (chip * heads + head) * HEAD
                for kind, piece in enumerate(
                    (
                        wq_ref[:, at : at + HEAD],
                        wkv_ref[:, at : at + HEAD],
                        wkv_ref[:, width + at : width + at + HEAD],
                    )
                ):
                    column = (head * 3 + kind) * LANES
                    weight[:, column : column + LANES] = jnp.concatenate([piece, gap], 1)

    ones = jnp.where((lane >= HEAD) & (lane < HEAD + 3), -1.0, 0.0)

    def bring(step, turn):
        chip = chip_order(z, step)
        block = 2 * chip + lax.rem(core + turn, 2)

        @pl.when((step == 0) & (turn == 1))
        def _():
            pltpu.make_async_remote_copy(
                src_ref=stage,
                dst_ref=normed.at[sibling],
                send_sem=sib_send,
                recv_sem=sib_recv,
                device_id=(dp, sibling),
                device_id_type=MESH,
            ).wait_recv()

        @pl.when(step > 0)
        def _():
            pltpu.make_async_remote_copy(
                src_ref=normed.at[block],
                dst_ref=normed.at[block],
                send_sem=line_send.at[block, 0],
                recv_sem=line_recv.at[block],
                device_id=(dp, sibling),
                device_id_type=MESH,
            ).wait_recv()

        @pl.when((step + turn > 0) & (chip <= z) & (z < 3))
        def _():
            line_copy(block, 1).start()

        @pl.when((step + turn > 0) & (chip >= z) & (z > 0))
        def _():
            line_copy(block, 0).start()

        keep(block, 0).start()
        pad_row = 1.0 - pad_ref[pl.ds(core, 1), place(block)].astype(f32)
        padded = jnp.transpose(jnp.broadcast_to(pad_row, (LANES, rows)))
        key, query = features(block, rows, lengths, views, core, padded)
        out = dot_nn(normed[block], weight[...]).astype(bf16).astype(f32)
        here = pl.ds(pl.multiple_of(block * rows, rows), rows)
        for head in range(heads):
            at = head * 3 * LANES
            qa[head, here, :] = (out[:, at : at + LANES] * (HEAD**-0.5) + query).astype(bf16)
            ka[head, here, :] = (out[:, at + LANES : at + 2 * LANES] + key).astype(bf16)
            va[head, here, :] = (out[:, at + 2 * LANES : at + 3 * LANES] + ones).astype(bf16)
            peak[head, here, :] = jnp.full((rows, LANES), -BIG, f32)
            o_ref[head, here, :] = jnp.zeros((rows, LANES), f32)
        keep(block, 1).start()
        keep(block, 2).start()

    wide = 2 * rows
    eye = lax.broadcasted_iota(jnp.int32, (wide, wide), 0) == lax.broadcasted_iota(
        jnp.int32, (wide, wide), 1
    )

    def attend(queries, keys, diagonal=False):
        found = []
        for head in range(heads):
            query = qa[head, queries, :]
            key = ka[head, keys, :]
            s = dot_nt(query, key)
            if diagonal:
                s = jnp.where(eye, dot_nt(query[:, :HEAD], key[:, :HEAD]), s)
            tiles = [s[:, i : i + LANES] for i in range(0, s.shape[1], LANES)]
            top = tiles[0]
            for tile in tiles[1:]:
                top = jnp.maximum(top, tile)
            old = peak[head, queries, :]
            new = jnp.maximum(old, jnp.max(top, -1, keepdims=True))
            p = jnp.concatenate([jnp.exp(tile - new).astype(bf16) for tile in tiles], 1)
            total = o_ref[head, queries, :] * jnp.exp(old - new) + dot_nn(p, va[head, keys, :])
            found.append((new, total))
        for head, (new, total) in enumerate(found):
            peak[head, queries, :] = new
            o_ref[head, queries, :] = total

    def out_copy(block):
        return pltpu.make_async_remote_copy(
            src_ref=outgoing.at[block],
            dst_ref=received.at[me],
            send_sem=out_send.at[block],
            recv_sem=out_recv.at[me],
            device_id=(dp, block),
            device_id_type=MESH,
        )

    def hand_back(chip):
        @pl.loop(0, 2)
        def _(turn):
            block = 2 * chip + lax.rem(core + turn, 2)
            here = pl.ds(pl.multiple_of(block * rows, rows), rows)
            results = []
            for head in range(heads):
                total = o_ref[head, here, :]
                mass = -total[:, HEAD : HEAD + 1]
                results.append((total / mass)[:, :HEAD].astype(bf16))
                log_total = peak[head, here, :] + jnp.log(mass)
                qa[head, here, :] = (
                    qa[head, here, :].astype(f32) - spread(log_total, HEAD + CODES + 1, lane)
                ).astype(bf16)
            both, third = pack_heads(results)
            outgoing[block, :rows, :] = both
            outgoing[block, rows:, :] = third

            @pl.when(block == me)
            def _():
                received[me, :rows, :] = both
                received[me, rows:, :] = third

            @pl.when(block != me)
            def _():
                out_copy(block).start()

            keep(block, 3).start()
            keep(block, 4).start()

    def span(chip):
        return pl.ds(pl.multiple_of(chip * wide, wide), wide)

    def across(chip):
        edge = (chip + 1) * wide
        attend(
            pl.ds(pl.multiple_of(edge - LANES, LANES), LANES),
            pl.ds(pl.multiple_of(edge, LANES), LANES),
        )

    @pl.loop(0, blocks // 2)
    def _(step):
        @pl.loop(0, 2)
        def _(turn):
            bring(step, turn)

        chip = chip_order(z, step)
        low, high = chip_span(z, step)

        @pl.when(chip > low)
        def _():
            across(chip - 1)

        @pl.when(chip < high)
        def _():
            across(chip)

        @pl.when((low == 0) & (chip == high) & (chip > 0))
        def _():
            hand_back(chip - 1)

        @pl.loop(low, high + 1)
        def _(other):
            top = jnp.maximum(chip, other)

            @pl.when(other == chip)
            def _():
                attend(span(chip), span(chip), True)

            @pl.when(other != chip)
            def _():
                attend(span(top), span(jnp.minimum(chip, other)))

            @pl.when((other >= chip) & (low == 0) & (high >= jnp.minimum(top + 1, blocks // 2 - 1)))
            def _():
                hand_back(top)

    sib_copy.wait_send()

    @pl.loop(0, blocks)
    def _(block):
        for number in range(5):
            keep(block, number).wait()

        @pl.when((block // 2 <= z) & (z < 3))
        def _():
            line_copy(block, 1).wait_send()

        @pl.when((block // 2 >= z) & (z > 0))
        def _():
            line_copy(block, 0).wait_send()

        @pl.when(block != me)
        def _():
            out_copy(block).wait_send()
            pltpu.make_async_remote_copy(
                src_ref=outgoing.at[block],
                dst_ref=received.at[block],
                send_sem=out_send.at[block],
                recv_sem=out_recv.at[block],
                device_id=(dp, block),
                device_id_type=MESH,
            ).wait_recv()


class Sums:
    def __init__(self, final, own, buffers, semaphores, local):
        self.final, self.own, self.local = final, own, local
        self.from_core, self.first, self.second, self.line, self.near, self.far = buffers
        self.sems = dict(zip(
            ("core", "first", "second", "inward", "across", "outward", "back", "wide", "twin"), semaphores
        ))
        self.count = own.shape[0]
        self.half, self.lanes = own.shape[1], own.shape[2]
        self.quarter = self.half // 4
        self.eighth = self.half // 8
        self.dp = lax.axis_index("dp")
        self.me = lax.axis_index("blk")
        self.core = lax.rem(self.me, 2)
        self.z = self.me // 2
        self.x = lax.rem(self.dp, 2)
        self.y = self.dp // 2
        self.along_x = (self.dp + 1 - 2 * self.x, self.me)
        self.along_y = (self.dp + 2 - 4 * self.y, self.me)
        self.twin = (self.dp, self.me + 1 - 2 * self.core)
        self.inner = (self.z == 1) | (self.z == 2)
        self.outer = (self.z == 0) | (self.z == 3)
        self.pair = (self.dp, self.me + 2 - 4 * lax.rem(self.z, 2))
        self.middle = (self.dp, jnp.where(self.z < 2, self.me + 2, self.me - 2))

    def copy(self, name, piece, src, dst, device, way=None):
        send, recv = self.sems[name]
        at = (piece,) if way is None else (piece, way)
        return pltpu.make_async_remote_copy(
            src_ref=src,
            dst_ref=dst,
            send_sem=send.at[at],
            recv_sem=recv.at[at],
            device_id=device,
            device_id_type=MESH,
        )

    def rows(self, start, count):
        return pl.ds(pl.multiple_of(start, 16), count)

    def place(self, ref, piece, start, count):
        cols = pl.ds(pl.multiple_of(lax.rem(piece, 2) * self.lanes, LANES), self.lanes)
        return ref.at[piece // 2, self.rows(start, count), cols]

    def to_core(self, piece, src=None):
        src = self.own.at[piece] if src is None else src
        return self.copy("core", piece, src, self.from_core.at[piece], self.twin)

    def to_first(self, piece):
        q = self.quarter
        return (
            self.copy("first", piece, self.own.at[piece, self.rows(q * (1 - self.x), q)], self.first.at[piece, 0], self.along_x, 0),
            self.copy("first", piece, self.own.at[piece, self.rows(2 * q + q * (1 - self.y), q)], self.first.at[piece, 1], self.along_y, 1),
        )

    def to_second(self, piece):
        q, e = self.quarter, self.eighth
        return (
            self.copy("second", piece, self.own.at[piece, self.rows(q * self.x + e * (1 - self.y), e)], self.second.at[piece, 0], self.along_y, 0),
            self.copy("second", piece, self.own.at[piece, self.rows(2 * q + q * self.y + e * (1 - self.x), e)], self.second.at[piece, 1], self.along_x, 1),
        )

    def inward(self, piece):
        return self.copy("inward", piece, self.line.at[piece], self.near.at[piece], self.pair)

    def across(self, piece):
        return self.copy("across", piece, self.line.at[piece], self.far.at[piece], self.middle)

    def outward(self, piece):
        return self.copy("outward", piece, self.far.at[piece], self.near.at[piece], self.pair)

    def mine(self):
        q, e = self.quarter, self.eighth
        base = self.core * self.half
        return base + q * self.x + e * self.y, base + 2 * q + q * self.y + e * self.x

    def keep(self, piece, total):
        e = self.eighth
        one, two = self.mine()
        return (
            pltpu.make_async_copy(total.at[piece, :e], self.place(self.final, piece, one, e), self.local.at[piece, 0]),
            pltpu.make_async_copy(total.at[piece, e:], self.place(self.final, piece, two, e), self.local.at[piece, 1]),
        )

    def back(self, piece, total):
        e = self.eighth
        one, two = self.mine()
        return (
            self.copy("back", piece, total.at[piece, :e], self.place(self.final, piece, one, e), self.along_y, 0),
            self.copy("back", piece, total.at[piece, e:], self.place(self.final, piece, two, e), self.along_x, 1),
        )

    def wide(self, piece):
        q = self.quarter
        base = self.core * self.half
        one = self.place(self.final, piece, base + q * self.x, q)
        two = self.place(self.final, piece, base + 2 * q + q * self.y, q)
        return (
            self.copy("wide", piece, one, one, self.along_x, 0),
            self.copy("wide", piece, two, two, self.along_y, 1),
        )

    def to_twin(self, piece):
        part = self.place(self.final, piece, self.core * self.half, self.half)
        return self.copy("twin", piece, part, part, self.twin)

    def step_1(self, piece):
        self.to_core(piece).wait_recv()
        self.own[piece] = self.own[piece] + self.from_core[piece]
        for copy in self.to_first(piece):
            copy.start()

    def step_2(self, piece):
        q = self.quarter
        one, two = self.to_first(piece)
        one.wait_recv()
        at = self.rows(q * self.x, q)
        self.own[piece, at, :] = self.own[piece, at, :] + self.first[piece, 0]
        two.wait_recv()
        at = self.rows(2 * q + q * self.y, q)
        self.own[piece, at, :] = self.own[piece, at, :] + self.first[piece, 1]
        for copy in self.to_second(piece):
            copy.start()

    def step_3(self, piece):
        q, e = self.quarter, self.eighth
        one, two = self.to_second(piece)
        one.wait_recv()
        at = self.rows(q * self.x + e * self.y, e)
        self.line[piece, :e, :] = self.own[piece, at, :] + self.second[piece, 0]
        two.wait_recv()
        at = self.rows(2 * q + q * self.y + e * self.x, e)
        self.line[piece, e:, :] = self.own[piece, at, :] + self.second[piece, 1]

        @pl.when(self.outer)
        def _():
            self.inward(piece).start()

    def step_4(self, piece):
        @pl.when(self.inner)
        def _():
            self.inward(piece).wait_recv()
            self.line[piece] = self.line[piece] + self.near[piece]
            self.across(piece).start()

    def step_5(self, piece):
        @pl.when(self.inner)
        def _():
            self.across(piece).wait_recv()
            self.far[piece] = self.line[piece] + self.far[piece]
            self.outward(piece).start()

    def step_6(self, piece):
        @pl.when(self.outer)
        def _():
            self.outward(piece).wait_recv()
            for copy in self.back(piece, self.near) + self.keep(piece, self.near):
                copy.start()

        @pl.when(self.inner)
        def _():
            for copy in self.back(piece, self.far) + self.keep(piece, self.far):
                copy.start()

    def step_7(self, piece):
        for copy in self.keep(piece, self.near):
            copy.wait()
        for copy in self.back(piece, self.near):
            copy.wait_recv()
        for copy in self.wide(piece):
            copy.start()

    def step_8(self, piece):
        for copy in self.wide(piece):
            copy.wait_recv()
        self.to_twin(piece).start()

    def step_9(self, piece):
        self.to_twin(piece).wait_recv()

    def tick(self, numbers, offsets, time, last):
        for place in reversed(range(len(numbers))):
            piece = time - offsets[place]

            @pl.when((piece >= 0) & (piece < last))
            def _():
                getattr(self, "step_" + str(numbers[place]))(piece)

    def finish(self, piece):
        for copies in (self.to_first(piece), self.to_second(piece), self.back(piece, self.near), self.wide(piece)):
            for copy in copies:
                copy.wait_send()
        self.to_twin(piece).wait_send()

        @pl.when(self.outer)
        def _():
            self.inward(piece).wait_send()

        @pl.when(self.inner)
        def _():
            self.across(piece).wait_send()
            self.outward(piece).wait_send()

    @staticmethod
    def scratch(count, half, lanes):
        def array(*shape):
            return pltpu.VMEM((count,) + shape + (lanes,), bf16)

        quarter, eighth = half // 4, half // 8
        dma = pltpu.SemaphoreType.DMA
        one, two = [dma((count,))] * 2, [dma((count, 2))] * 2
        return (
            [array(half)] * 2
            + [array(2, quarter), array(2, eighth)]
            + [array(quarter)] * 3
            + one + two + two + one + one + one + two + two + one
            + [dma((count, 2))]
        )

    @classmethod
    def gather(cls, final, refs):
        sems = refs[7:25]
        pairs = [(sems[2 * i], sems[2 * i + 1]) for i in range(9)]
        return cls(final, refs[0], refs[1:7], pairs, refs[25])


class UnitSum:
    def __init__(self, sums, final, refs):
        self.sums, self.final = sums, final
        (
            self.own, self.give, self.from_core, self.first, self.second, self.line,
            self.core_sems, self.first_sems, self.second_sems, self.line_send, self.line_recv,
            self.back_sems, self.wide_sems, self.twin_sems, self.local,
        ) = refs

    def copy(self, sems, at, src, dst, device):
        return pltpu.make_async_remote_copy(
            src_ref=src,
            dst_ref=dst,
            send_sem=sems.at[0, at],
            recv_sem=sems.at[1, at],
            device_id=device,
            device_id_type=MESH,
        )

    def to_core(self):
        return self.copy(self.core_sems, 0, self.give, self.from_core, self.sums.twin)

    def to_first(self):
        s, q = self.sums, self.sums.quarter
        return (
            self.copy(self.first_sems, 0, self.own.at[s.rows(q * (1 - s.x), q)], self.first.at[0], s.along_x),
            self.copy(self.first_sems, 1, self.own.at[s.rows(2 * q + q * (1 - s.y), q)], self.first.at[1], s.along_y),
        )

    def to_second(self):
        s, q, e = self.sums, self.sums.quarter, self.sums.eighth
        return (
            self.copy(self.second_sems, 0, self.own.at[s.rows(q * s.x + e * (1 - s.y), e)], self.second.at[0], s.along_y),
            self.copy(self.second_sems, 1, self.own.at[s.rows(2 * q + q * s.y + e * (1 - s.x), e)], self.second.at[1], s.along_x),
        )

    def along_line(self, chip):
        s = self.sums
        return pltpu.make_async_remote_copy(
            src_ref=self.line.at[s.z],
            dst_ref=self.line.at[s.z],
            send_sem=self.line_send.at[chip],
            recv_sem=self.line_recv.at[s.z],
            device_id=(s.dp, 2 * chip + s.core),
            device_id_type=MESH,
        )

    def from_line(self, chip):
        s = self.sums
        return pltpu.make_async_remote_copy(
            src_ref=self.line.at[chip],
            dst_ref=self.line.at[chip],
            send_sem=self.line_send.at[chip],
            recv_sem=self.line_recv.at[chip],
            device_id=(s.dp, 2 * chip + s.core),
            device_id_type=MESH,
        )

    def keep(self):
        s, e = self.sums, self.sums.eighth
        one, two = s.mine()
        return (
            pltpu.make_async_copy(self.line.at[:, :e], self.final.at[:, s.rows(one, e)], self.local.at[0]),
            pltpu.make_async_copy(self.line.at[:, e:], self.final.at[:, s.rows(two, e)], self.local.at[1]),
        )

    def back(self):
        s, e = self.sums, self.sums.eighth
        one, two = s.mine()
        return (
            self.copy(self.back_sems, 0, self.line.at[:, :e], self.final.at[:, s.rows(one, e)], s.along_y),
            self.copy(self.back_sems, 1, self.line.at[:, e:], self.final.at[:, s.rows(two, e)], s.along_x),
        )

    def wide(self):
        s, q = self.sums, self.sums.quarter
        base = s.core * s.half
        one = self.final.at[:, s.rows(base + q * s.x, q)]
        two = self.final.at[:, s.rows(base + 2 * q + q * s.y, q)]
        return (
            self.copy(self.wide_sems, 0, one, one, s.along_x),
            self.copy(self.wide_sems, 1, two, two, s.along_y),
        )

    def to_twin(self):
        s = self.sums
        part = self.final.at[:, s.rows(s.core * s.half, s.half)]
        return self.copy(self.twin_sems, 0, part, part, s.twin)

    def step(self, number):
        s, q, e = self.sums, self.sums.quarter, self.sums.eighth
        if number == 0:
            self.to_core().start()
        elif number == 1:
            self.to_core().wait_recv()
            self.own[...] = self.own[...] + self.from_core[...]
            for copy in self.to_first():
                copy.start()
        elif number == 2:
            for way, start in ((0, q * s.x), (1, 2 * q + q * s.y)):
                self.to_first()[way].wait_recv()
                at = s.rows(start, q)
                self.own[at, :] = self.own[at, :] + self.first[way]
            for copy in self.to_second():
                copy.start()
        elif number == 3:
            for way, start in ((0, q * s.x + e * s.y), (1, 2 * q + q * s.y + e * s.x)):
                self.to_second()[way].wait_recv()
                self.line[s.z, way * e : (way + 1) * e, :] = self.own[s.rows(start, e), :] + self.second[way]
            for ahead in (2, 1, 3):
                self.along_line(lax.rem(s.z + ahead, 4)).start()
        elif number == 4:
            for ahead in (1, 2, 3):
                self.from_line(lax.rem(s.z + ahead, 4)).wait_recv()
            for copy in self.back() + self.keep():
                copy.start()
        elif number == 5:
            for copy in self.keep():
                copy.wait()
            for copy in self.back():
                copy.wait_recv()
            for copy in self.wide():
                copy.start()
        elif number == 6:
            for copy in self.wide():
                copy.wait_recv()
            self.to_twin().start()
        else:
            self.to_twin().wait_recv()

    def finish(self):
        s = self.sums
        for copy in (self.to_core(), self.to_twin()) + self.to_first() + self.to_second() + self.back() + self.wide():
            copy.wait_send()
        for ahead in (1, 2, 3):
            self.along_line(lax.rem(s.z + ahead, 4)).wait_send()

    @staticmethod
    def scratch(chips, half, lanes):
        dma = pltpu.SemaphoreType.DMA
        quarter, eighth = half // 4, half // 8
        array = [pltpu.VMEM((half, lanes), bf16)]
        return (
            array * 3
            + [
                pltpu.VMEM((2, quarter, lanes), bf16),
                pltpu.VMEM((2, eighth, lanes), bf16),
                pltpu.VMEM((chips, quarter, lanes), bf16),
                dma((2, 1)),
                dma((2, 2)),
                dma((2, 2)),
                dma((chips,)),
                dma((chips,)),
                dma((2, 2)),
                dma((2, 2)),
                dma((2, 1)),
                dma((2,)),
            ]
        )


def backward_kernel(
    first_gain, second_gain, received_in, x_in, up_in, normed_in, qa_in, ka_in, va_in, o_in,
    wq_in, wkv_in, wo_in, we_in, wc_in,
    result_ref, input_grad, final, pair_final, query_final,
    acts, pool, result_acc, second_acc, out, grad_out, received, key_turned, dqt, dvk, send_query, send_pair,
    got_query, got_pair, give,
    load_tiles, load_first, load_output, load_heads, load_late, out_send, out_recv, query_send, query_recv, pair_send, pair_recv,
    save, *sum_refs,
):
    blocks, packed = grad_out.shape[0], grad_out.shape[1]
    rows = 2 * packed // 3
    micro, _, width = input_grad.shape
    heads, _, total = key_turned.shape
    chips = blocks // 2
    tall = acts.shape[1]
    tiles = width // LANES
    dp = lax.axis_index("dp")
    me = lax.axis_index("blk")
    z = me // 2
    core = lax.rem(me, 2)
    lane = lax.broadcasted_iota(jnp.int32, (rows, LANES), 1)
    sums = Sums.gather(final, sum_refs[:26])
    pair_sum = UnitSum(sums, pair_final, sum_refs[26:41])
    query_sum = UnitSum(sums, query_final, sum_refs[41:])
    count = sums.count
    parts = (count // 2 - 1) // 2
    low, up, attended, branch = 2 * parts, 2 * parts + 1, 2 * parts + 2, 2 * parts + 3
    arrived = greet(dp, me, blocks, (sums.along_x, sums.along_y))

    at_query, at_key, at_value, at_grad, at_right = (number * heads * total for number in range(5))

    def in_pool(base, head, start, size):
        return pl.ds(pl.multiple_of(base + head * total + start, LANES), size)

    def fetch(number):
        part = number % parts
        copies = []
        for tile in range(tiles):
            if number < parts:
                src = we_in.at[:, pl.ds(part * width + tile * LANES, LANES)]
            else:
                src = wc_in.at[pl.ds(part * width, width), pl.ds(tile * LANES, LANES)]
            place = number * tiles + tile
            copies.append(
                pltpu.make_async_copy(src, pool.at[pl.ds(place * width, width)], load_tiles.at[place])
            )
        return copies

    def weight(number):
        return jnp.concatenate(
            [pool[pl.ds(pl.multiple_of((number * tiles + tile) * width, LANES), width), :] for tile in range(tiles)], 1
        )

    def openers():
        copies = [
            pltpu.make_async_copy(received_in, send_query, load_first.at[0]),
        ]
        for tile in range(tiles):
            src = wo_in.at[:, pl.ds(tile * LANES, LANES)]
            copies.append(pltpu.make_async_copy(src, send_pair.at[tile], load_output.at[tile]))
        for row in range(micro):
            here = pl.ds(row * rows, rows)
            copies.append(pltpu.make_async_copy(x_in.at[row], acts.at[branch, here], load_first.at[1 + 2 * row]))
            copies.append(pltpu.make_async_copy(up_in.at[row], acts.at[up, here], load_first.at[2 + 2 * row]))
        return copies

    def load_head(number):
        src = (qa_in, ka_in, va_in, o_in)[number]
        base = (at_query, at_key, at_value)
        dst = out if number == 3 else pool.at[pl.ds(base[number], heads * total)]
        return pltpu.make_async_copy(src, dst, load_heads.at[number])

    for copy in openers():
        copy.start()
    for part in range(parts):
        for copy in fetch(part) + fetch(parts + part):
            copy.start()

    kinds = {
        "grad": (grad_out, received, out_send, out_recv),
        "query": (send_query, got_query, query_send, query_recv),
        "pair": (send_pair, got_pair, pair_send, pair_recv),
    }

    def send(kind, block):
        src, dst, send_sem, recv_sem = kinds[kind]
        return pltpu.make_async_remote_copy(
            src_ref=src.at[block],
            dst_ref=dst.at[me],
            send_sem=send_sem.at[block],
            recv_sem=recv_sem.at[me],
            device_id=(dp, block),
            device_id_type=MESH,
        )

    def arrive(kind, block):
        src, dst, send_sem, recv_sem = kinds[kind]
        return pltpu.make_async_remote_copy(
            src_ref=src.at[block],
            dst_ref=dst.at[block],
            send_sem=send_sem.at[block],
            recv_sem=recv_sem.at[block],
            device_id=(dp, block),
            device_id_type=MESH,
        )

    def message(number):
        return 2 * far_order(z, number // 2) + lax.rem(core + number, 2)

    def slot(time):
        for kind, starts in (("pair", PAIR_SLOTS), ("query", QUERY_SLOTS)):
            for number, start in enumerate(starts):
                block = message(jnp.int32(2 * chips - 1 if number == 2 * chips - 2 else number))

                @pl.when(time == start)
                def _():
                    send(kind, block).start()

        sums.tick(OUT, OUT_AT, time, count)
        sums.tick(BACK, BACK_AT, time - LATE, count)

    side = sums.half

    def weigh(piece):
        whole = piece // 2
        left = jnp.where(whole < parts, whole, jnp.where(whole < 2 * parts, low, attended))
        right = jnp.where(whole < parts, up, jnp.where(whole < 2 * parts, whole, branch))
        cols = pl.ds(pl.multiple_of(lax.rem(piece, 2) * side, LANES), side)
        turn = lax.rem(piece, GIVE)

        theirs = pl.ds(pl.multiple_of((1 - core) * side, 16), side)
        ours = pl.ds(pl.multiple_of(core * side, 16), side)

        @pl.when(piece >= GIVE)
        def _():
            sums.to_core(piece - GIVE, give.at[turn, theirs]).wait_send()

        give[turn] = dot_tn(acts[left], acts[right, :, cols]).astype(bf16)
        sums.to_core(piece, give.at[turn, theirs]).start()
        sums.own[piece] = give[turn, ours, :]

    def output():
        return jnp.concatenate([send_pair[tile] for tile in range(tiles)], 1)

    opening = openers()
    gain = second_gain[...].reshape(1, width)
    opening[0].wait()
    for row in range(micro):
        acts[attended, row * rows : (row + 1) * rows, :] = columns_of(send_query, row, rows, blocks)
    for copy in opening[1:]:
        copy.wait()
    for row in range(micro):
        at = slice(row * rows, (row + 1) * rows)
        value = acts[branch, at, :].astype(f32) + dot_nn(acts[attended, at, :], output())
        result_acc[at, :] = value
        acts[low, at, :] = (normal(value)[0] * gain).astype(bf16)
    second_acc[...] = jnp.zeros_like(second_acc)

    def through(part, row):
        at = slice(row * rows, (row + 1) * rows)
        widen, narrow = weight(part), weight(parts + part)
        hidden = dot_nn(acts[low, at, :], widen)
        active_grad = dot_nt(acts[up, at, :], narrow)
        square = hidden * hidden
        c = 0.7978845608028654
        bend = jnp.tanh(hidden * (c + 0.044715 * c * square))
        gate = 0.5 + 0.5 * bend
        slope = gate + 0.5 * hidden * (1.0 - bend * bend) * (c + 3.0 * 0.044715 * c * square)
        active = (hidden * gate).astype(bf16)
        grad = (active_grad * slope).astype(bf16)
        acts[part, at, :] = active
        acts[parts + part, at, :] = grad
        result_acc[at, :] += dot_nn(active, narrow)
        second_acc[at, :] += dot_nt(grad, widen)

    def turn_back(row):
        at = slice(row * rows, (row + 1) * rows)
        result_ref[row] = result_acc[at, :].astype(bf16)
        project = output()
        value = acts[branch, at, :].astype(f32) + dot_nn(acts[attended, at, :], project)
        unit_, scale = normal(value)
        grad = acts[up, at, :].astype(f32) + normal_pull(second_acc[at, :] * gain, unit_, scale)
        second_acc[at, :] = grad
        acts[branch, at, :] = grad.astype(bf16)
        back = dot_nt(acts[branch, at, :], project).astype(bf16)
        for chip in range(chips):
            start = chip * heads * HEAD
            wide, narrow = pack_heads(
                [back[:, start + h * HEAD : start + (h + 1) * HEAD] for h in range(heads)]
            )
            grad_out[2 * chip + row, :rows, :] = wide
            grad_out[2 * chip + row, rows:, :] = narrow
        for step in range(chips):
            block = 2 * far_order(z, jnp.int32(step)) + row

            @pl.when(block != me)
            def _():
                send("grad", block).start()

    for part in range(parts):
        for copy in fetch(part) + fetch(parts + part):
            copy.wait()
        through(part, 0)
    arrived()
    turn_back(0)

    @pl.loop(0, parts)
    def _(part):
        through(part, 1)
        for turn in range(2):
            weigh(2 * part + turn)

            @pl.when(part > 0)
            def _():
                slot(2 * part - 2 + turn)

    turn_back(1)
    received[me] = grad_out[me]
    for number in range(4):
        load_head(number).start()

    for number in range(2 * parts - 2, 2 * parts):
        slot(jnp.int32(number))

    @pl.loop(2 * parts, count)
    def _(piece):
        weigh(piece)

        @pl.when((lax.rem(piece, 2) == 1) & (piece > 2 * parts + 1))
        def _():
            slot(2 * parts + (piece - 2 * parts - 3) // 2)

    squares = [(wq_in, 0), (wkv_in, 0), (wkv_in, width)]

    def late():
        copies = [
            pltpu.make_async_copy(normed_in.at[chip], acts.at[chip], load_late.at[chip]) for chip in range(chips)
        ]
        for number, (src, start) in enumerate(squares):
            cols = pl.ds(start, width)
            copies.append(
                pltpu.make_async_copy(
                    src.at[pl.ds(0, tall), cols], acts.at[chips + 2 * number], load_late.at[chips + 2 * number]
                )
            )
            copies.append(
                pltpu.make_async_copy(
                    src.at[pl.ds(tall, width - tall), cols],
                    acts.at[chips + 2 * number + 1, pl.ds(0, width - tall)],
                    load_late.at[chips + 2 * number + 1],
                )
            )
        for row in range(micro):
            copies.append(
                pltpu.make_async_copy(
                    x_in.at[row],
                    acts.at[chips + 6, pl.ds(row * rows, rows)],
                    load_late.at[chips + 6 + row],
                )
            )
        return copies

    for copy in late():
        copy.start()

    dqt[...] = jnp.zeros_like(dqt)
    for number in range(4):
        load_head(number).wait()

    @pl.loop(0, blocks)
    def _(block):
        here = pl.ds(pl.multiple_of(block * rows, rows), rows)
        for head in range(heads):
            key = pool[in_pool(at_key, head, block * rows, rows), :][:, :HEAD].astype(f32)
            key_turned[head, :, here] = jnp.transpose(key).astype(bf16)
            query = pool[in_pool(at_query, head, block * rows, rows), :][:, :HEAD]
            pool[in_pool(at_right, head, block * rows, rows), :] = jnp.concatenate([jnp.zeros_like(query), query], 1)

    @pl.loop(0, blocks)
    def _(step):
        block = 2 * chip_order(z, step // 2) + lax.rem(core + step, 2)

        @pl.when(block != me)
        def _():
            arrive("grad", block).wait_recv()

        wide = received[block, :rows, :].astype(f32)
        narrow = received[block, rows:, :].astype(f32)
        shares = heads_of(wide * out[block, :rows, :].astype(f32), narrow * out[block, rows:, :].astype(f32))
        gap = jnp.zeros((rows, LANES - HEAD), f32)
        for head, piece in enumerate(heads_of(wide, narrow)):
            delta = jnp.sum(shares[head], -1, keepdims=True)
            value = jnp.concatenate([piece, gap], 1)
            pool[in_pool(at_grad, head, block * rows, rows), :] = (value + spread(delta, HEAD, lane)).astype(bf16)

    wide_rows = 2 * rows
    eye = lax.broadcasted_iota(jnp.int32, (wide_rows, wide_rows), 0) == lax.broadcasted_iota(
        jnp.int32, (wide_rows, wide_rows), 1
    )
    half = LANES

    def pull(keys, queries, diagonal=False):
        found = []
        for head in range(heads):
            k = pool[in_pool(at_key, head, *keys), :]
            q = pool[in_pool(at_query, head, *queries), :]
            g = pool[in_pool(at_grad, head, *queries), :]
            at = lax.broadcasted_iota(jnp.int32, k.shape, 1)
            s = dot_nt(k, q)
            if diagonal:
                bare = (at < HEAD) | (at > HEAD + CODES)
                s = jnp.where(eye, dot_nt(jnp.where(bare, k, 0.0).astype(bf16), q), s)
            p = jnp.exp(s)
            ds = (p * dot_nt(pool[in_pool(at_value, head, *keys), :], g)).astype(bf16)
            left = jnp.concatenate([p.astype(bf16), ds], 1)
            at = lax.broadcasted_iota(jnp.int32, g.shape, 1)
            value = jnp.where(at < HEAD, g, 0.0).astype(bf16)
            right = jnp.concatenate([value, pool[in_pool(at_right, head, *queries), :]], 0)
            turned = key_turned[head, :, pl.ds(pl.multiple_of(keys[0], LANES), keys[1])]
            found.append((dot_nn(left, right), dot_nn(turned, ds)))
        return found

    @pl.loop(0, chips)
    def _(step):
        chip = far_order(z, step)
        span = (chip * wide_rows, wide_rows)
        here = pl.ds(pl.multiple_of(chip * wide_rows, wide_rows), wide_rows)
        for head, (pair, query) in enumerate(pull(span, span, True)):
            dvk[head] = pair
            dqt[head, :, here] += query
        time = EARLY
        for earlier in range(chips - 1):
            done = far_order(z, earlier)
            bodies = chips - done + jnp.where(done > 0, 1, 0)
            time = time + jnp.where(earlier < step, bodies, 0)
        slot(time)

        @pl.loop(chip + 1, chips)
        def _(other):
            there = pl.ds(pl.multiple_of(other * wide_rows, wide_rows), wide_rows)
            for head, (pair, query) in enumerate(pull(span, (other * wide_rows, wide_rows))):
                dvk[head] += pair
                dqt[head, :, there] += query
            slot(time + other - chip)

        @pl.when(chip > 0)
        def _():
            edge = chip * wide_rows
            queries = pl.ds(pl.multiple_of(edge - half, half), half)
            for head, (pair, query) in enumerate(pull((edge, half), (edge - half, half))):
                dvk[head, :half] += pair
                dqt[head, :, queries] += query
            slot(time + chips - chip)

        for turn in range(2):
            block = 2 * chip + turn
            for head in range(heads):
                send_pair[block, head * rows : (head + 1) * rows, :] = dvk[
                    head, turn * rows : (turn + 1) * rows
                ].astype(bf16)

            @pl.when(block == me)
            def _():
                got_pair[me] = send_pair[me]

    for copy in late():
        copy.wait()

    def columns(tile):
        right = jnp.concatenate([jnp.concatenate(tile(block), 1) for block in range(blocks)], 0)
        for unit, which in (("give", 1 - core), ("own", core)):
            cols = pl.ds(pl.multiple_of(which * side, LANES), side)
            left = acts[:chips, :, cols].reshape(total, side)
            yield unit, dot_tn(left, right).astype(bf16)

    for unit, value in columns(
        lambda block: [send_pair[block, head * rows : (head + 1) * rows, :] for head in range(heads)]
    ):
        getattr(pair_sum, unit)[...] = value
        if unit == "give":
            pair_sum.step(0)
    slot(jnp.int32(EARLY + 13))

    @pl.loop(0, blocks)
    def _(block):
        here = pl.ds(pl.multiple_of(block * rows, rows), rows)
        wide, narrow = pack_heads(
            [(jnp.transpose(dqt[h, :, here]) * (HEAD**-0.5)).astype(bf16) for h in range(heads)]
        )
        send_query[block, :rows, :] = wide
        send_query[block, rows:, :] = narrow

        @pl.when(block == me)
        def _():
            got_query[me] = send_query[me]

    gap = jnp.zeros((rows, LANES - HEAD), bf16)
    for unit, value in columns(
        lambda block: heads_of(send_query[block, :rows, :], send_query[block, rows:, :]) + [gap]
    ):
        getattr(query_sum, unit)[...] = value
        if unit == "give":
            query_sum.step(0)
    slot(jnp.int32(EARLY + 14))

    ready = EARLY + 15
    end = LATE + count + BACK_AT[-1]

    def normed_part(row, operands, first):
        grad = []
        for part in range(2):
            height = tall if part == 0 else width - tall
            total_ = jnp.zeros((rows, height), f32)
            for number, operand in enumerate(operands):
                total_ = total_ + dot_nt(operand, acts[chips + 2 * (first + number) + part, :height])
            grad.append(total_)
        return jnp.concatenate(grad, 1)

    def pair_part(row):
        keys, values = [], []
        for chip in range(chips):
            for head in range(heads):
                both = got_pair[2 * chip + row, head * rows : (head + 1) * rows, :]
                keys.append(both[:, HEAD:])
                values.append(both[:, :HEAD])
        operands = [jnp.concatenate(keys, 1), jnp.concatenate(values, 1)]
        result_acc[row * rows : (row + 1) * rows, :] = normed_part(row, operands, 1)

    def last(row):
        at = slice(row * rows, (row + 1) * rows)
        grad = result_acc[at, :] + normed_part(row, [columns_of(got_query, row, rows, blocks)], 0)
        unit_, scale = normal(acts[chips + 6, at, :].astype(f32))
        pulled = normal_pull(grad * first_gain[...].reshape(1, width), unit_, scale)
        acts[chips + 7, at, :] = (second_acc[at, :] + pulled).astype(bf16)
        return pltpu.make_async_copy(acts.at[chips + 7, pl.ds(row * rows, rows)], input_grad.at[row], save.at[row])

    def wait_for(kind):
        @pl.loop(0, blocks)
        def _(block):
            @pl.when(block != me)
            def _():
                arrive(kind, block).wait_recv()

    @pl.loop(ready, max(end, ready + max(PAIR_SUM_SLOTS + QUERY_SUM_SLOTS) + 1))
    def _(time):
        for unit, places in ((pair_sum, PAIR_SUM_SLOTS), (query_sum, QUERY_SUM_SLOTS)):
            for number, place in enumerate(places):

                @pl.when(time == ready + place)
                def _():
                    unit.step(number + 1)

        slot(time)

        @pl.when(time == PAIR_DONE)
        def _():
            wait_for("pair")
            for row in range(micro):
                pair_part(row)

    wait_for("query")
    saves = [last(row) for row in range(micro)]
    for copy in saves:
        copy.start()

    @pl.loop(0, blocks)
    def _(block):
        @pl.when(block != me)
        def _():
            send("grad", block).wait_send()
            send("query", block).wait_send()
            send("pair", block).wait_send()

    theirs = pl.ds(pl.multiple_of((1 - core) * side, 16), side)
    for piece in range(count - GIVE, count):
        sums.to_core(piece, give.at[piece % GIVE, theirs]).wait_send()

    @pl.loop(0, count)
    def _(piece):
        sums.finish(piece)

    pair_sum.finish()
    query_sum.finish()
    for copy in saves:
        copy.wait()


def final_kernel(
    final, we_ref, first_gain, second_gain, pair_in, query_in, wq_in, wkv_in, result_in, grad_in,
    first_ref, query_ref, pair_ref, output_ref, second_ref, expand_ref, contract_ref, result_out, grad_out,
    first_acc, second_acc, pair_unit, query_unit, wq_ref, wkv_ref, fetch,
):
    step = pl.program_id(0)
    width = wq_ref.shape[0]
    chips = pair_in.shape[0]
    heads = width // HEAD // chips
    parts = (pl.num_programs(0) - 4) // 2

    def fold(array):
        return sum(array[:, i : i + LANES] for i in range(0, width, LANES))

    def loads():
        pairs = ((pair_in, pair_unit), (query_in, query_unit), (wq_in, wq_ref), (wkv_in, wkv_ref))
        return [pltpu.make_async_copy(src, dst, fetch.at[i]) for i, (src, dst) in enumerate(pairs)]

    @pl.when(step == 0)
    def _():
        for copy in loads():
            copy.start()
        first_acc[...] = jnp.zeros_like(first_acc)
        second_acc[...] = jnp.zeros_like(second_acc)

    @pl.when(step == 1)
    def _():
        result_out[...] = result_in[...]
        grad_out[...] = grad_in[...]

    @pl.when(step < parts)
    def _():
        contract_ref[...] = final[0].astype(f32)

    @pl.when((step >= parts) & (step < 2 * parts))
    def _():
        value = final[0].astype(f32)
        expand_ref[...] = value
        second_acc[...] += fold(value * we_ref[...].astype(f32))

    @pl.when(step == 2 * parts)
    def _():
        output_ref[...] = final[0].astype(f32)

    def columns(unit, place):
        return jnp.concatenate(
            [unit[chip][:, place(head) : place(head) + HEAD] for chip in range(chips) for head in range(heads)], 1
        ).astype(f32)

    @pl.when(step == 2 * parts + 1)
    def _():
        for copy in loads():
            copy.wait()
        value = columns(query_unit, lambda head: head * HEAD)
        query_ref[...] = value
        first_acc[...] += fold(value * wq_ref[...].astype(f32))

    for side in range(2):

        @pl.when(step == 2 * parts + 2 + side)
        def _():
            value = columns(pair_unit, lambda head: head * LANES + (HEAD if side == 0 else 0))
            pair_ref[...] = value
            first_acc[...] += fold(value * wkv_ref[:, side * width : (side + 1) * width].astype(f32))

    @pl.when(step == pl.num_programs(0) - 1)
    def _():
        first_ref[...] = jnp.sum(jnp.transpose(first_acc[...]), 0) / first_gain[...]
        second_ref[...] = jnp.sum(jnp.transpose(second_acc[...]), 0) / second_gain[...]


VMEM = pl.BlockSpec(memory_space=pltpu.VMEM)
SMEM = pl.BlockSpec(memory_space=pltpu.SMEM)
ANY = pl.BlockSpec(memory_space=pl.ANY)


def attention_forward(inputs, gain, lengths, views, padding, query_weight, pair_weight, blocks):
    micro, rows, width = inputs.shape
    total = rows * blocks
    heads = width // HEAD // (blocks // micro)
    packed = rows * heads // 2
    shape = jax.ShapeDtypeStruct
    dma = pltpu.SemaphoreType.DMA
    unit = (heads, total, LANES)
    return pl.pallas_call(
        forward_kernel,
        out_shape=(
            shape((blocks // 2, 2 * rows, width), bf16),
            shape(unit, bf16),
            shape(unit, bf16),
            shape(unit, bf16),
            shape((blocks, packed, LANES), bf16),
            shape((blocks, packed, LANES), bf16),
        ),
        in_specs=[SMEM, SMEM] + [VMEM] * 3 + [ANY] * 2,
        out_specs=(ANY,) * 5 + (VMEM,),
        scratch_shapes=[
            pltpu.VMEM((blocks, rows, width), bf16),
            pltpu.VMEM(unit, bf16),
            pltpu.VMEM(unit, bf16),
            pltpu.VMEM(unit, bf16),
            pltpu.VMEM(unit, f32),
            pltpu.VMEM((width, heads * 3 * LANES), bf16),
            pltpu.VMEM(query_weight.shape, bf16),
            pltpu.VMEM(pair_weight.shape, bf16),
            pltpu.VMEM((rows, width), bf16),
            pltpu.VMEM(unit, f32),
            pltpu.VMEM((blocks, packed, LANES), bf16),
            dma((2,)),
            dma,
            dma,
            dma((blocks, 2)),
            dma((blocks,)),
            dma((blocks,)),
            dma((blocks,)),
            dma((blocks, 5)),
        ],
        compiler_params=pltpu.CompilerParams(
            collective_id=0, has_side_effects=True, vmem_limit_bytes=63 << 20
        ),
        name="attention_forward",
    )(lengths, views, inputs, gain, padding, query_weight, pair_weight)


def attention_backward(
    first_gain, second_gain, received, inputs, cotangent, normed, qa, ka, va, out,
    query_weight, pair_weight, output_weight, expand_weight, contract_weight,
):
    micro, rows, width = inputs.shape
    blocks, packed, _ = received.shape
    heads, total, _ = qa.shape
    chips = blocks // 2
    tokens = micro * rows
    parts = expand_weight.shape[1] // width
    pieces = 2 * parts + 1
    count = 2 * pieces
    side = width // 2
    flat = (heads * total, LANES)
    shape = jax.ShapeDtypeStruct
    dma = pltpu.SemaphoreType.DMA
    message = pltpu.VMEM((blocks, packed, LANES), bf16)
    return pl.pallas_call(
        backward_kernel,
        out_shape=(
            shape(inputs.shape, bf16),
            shape(inputs.shape, bf16),
            shape((pieces, width, width), bf16),
            shape((chips, width, heads * LANES), bf16),
            shape((chips, width, 2 * LANES), bf16),
        ),
        in_specs=[VMEM] * 2 + [ANY] * 13,
        out_specs=(VMEM, ANY, ANY, ANY, ANY),
        scratch_shapes=[
            pltpu.VMEM((2 * parts + 4, tokens, width), bf16),
            pltpu.VMEM((2 * parts * width // LANES * width, LANES), bf16),
            pltpu.VMEM((tokens, width), f32),
            pltpu.VMEM((tokens, width), f32),
            message,
            message,
            message,
            pltpu.VMEM((heads, HEAD, total), bf16),
            pltpu.VMEM((heads, HEAD, total), f32),
            pltpu.VMEM((heads, 2 * rows, LANES), f32),
            message,
            pltpu.VMEM((blocks, heads * rows, LANES), bf16),
            message,
            pltpu.VMEM((blocks, heads * rows, LANES), bf16),
            pltpu.VMEM((GIVE, width, side), bf16),
            dma((2 * parts * width // LANES,)),
            dma((1 + 2 * micro,)),
            dma((width // LANES,)),
            dma((4,)),
            dma((chips + 6 + micro,)),
        ]
        + [dma((blocks,))] * 6
        + [dma((micro,))]
        + Sums.scratch(count, side, side)
        + UnitSum.scratch(chips, side, heads * LANES)
        + UnitSum.scratch(chips, side, 2 * LANES),
        compiler_params=pltpu.CompilerParams(
            collective_id=1, has_side_effects=True, vmem_limit_bytes=63 << 20
        ),
        name="backward",
    )(
        first_gain, second_gain, received, inputs, cotangent, normed,
        qa.reshape(flat), ka.reshape(flat), va.reshape(flat), out,
        query_weight, pair_weight, output_weight, expand_weight, contract_weight,
    )


def finish(final, pair_final, query_final, first_gain, second_gain, query_weight, pair_weight, expand_weight, result, input_grad):
    pieces, width, _ = final.shape
    steps = pieces + 3
    parts = (pieces - 1) // 2
    shape = jax.ShapeDtypeStruct
    square = (width, width)

    def whole(array):
        return pl.BlockSpec(array.shape, lambda p: (0,) * array.ndim)

    def clip(p, start, count):
        return jnp.clip(p - start, 0, count - 1)

    fixed = (first_gain, second_gain)
    later = (pair_final, query_final, query_weight, pair_weight)
    through = (result, input_grad)
    row = pl.BlockSpec((width,), lambda p: (0,))
    return pl.pallas_call(
        final_kernel,
        grid=(steps,),
        out_shape=(
            shape((width,), f32),
            shape(square, f32),
            shape((width, 2 * width), f32),
            shape(square, f32),
            shape((width,), f32),
            shape((width, parts * width), f32),
            shape((parts * width, width), f32),
            shape(result.shape, bf16),
            shape(result.shape, bf16),
        ),
        in_specs=[
            pl.BlockSpec((1,) + square, lambda p: (clip(p, 0, pieces), 0, 0)),
            pl.BlockSpec(square, lambda p: (0, clip(p, parts, parts))),
        ]
        + [whole(array) for array in fixed]
        + [ANY] * 4
        + [whole(array) for array in through],
        out_specs=(
            row,
            pl.BlockSpec(square, lambda p: (0, 0)),
            pl.BlockSpec(square, lambda p: (0, clip(p, 2 * parts + 2, 2))),
            pl.BlockSpec(square, lambda p: (0, 0)),
            row,
            pl.BlockSpec(square, lambda p: (0, clip(p, parts, parts))),
            pl.BlockSpec(square, lambda p: (clip(p, 0, parts), 0)),
            whole(result),
            whole(result),
        ),
        scratch_shapes=[pltpu.VMEM((width, LANES), f32), pltpu.VMEM((width, LANES), f32)]
        + [pltpu.VMEM(array.shape, bf16) for array in later]
        + [pltpu.SemaphoreType.DMA((4,))],
        compiler_params=pltpu.CompilerParams(vmem_limit_bytes=63 << 20),
        name="finish",
    )(final, expand_weight, *fixed, *later, *through)


def layer_norm(value, gain):
    mean = jnp.mean(value, -1, keepdims=True)
    centred = value - mean
    spread = jnp.mean(centred * centred, -1, keepdims=True)
    return centred * lax.rsqrt(spread + epsilon) * gain


def token_info(lengths, views, positions):
    ends = jnp.cumsum(lengths)
    starts = ends - lengths
    inside = (positions[:, None] >= starts[None, :]) & (positions[:, None] < ends[None, :])
    number = jnp.arange(lengths.shape[0], dtype=jnp.int32)
    item = jnp.sum(jnp.where(inside, number[None, :], 0), 1)
    first = jnp.sum(jnp.where(inside, starts[None, :], 0), 1)
    span = jnp.sum(jnp.where(inside, views[None, :], 0), 1) * PATCHES
    frame = (positions - first) // span
    return (item, frame)


def visible(query_pos, query_item, query_frame, key_pos, key_item, key_frame, key_pad):
    same = query_item[:, None] == key_item[None, :]
    order = key_frame[None, :] <= query_frame[:, None]
    usable = (key_pad[None, :] == 1) | (query_pos[:, None] == key_pos[None, :])
    return same & order & usable


def in_blocks(update, carry, piece, block_rows):
    count = piece[0].shape[0]

    def advance(number, inner):
        begin = number * block_rows
        part = (
            lax.dynamic_slice_in_dim(piece[0], begin, block_rows),
            lax.dynamic_slice_in_dim(piece[1], begin, block_rows),
        )
        return update(inner, part, begin)

    return lax.fori_loop(0, count // block_rows, advance, carry)


def score_parts(query_heads, grad_heads, total, shift, key_heads, value_heads, mask, scale):
    scores = (
        jnp.einsum("qhd,khd->hqk", query_heads, key_heads, preferred_element_type=jnp.float32)
        * scale
    )
    chance = jnp.where(mask[None], jnp.exp(scores - total[..., None]), 0.0)
    chance_grad = jnp.einsum(
        "qhd,khd->hqk", grad_heads, value_heads, preferred_element_type=jnp.float32
    )
    score_grad = (chance * (chance_grad - shift[..., None])).astype(jnp.bfloat16)
    return (chance, score_grad)


def on_device(
    inputs,
    cotangent,
    lengths,
    view_counts,
    padding,
    first_gain,
    query_weight,
    key_value_weight,
    output_weight,
    second_gain,
    expand_weight,
    contract_weight,
):
    micro_count, row_count, width = inputs.shape
    head_count = width // HEAD
    scale = HEAD ** (-0.5)
    cycle_size = lax.axis_size("blk")
    own_start = lax.axis_index("blk") * row_count
    query_positions = own_start + jnp.arange(row_count, dtype=jnp.int32)
    gelu = partial(jax.nn.gelu, approximate=True)
    grads = tuple(
        (
            jnp.zeros(array.shape, jnp.float32)
            for array in (
                first_gain,
                query_weight,
                key_value_weight,
                output_weight,
                second_gain,
                expand_weight,
                contract_weight,
            )
        )
    )
    outputs = []
    input_grads = []
    for micro in range(micro_count):
        row_lengths = lengths[micro]
        row_views = view_counts[micro]
        row_pad = padding[micro]
        query_item, query_frame = token_info(row_lengths, row_views, query_positions)
        flat = inputs[micro].astype(jnp.float32)
        normed, first_pull = jax.vjp(layer_norm, flat, first_gain)
        normed_low = normed.astype(jnp.bfloat16)
        query = jnp.dot(normed_low, query_weight, preferred_element_type=jnp.float32).astype(
            jnp.bfloat16
        )
        pair = jnp.dot(normed_low, key_value_weight, preferred_element_type=jnp.float32).astype(
            jnp.bfloat16
        )
        keys = pair[:, :width]
        values = pair[:, width:]
        query_heads = query.reshape(row_count, head_count, HEAD)

        def mask_for(start, count):
            key_positions = start + jnp.arange(count, dtype=jnp.int32)
            key_item, key_frame = token_info(row_lengths, row_views, key_positions)
            key_pad = lax.dynamic_slice_in_dim(row_pad, start, count)
            return visible(
                query_positions,
                query_item,
                query_frame,
                key_positions,
                key_item,
                key_frame,
                key_pad,
            )

        def forward_block(carry, piece, start):
            count = piece[0].shape[0]
            mask = mask_for(start, count)

            def forward_work(state):
                peak, denominator, weighted = state
                key_heads = piece[0].reshape(count, head_count, HEAD)
                value_heads = piece[1].reshape(count, head_count, HEAD)
                scores = (
                    jnp.einsum(
                        "qhd,khd->hqk", query_heads, key_heads, preferred_element_type=jnp.float32
                    )
                    * scale
                )
                scores = jnp.where(mask[None], scores, lowest)
                new_peak = jnp.maximum(peak, jnp.max(scores, -1))
                raised = jnp.where(mask[None], jnp.exp(scores - new_peak[..., None]), 0.0)
                shrink = jnp.exp(peak - new_peak)
                denominator = denominator * shrink + jnp.sum(raised, -1)
                weighted = weighted * shrink[..., None] + jnp.einsum(
                    "hqk,khd->hqd",
                    raised.astype(jnp.bfloat16),
                    value_heads,
                    preferred_element_type=jnp.float32,
                )
                return (new_peak, denominator, weighted)

            return lax.cond(jnp.any(mask), forward_work, lambda state: state, carry)

        initial = (
            jnp.full((head_count, row_count), lowest, jnp.float32),
            jnp.zeros((head_count, row_count), jnp.float32),
            jnp.zeros((head_count, row_count, HEAD), jnp.float32),
        )
        peak, denominator, weighted = in_blocks(
            forward_block,
            initial,
            (
                lax.all_gather(keys, "blk", axis=0, tiled=True),
                lax.all_gather(values, "blk", axis=0, tiled=True),
            ),
            row_count,
        )
        attended_heads = weighted / denominator[..., None]
        log_total = peak + jnp.log(denominator)
        attended_low = (
            jnp.transpose(attended_heads, (1, 0, 2)).reshape(row_count, width).astype(jnp.bfloat16)
        )
        mixed = flat + jnp.dot(attended_low, output_weight, preferred_element_type=jnp.float32)
        second, second_pull = jax.vjp(layer_norm, mixed, second_gain)
        second_low = second.astype(jnp.bfloat16)
        hidden = jnp.dot(second_low, expand_weight, preferred_element_type=jnp.float32)
        activated, gelu_pull = jax.vjp(gelu, hidden)
        activated_low = activated.astype(jnp.bfloat16)
        output = mixed + jnp.dot(activated_low, contract_weight, preferred_element_type=jnp.float32)
        outputs.append(output.astype(jnp.bfloat16))
        upstream = cotangent[micro]
        grad_contract = jnp.einsum(
            "rf,rd->fd", activated_low, upstream, preferred_element_type=jnp.float32
        )
        activated_grad = jnp.einsum(
            "rd,fd->rf", upstream, contract_weight, preferred_element_type=jnp.float32
        )
        hidden_grad = gelu_pull(activated_grad)[0].astype(jnp.bfloat16)
        grad_expand = jnp.einsum(
            "rd,rf->df", second_low, hidden_grad, preferred_element_type=jnp.float32
        )
        second_grad = jnp.einsum(
            "rf,df->rd", hidden_grad, expand_weight, preferred_element_type=jnp.float32
        )
        mixed_part, grad_second = second_pull(second_grad)
        mixed_grad = upstream.astype(jnp.float32) + mixed_part
        branch_grad = mixed_grad.astype(jnp.bfloat16)
        grad_output = jnp.einsum(
            "rd,re->de", attended_low, branch_grad, preferred_element_type=jnp.float32
        )
        attended_grad = jnp.einsum(
            "re,de->rd", branch_grad, output_weight, preferred_element_type=jnp.float32
        ).astype(jnp.bfloat16)
        grad_heads = attended_grad.reshape(row_count, head_count, HEAD)
        delta = jnp.sum(
            jnp.transpose(grad_heads, (1, 0, 2)).astype(jnp.float32) * attended_heads, -1
        )

        def backward_block(carry, piece, start):
            count = piece[0].shape[0]
            mask = mask_for(start, count)

            def backward_work(state):
                query_sum, pair_terms = state
                key_heads = piece[0].reshape(count, head_count, HEAD)
                value_heads = piece[1].reshape(count, head_count, HEAD)
                chance, score_grad = score_parts(
                    query_heads, grad_heads, log_total, delta, key_heads, value_heads, mask, scale
                )
                value_term = jnp.einsum(
                    "hqk,qhd->khd",
                    chance.astype(jnp.bfloat16),
                    grad_heads,
                    preferred_element_type=jnp.float32,
                )
                query_sum = (
                    query_sum
                    + jnp.einsum(
                        "hqk,khd->qhd", score_grad, key_heads, preferred_element_type=jnp.float32
                    )
                    * scale
                )
                key_term = (
                    jnp.einsum(
                        "hqk,qhd->khd", score_grad, query_heads, preferred_element_type=jnp.float32
                    )
                    * scale
                )
                term = jnp.concatenate(
                    [key_term.reshape(count, width), value_term.reshape(count, width)], 1
                )
                previous = lax.dynamic_slice_in_dim(pair_terms, start, count)
                pair_terms = lax.dynamic_update_slice_in_dim(pair_terms, previous + term, start, 0)
                return (query_sum, pair_terms)

            return lax.cond(jnp.any(mask), backward_work, lambda state: state, carry)

        start_back = (
            jnp.zeros((row_count, head_count, HEAD), jnp.float32),
            jnp.zeros((row_count * cycle_size, 2 * width), jnp.float32),
        )
        back_state = in_blocks(
            backward_block,
            start_back,
            (
                lax.all_gather(keys, "blk", axis=0, tiled=True),
                lax.all_gather(values, "blk", axis=0, tiled=True),
            ),
            row_count,
        )
        query_sum, pair_terms = back_state
        pair_grad = lax.psum_scatter(
            pair_terms.astype(jnp.bfloat16), "blk", scatter_dimension=0, tiled=True
        )
        query_grad = query_sum.reshape(row_count, width).astype(jnp.bfloat16)
        grad_query = jnp.einsum(
            "rd,re->de", normed_low, query_grad, preferred_element_type=jnp.float32
        )
        grad_pair = jnp.einsum(
            "rd,re->de", normed_low, pair_grad, preferred_element_type=jnp.float32
        )
        normed_grad = jnp.einsum(
            "re,de->rd", query_grad, query_weight, preferred_element_type=jnp.float32
        )
        normed_grad = normed_grad + jnp.einsum(
            "re,de->rd", pair_grad, key_value_weight, preferred_element_type=jnp.float32
        )
        input_part, grad_first = first_pull(normed_grad)
        input_grads.append((mixed_grad + input_part).astype(jnp.bfloat16))
        terms = (
            grad_first,
            grad_query,
            grad_pair,
            grad_output,
            grad_second,
            grad_expand,
            grad_contract,
        )
        grads = tuple((total + term for total, term in zip(grads, terms)))
    summed = lax.psum(
        (grads[0], grads[1], grads[2], grads[3], grads[4], grads[5], grads[6]), ("dp", "blk")
    )
    return (
        jnp.stack(outputs),
        jnp.stack(input_grads),
        summed[0],
        summed[1],
        summed[2],
        summed[3],
        summed[4],
        summed[5],
        summed[6],
    )


def fast_on_device(
    inputs, cotangent, lengths, view_counts, padding, first_gain, query_weight, key_value_weight,
    output_weight, second_gain, expand_weight, contract_weight,
):
    normed, qa, ka, va, out, received = attention_forward(
        inputs, first_gain, lengths, view_counts, padding, query_weight, key_value_weight, lax.axis_size("blk")
    )
    result, input_grad, final, pair_final, query_final = attention_backward(
        first_gain, second_gain, received, inputs, cotangent, normed, qa, ka, va, out,
        query_weight, key_value_weight, output_weight, expand_weight, contract_weight,
    )
    first, query, pair, output, second, expand, contract, result, input_grad = finish(
        final, pair_final, query_final, first_gain, second_gain, query_weight, key_value_weight, expand_weight,
        result, input_grad,
    )
    return result, input_grad, first, query, pair, output, second, expand, contract


def solution(mesh):
    placed = (
        P("dp", "blk", None),
        P("dp", "blk", None),
        P("dp", None),
        P("dp", None),
        P("dp", None),
    ) + (P(),) * 7

    def program(*arrays):
        inputs, lengths = arrays[0], arrays[2]
        dp, blk = mesh.shape["dp"], mesh.shape["blk"]
        rows, total, width = inputs.shape
        items = lengths.shape[1]
        chips = blk // 2
        fits = (
            (dp, blk) == (4, 8)
            and rows == 2 * dp
            and total % (blk * 2 * LANES) == 0
            and width % (LANES * HEAD // 64) == 0
            and width // HEAD == 3 * chips
            and total // PATCHES + items <= CODES
        )
        return jax.shard_map(
            fast_on_device if fits else on_device,
            mesh=mesh,
            in_specs=placed,
            out_specs=(P("dp", "blk", None), P("dp", "blk", None)) + (P(),) * 7,
            check_vma=False,
        )(*arrays)

    return program
```

```python
from functools import partial

import jax
import jax.numpy as jnp
from jax import lax
from jax.experimental import pallas as pl
from jax.experimental.pallas import tpu as pltpu
from jax.sharding import PartitionSpec as P

HEAD = 64
PATCHES = 64
CODES = 40
BIG = 1e30
EARLY = 12
OUT_AT = (0, 3, 6, 9, 12)
BACK_AT = (0, 3, 6, 9)
LATE = 13
GIVE = 2
PAIR_SLOTS = (18, 23, 28, 31, 34, 35, 28)
QUERY_SLOTS = (36, 37, 38, 39, 40, 40, 31)
PAIR_SUM_SLOTS = (1, 3, 6, 9, 11, 13, 15)
QUERY_SUM_SLOTS = (2, 4, 7, 10, 12, 14, 16)
PAIR_DONE = 40
OUT = (1, 2, 3, 4, 5)
BACK = (6, 7, 8, 9)
LANES = 128
MESH = pl.DeviceIdType.MESH
bf16 = jnp.bfloat16
f32 = jnp.float32

epsilon = 1e-05
lowest = -1e30


def dot_nn(a, b):
    return lax.dot_general(a, b, (((1,), (0,)), ((), ())), preferred_element_type=f32)


def dot_nt(a, b):
    return lax.dot_general(a, b, (((1,), (1,)), ((), ())), preferred_element_type=f32)


def dot_tn(a, b):
    return lax.dot_general(a, b, (((0,), (0,)), ((), ())), preferred_element_type=f32)


def chip_order(z, step):
    code = jnp.where(z == 0, 3210, jnp.where(z == 1, 3201, jnp.where(z == 2, 312, 123)))
    return digit(code, step)


def digit(code, step):
    power = jnp.where(step == 0, 1, jnp.where(step == 1, 10, jnp.where(step == 2, 100, 1000)))
    return lax.rem(code // power, 10)


def chip_span(z, step):
    low = jnp.where(z == 0, 0, jnp.where(z == 1, 1, jnp.where(z == 2, 112, 123)))
    high = jnp.where(z == 0, 3210, jnp.where(z == 1, 3211, jnp.where(z == 2, 3322, 3333)))
    return digit(low, step), digit(high, step)


def far_order(z, step):
    return jnp.where(
        step == 0,
        lax.rem(z + 2, 4),
        jnp.where(step == 1, 3 - z, jnp.where(step == 2, z + 1 - 2 * lax.rem(z, 2), z)),
    )


def features(block, rows, lengths, views, row, padded):
    lane = lax.broadcasted_iota(jnp.int32, (rows, LANES), 1) - HEAD
    position = block * rows + lax.broadcasted_iota(jnp.int32, (rows, LANES), 0)
    code = jnp.zeros((rows, LANES), jnp.int32)
    base = jnp.zeros((rows, LANES), jnp.int32)
    start = jnp.int32(0)
    first = jnp.int32(0)
    for item in range(lengths.shape[1]):
        length = lengths[row, item]
        view = views[row, item]
        offset = position - start
        inside = (offset >= 0) & (offset < length)
        frame = (offset >> 6) * (2 - view) + (offset >> 7) * (view - 1)
        code = jnp.where(inside, first + frame, code)
        base = jnp.where(inside, first, base)
        first = first + ((length + 63) >> 6) * (2 - view) + ((length + 127) >> 7) * (view - 1)
        start = start + length
    coded = (lane >= 0) & (lane < CODES)
    key = jnp.where(coded & (lane == code), 1.0, 0.0)
    key = jnp.where((lane > CODES) & (lane < CODES + 4), 1.0, key)
    key = jnp.where(lane == CODES, padded, key)
    hidden = (coded & ((lane < base) | (lane > code))) | (lane == CODES)
    query = jnp.where(hidden, -BIG, 0.0)
    return key, query


def three_parts(value):
    high = value.astype(bf16).astype(f32)
    rest = value - high
    middle = rest.astype(bf16).astype(f32)
    low = (rest - middle).astype(bf16).astype(f32)
    return high, middle, low


def spread(value, first, lane):
    high, middle, low = three_parts(value)
    return jnp.where(
        lane == first, high, jnp.where(lane == first + 1, middle, jnp.where(lane == first + 2, low, 0.0))
    )


def pack_heads(heads):
    half = heads[2].shape[0] // 2
    wide = jnp.concatenate([heads[0], heads[1]], 1)
    narrow = jnp.concatenate([heads[2][:half], heads[2][half:]], 1)
    return wide, narrow


def greet(dp, me, count, others=()):
    barrier = pltpu.get_barrier_semaphore()
    for step in range(1, count):
        pl.semaphore_signal(
            barrier, inc=1, device_id=(dp, lax.rem(me + step, count)), device_id_type=MESH
        )
    for other in others:
        pl.semaphore_signal(barrier, inc=1, device_id=other, device_id_type=MESH)
    return lambda: pl.semaphore_wait(barrier, count - 1 + len(others))


def heads_of(wide, narrow):
    return [
        wide[:, :HEAD],
        wide[:, HEAD:],
        jnp.concatenate([narrow[:, :HEAD], narrow[:, HEAD:]], 0),
    ]


def columns_of(received, row, rows, blocks):
    pieces = []
    for chip in range(blocks // 2):
        block = 2 * chip + row
        pieces += heads_of(received[block, :rows, :], received[block, rows:, :])
    return jnp.concatenate(pieces, 1)


def normal(value):
    mean = jnp.mean(value, -1, keepdims=True)
    centred = value - mean
    scale = lax.rsqrt(jnp.mean(centred * centred, -1, keepdims=True) + epsilon)
    return centred * scale, scale


def normal_pull(grad, unit, scale):
    return scale * (
        grad - jnp.mean(grad, -1, keepdims=True) - unit * jnp.mean(grad * unit, -1, keepdims=True)
    )


def forward_kernel(
    lengths, views, x_ref, gain_ref, pad_ref, wq_in, wkv_in,
    normed_out, qa_out, ka_out, va_out, o_out, received,
    normed, qa, ka, va, o_ref, weight, wq_ref, wkv_ref, stage, peak, outgoing,
    fetch, sib_send, sib_recv, line_send, line_recv, out_send, out_recv, store,
):
    rows, width = x_ref.shape[1], x_ref.shape[2]
    blocks = normed.shape[0]
    heads = qa.shape[0]
    dp = lax.axis_index("dp")
    me = lax.axis_index("blk")
    z = me // 2
    core = lax.rem(me, 2)
    sibling = me + 1 - 2 * core
    lane = lax.broadcasted_iota(jnp.int32, (rows, LANES), 1)

    arrived = greet(dp, me, blocks)
    loads = [
        pltpu.make_async_copy(wq_in, wq_ref, fetch.at[0]),
        pltpu.make_async_copy(wkv_in, wkv_ref, fetch.at[1]),
    ]
    for copy in loads:
        copy.start()
    gain = gain_ref[...].reshape(1, width)

    def norm(value):
        return (normal(value.astype(f32))[0] * gain).astype(bf16)

    normed[me] = norm(x_ref[core])
    arrived()

    def place(block):
        return pl.ds(pl.multiple_of(block * rows, rows), rows)

    def keep(block, number):
        here = place(block)
        src, dst = (
            (normed.at[block], normed_out.at[block // 2, pl.ds(pl.multiple_of(lax.rem(block, 2) * rows, rows), rows)]),
            (ka.at[:, here, :], ka_out.at[:, here, :]),
            (va.at[:, here, :], va_out.at[:, here, :]),
            (qa.at[:, here, :], qa_out.at[:, here, :]),
            (outgoing.at[block], o_out.at[block]),
        )[number]
        return pltpu.make_async_copy(src, dst, store.at[block, number])

    def line_copy(block, up):
        return pltpu.make_async_remote_copy(
            src_ref=normed.at[block],
            dst_ref=normed.at[block],
            send_sem=line_send.at[block, up],
            recv_sem=line_recv.at[block],
            device_id=(dp, me + (2 if up else -2)),
            device_id_type=MESH,
        )

    @pl.when(z < 3)
    def _():
        line_copy(me, 1).start()

    @pl.when(z > 0)
    def _():
        line_copy(me, 0).start()

    stage[...] = norm(x_ref[1 - core])
    sib_copy = pltpu.make_async_remote_copy(
        src_ref=stage,
        dst_ref=normed.at[me],
        send_sem=sib_send,
        recv_sem=sib_recv,
        device_id=(dp, sibling),
        device_id_type=MESH,
    )
    sib_copy.start()

    for copy in loads:
        copy.wait()
    gap = jnp.zeros((width, LANES - HEAD), bf16)
    for chip in range(blocks // 2):

        @pl.when(z == chip)
        def _():
            for head in range(heads):
                at = (chip * heads + head) * HEAD
                for kind, piece in enumerate(
                    (
                        wq_ref[:, at : at + HEAD],
                        wkv_ref[:, at : at + HEAD],
                        wkv_ref[:, width + at : width + at + HEAD],
                    )
                ):
                    column = (head * 3 + kind) * LANES
                    weight[:, column : column + LANES] = jnp.concatenate([piece, gap], 1)

    ones = jnp.where((lane >= HEAD) & (lane < HEAD + 3), -1.0, 0.0)

    def bring(step, turn):
        chip = chip_order(z, step)
        block = 2 * chip + lax.rem(core + turn, 2)

        @pl.when((step == 0) & (turn == 1))
        def _():
            pltpu.make_async_remote_copy(
                src_ref=stage,
                dst_ref=normed.at[sibling],
                send_sem=sib_send,
                recv_sem=sib_recv,
                device_id=(dp, sibling),
                device_id_type=MESH,
            ).wait_recv()

        @pl.when(step > 0)
        def _():
            pltpu.make_async_remote_copy(
                src_ref=normed.at[block],
                dst_ref=normed.at[block],
                send_sem=line_send.at[block, 0],
                recv_sem=line_recv.at[block],
                device_id=(dp, sibling),
                device_id_type=MESH,
            ).wait_recv()

        @pl.when((step + turn > 0) & (chip <= z) & (z < 3))
        def _():
            line_copy(block, 1).start()

        @pl.when((step + turn > 0) & (chip >= z) & (z > 0))
        def _():
            line_copy(block, 0).start()

        keep(block, 0).start()
        pad_row = 1.0 - pad_ref[pl.ds(core, 1), place(block)].astype(f32)
        padded = jnp.transpose(jnp.broadcast_to(pad_row, (LANES, rows)))
        key, query = features(block, rows, lengths, views, core, padded)
        out = dot_nn(normed[block], weight[...]).astype(bf16).astype(f32)
        here = pl.ds(pl.multiple_of(block * rows, rows), rows)
        for head in range(heads):
            at = head * 3 * LANES
            qa[head, here, :] = (out[:, at : at + LANES] * (HEAD**-0.5) + query).astype(bf16)
            ka[head, here, :] = (out[:, at + LANES : at + 2 * LANES] + key).astype(bf16)
            va[head, here, :] = (out[:, at + 2 * LANES : at + 3 * LANES] + ones).astype(bf16)
            peak[head, here, :] = jnp.full((rows, LANES), -BIG, f32)
            o_ref[head, here, :] = jnp.zeros((rows, LANES), f32)
        keep(block, 1).start()
        keep(block, 2).start()

    wide = 2 * rows
    eye = lax.broadcasted_iota(jnp.int32, (wide, wide), 0) == lax.broadcasted_iota(
        jnp.int32, (wide, wide), 1
    )

    def attend(queries, keys, diagonal=False):
        found = []
        for head in range(heads):
            query = qa[head, queries, :]
            key = ka[head, keys, :]
            s = dot_nt(query, key)
            if diagonal:
                s = jnp.where(eye, dot_nt(query[:, :HEAD], key[:, :HEAD]), s)
            tiles = [s[:, i : i + LANES] for i in range(0, s.shape[1], LANES)]
            top = tiles[0]
            for tile in tiles[1:]:
                top = jnp.maximum(top, tile)
            old = peak[head, queries, :]
            new = jnp.maximum(old, jnp.max(top, -1, keepdims=True))
            p = jnp.concatenate([jnp.exp(tile - new).astype(bf16) for tile in tiles], 1)
            total = o_ref[head, queries, :] * jnp.exp(old - new) + dot_nn(p, va[head, keys, :])
            found.append((new, total))
        for head, (new, total) in enumerate(found):
            peak[head, queries, :] = new
            o_ref[head, queries, :] = total

    def out_copy(block):
        return pltpu.make_async_remote_copy(
            src_ref=outgoing.at[block],
            dst_ref=received.at[me],
            send_sem=out_send.at[block],
            recv_sem=out_recv.at[me],
            device_id=(dp, block),
            device_id_type=MESH,
        )

    def hand_back(chip):
        @pl.loop(0, 2)
        def _(turn):
            block = 2 * chip + lax.rem(core + turn, 2)
            here = pl.ds(pl.multiple_of(block * rows, rows), rows)
            results = []
            for head in range(heads):
                total = o_ref[head, here, :]
                mass = -total[:, HEAD : HEAD + 1]
                results.append((total / mass)[:, :HEAD].astype(bf16))
                log_total = peak[head, here, :] + jnp.log(mass)
                qa[head, here, :] = (
                    qa[head, here, :].astype(f32) - spread(log_total, HEAD + CODES + 1, lane)
                ).astype(bf16)
            both, third = pack_heads(results)
            outgoing[block, :rows, :] = both
            outgoing[block, rows:, :] = third

            @pl.when(block == me)
            def _():
                received[me, :rows, :] = both
                received[me, rows:, :] = third

            @pl.when(block != me)
            def _():
                out_copy(block).start()

            keep(block, 3).start()
            keep(block, 4).start()

    def span(chip):
        return pl.ds(pl.multiple_of(chip * wide, wide), wide)

    def across(chip):
        edge = (chip + 1) * wide
        attend(
            pl.ds(pl.multiple_of(edge - LANES, LANES), LANES),
            pl.ds(pl.multiple_of(edge, LANES), LANES),
        )

    @pl.loop(0, blocks // 2)
    def _(step):
        @pl.loop(0, 2)
        def _(turn):
            bring(step, turn)

        chip = chip_order(z, step)
        low, high = chip_span(z, step)

        @pl.when(chip > low)
        def _():
            across(chip - 1)

        @pl.when(chip < high)
        def _():
            across(chip)

        @pl.when((low == 0) & (chip == high) & (chip > 0))
        def _():
            hand_back(chip - 1)

        @pl.loop(low, high + 1)
        def _(other):
            top = jnp.maximum(chip, other)

            @pl.when(other == chip)
            def _():
                attend(span(chip), span(chip), True)

            @pl.when(other != chip)
            def _():
                attend(span(top), span(jnp.minimum(chip, other)))

            @pl.when((other >= chip) & (low == 0) & (high >= jnp.minimum(top + 1, blocks // 2 - 1)))
            def _():
                hand_back(top)

    sib_copy.wait_send()

    @pl.loop(0, blocks)
    def _(block):
        for number in range(5):
            keep(block, number).wait()

        @pl.when((block // 2 <= z) & (z < 3))
        def _():
            line_copy(block, 1).wait_send()

        @pl.when((block // 2 >= z) & (z > 0))
        def _():
            line_copy(block, 0).wait_send()

        @pl.when(block != me)
        def _():
            out_copy(block).wait_send()
            pltpu.make_async_remote_copy(
                src_ref=outgoing.at[block],
                dst_ref=received.at[block],
                send_sem=out_send.at[block],
                recv_sem=out_recv.at[block],
                device_id=(dp, block),
                device_id_type=MESH,
            ).wait_recv()


class Sums:
    def __init__(self, final, own, buffers, semaphores, local):
        self.final, self.own, self.local = final, own, local
        self.from_core, self.first, self.second, self.line, self.near, self.far = buffers
        self.sems = dict(zip(
            ("core", "first", "second", "inward", "across", "outward", "back", "wide", "twin"), semaphores
        ))
        self.count = own.shape[0]
        self.half, self.lanes = own.shape[1], own.shape[2]
        self.quarter = self.half // 4
        self.eighth = self.half // 8
        self.dp = lax.axis_index("dp")
        self.me = lax.axis_index("blk")
        self.core = lax.rem(self.me, 2)
        self.z = self.me // 2
        self.x = lax.rem(self.dp, 2)
        self.y = self.dp // 2
        self.along_x = (self.dp + 1 - 2 * self.x, self.me)
        self.along_y = (self.dp + 2 - 4 * self.y, self.me)
        self.twin = (self.dp, self.me + 1 - 2 * self.core)
        self.inner = (self.z == 1) | (self.z == 2)
        self.outer = (self.z == 0) | (self.z == 3)
        self.pair = (self.dp, self.me + 2 - 4 * lax.rem(self.z, 2))
        self.middle = (self.dp, jnp.where(self.z < 2, self.me + 2, self.me - 2))

    def copy(self, name, piece, src, dst, device, way=None):
        send, recv = self.sems[name]
        at = (piece,) if way is None else (piece, way)
        return pltpu.make_async_remote_copy(
            src_ref=src,
            dst_ref=dst,
            send_sem=send.at[at],
            recv_sem=recv.at[at],
            device_id=device,
            device_id_type=MESH,
        )

    def rows(self, start, count):
        return pl.ds(pl.multiple_of(start, 16), count)

    def place(self, ref, piece, start, count):
        cols = pl.ds(pl.multiple_of(lax.rem(piece, 2) * self.lanes, LANES), self.lanes)
        return ref.at[piece // 2, self.rows(start, count), cols]

    def to_core(self, piece, src=None):
        src = self.own.at[piece] if src is None else src
        return self.copy("core", piece, src, self.from_core.at[piece], self.twin)

    def to_first(self, piece):
        q = self.quarter
        return (
            self.copy("first", piece, self.own.at[piece, self.rows(q * (1 - self.x), q)], self.first.at[piece, 0], self.along_x, 0),
            self.copy("first", piece, self.own.at[piece, self.rows(2 * q + q * (1 - self.y), q)], self.first.at[piece, 1], self.along_y, 1),
        )

    def to_second(self, piece):
        q, e = self.quarter, self.eighth
        return (
            self.copy("second", piece, self.own.at[piece, self.rows(q * self.x + e * (1 - self.y), e)], self.second.at[piece, 0], self.along_y, 0),
            self.copy("second", piece, self.own.at[piece, self.rows(2 * q + q * self.y + e * (1 - self.x), e)], self.second.at[piece, 1], self.along_x, 1),
        )

    def inward(self, piece):
        return self.copy("inward", piece, self.line.at[piece], self.near.at[piece], self.pair)

    def across(self, piece):
        return self.copy("across", piece, self.line.at[piece], self.far.at[piece], self.middle)

    def outward(self, piece):
        return self.copy("outward", piece, self.far.at[piece], self.near.at[piece], self.pair)

    def mine(self):
        q, e = self.quarter, self.eighth
        base = self.core * self.half
        return base + q * self.x + e * self.y, base + 2 * q + q * self.y + e * self.x

    def keep(self, piece, total):
        e = self.eighth
        one, two = self.mine()
        return (
            pltpu.make_async_copy(total.at[piece, :e], self.place(self.final, piece, one, e), self.local.at[piece, 0]),
            pltpu.make_async_copy(total.at[piece, e:], self.place(self.final, piece, two, e), self.local.at[piece, 1]),
        )

    def back(self, piece, total):
        e = self.eighth
        one, two = self.mine()
        return (
            self.copy("back", piece, total.at[piece, :e], self.place(self.final, piece, one, e), self.along_y, 0),
            self.copy("back", piece, total.at[piece, e:], self.place(self.final, piece, two, e), self.along_x, 1),
        )

    def wide(self, piece):
        q = self.quarter
        base = self.core * self.half
        one = self.place(self.final, piece, base + q * self.x, q)
        two = self.place(self.final, piece, base + 2 * q + q * self.y, q)
        return (
            self.copy("wide", piece, one, one, self.along_x, 0),
            self.copy("wide", piece, two, two, self.along_y, 1),
        )

    def to_twin(self, piece):
        part = self.place(self.final, piece, self.core * self.half, self.half)
        return self.copy("twin", piece, part, part, self.twin)

    def step_1(self, piece):
        self.to_core(piece).wait_recv()
        self.own[piece] = self.own[piece] + self.from_core[piece]
        for copy in self.to_first(piece):
            copy.start()

    def step_2(self, piece):
        q = self.quarter
        one, two = self.to_first(piece)
        one.wait_recv()
        at = self.rows(q * self.x, q)
        self.own[piece, at, :] = self.own[piece, at, :] + self.first[piece, 0]
        two.wait_recv()
        at = self.rows(2 * q + q * self.y, q)
        self.own[piece, at, :] = self.own[piece, at, :] + self.first[piece, 1]
        for copy in self.to_second(piece):
            copy.start()

    def step_3(self, piece):
        q, e = self.quarter, self.eighth
        one, two = self.to_second(piece)
        one.wait_recv()
        at = self.rows(q * self.x + e * self.y, e)
        self.line[piece, :e, :] = self.own[piece, at, :] + self.second[piece, 0]
        two.wait_recv()
        at = self.rows(2 * q + q * self.y + e * self.x, e)
        self.line[piece, e:, :] = self.own[piece, at, :] + self.second[piece, 1]

        @pl.when(self.outer)
        def _():
            self.inward(piece).start()

    def step_4(self, piece):
        @pl.when(self.inner)
        def _():
            self.inward(piece).wait_recv()
            self.line[piece] = self.line[piece] + self.near[piece]
            self.across(piece).start()

    def step_5(self, piece):
        @pl.when(self.inner)
        def _():
            self.across(piece).wait_recv()
            self.far[piece] = self.line[piece] + self.far[piece]
            self.outward(piece).start()

    def step_6(self, piece):
        @pl.when(self.outer)
        def _():
            self.outward(piece).wait_recv()
            for copy in self.back(piece, self.near) + self.keep(piece, self.near):
                copy.start()

        @pl.when(self.inner)
        def _():
            for copy in self.back(piece, self.far) + self.keep(piece, self.far):
                copy.start()

    def step_7(self, piece):
        for copy in self.keep(piece, self.near):
            copy.wait()
        for copy in self.back(piece, self.near):
            copy.wait_recv()
        for copy in self.wide(piece):
            copy.start()

    def step_8(self, piece):
        for copy in self.wide(piece):
            copy.wait_recv()
        self.to_twin(piece).start()

    def step_9(self, piece):
        self.to_twin(piece).wait_recv()

    def tick(self, numbers, offsets, time, last):
        for place in reversed(range(len(numbers))):
            piece = time - offsets[place]

            @pl.when((piece >= 0) & (piece < last))
            def _():
                getattr(self, "step_" + str(numbers[place]))(piece)

    def finish(self, piece):
        for copies in (self.to_first(piece), self.to_second(piece), self.back(piece, self.near), self.wide(piece)):
            for copy in copies:
                copy.wait_send()
        self.to_twin(piece).wait_send()

        @pl.when(self.outer)
        def _():
            self.inward(piece).wait_send()

        @pl.when(self.inner)
        def _():
            self.across(piece).wait_send()
            self.outward(piece).wait_send()

    @staticmethod
    def scratch(count, half, lanes):
        def array(*shape):
            return pltpu.VMEM((count,) + shape + (lanes,), bf16)

        quarter, eighth = half // 4, half // 8
        dma = pltpu.SemaphoreType.DMA
        one, two = [dma((count,))] * 2, [dma((count, 2))] * 2
        return (
            [array(half)] * 2
            + [array(2, quarter), array(2, eighth)]
            + [array(quarter)] * 3
            + one + two + two + one + one + one + two + two + one
            + [dma((count, 2))]
        )

    @classmethod
    def gather(cls, final, refs):
        sems = refs[7:25]
        pairs = [(sems[2 * i], sems[2 * i + 1]) for i in range(9)]
        return cls(final, refs[0], refs[1:7], pairs, refs[25])


class UnitSum:
    def __init__(self, sums, final, refs):
        self.sums, self.final = sums, final
        (
            self.own, self.give, self.from_core, self.first, self.second, self.line,
            self.core_sems, self.first_sems, self.second_sems, self.line_send, self.line_recv,
            self.back_sems, self.wide_sems, self.twin_sems, self.local,
        ) = refs

    def copy(self, sems, at, src, dst, device):
        return pltpu.make_async_remote_copy(
            src_ref=src,
            dst_ref=dst,
            send_sem=sems.at[0, at],
            recv_sem=sems.at[1, at],
            device_id=device,
            device_id_type=MESH,
        )

    def to_core(self):
        return self.copy(self.core_sems, 0, self.give, self.from_core, self.sums.twin)

    def to_first(self):
        s, q = self.sums, self.sums.quarter
        return (
            self.copy(self.first_sems, 0, self.own.at[s.rows(q * (1 - s.x), q)], self.first.at[0], s.along_x),
            self.copy(self.first_sems, 1, self.own.at[s.rows(2 * q + q * (1 - s.y), q)], self.first.at[1], s.along_y),
        )

    def to_second(self):
        s, q, e = self.sums, self.sums.quarter, self.sums.eighth
        return (
            self.copy(self.second_sems, 0, self.own.at[s.rows(q * s.x + e * (1 - s.y), e)], self.second.at[0], s.along_y),
            self.copy(self.second_sems, 1, self.own.at[s.rows(2 * q + q * s.y + e * (1 - s.x), e)], self.second.at[1], s.along_x),
        )

    def along_line(self, chip):
        s = self.sums
        return pltpu.make_async_remote_copy(
            src_ref=self.line.at[s.z],
            dst_ref=self.line.at[s.z],
            send_sem=self.line_send.at[chip],
            recv_sem=self.line_recv.at[s.z],
            device_id=(s.dp, 2 * chip + s.core),
            device_id_type=MESH,
        )

    def from_line(self, chip):
        s = self.sums
        return pltpu.make_async_remote_copy(
            src_ref=self.line.at[chip],
            dst_ref=self.line.at[chip],
            send_sem=self.line_send.at[chip],
            recv_sem=self.line_recv.at[chip],
            device_id=(s.dp, 2 * chip + s.core),
            device_id_type=MESH,
        )

    def keep(self):
        s, e = self.sums, self.sums.eighth
        one, two = s.mine()
        return (
            pltpu.make_async_copy(self.line.at[:, :e], self.final.at[:, s.rows(one, e)], self.local.at[0]),
            pltpu.make_async_copy(self.line.at[:, e:], self.final.at[:, s.rows(two, e)], self.local.at[1]),
        )

    def back(self):
        s, e = self.sums, self.sums.eighth
        one, two = s.mine()
        return (
            self.copy(self.back_sems, 0, self.line.at[:, :e], self.final.at[:, s.rows(one, e)], s.along_y),
            self.copy(self.back_sems, 1, self.line.at[:, e:], self.final.at[:, s.rows(two, e)], s.along_x),
        )

    def wide(self):
        s, q = self.sums, self.sums.quarter
        base = s.core * s.half
        one = self.final.at[:, s.rows(base + q * s.x, q)]
        two = self.final.at[:, s.rows(base + 2 * q + q * s.y, q)]
        return (
            self.copy(self.wide_sems, 0, one, one, s.along_x),
            self.copy(self.wide_sems, 1, two, two, s.along_y),
        )

    def to_twin(self):
        s = self.sums
        part = self.final.at[:, s.rows(s.core * s.half, s.half)]
        return self.copy(self.twin_sems, 0, part, part, s.twin)

    def step(self, number):
        s, q, e = self.sums, self.sums.quarter, self.sums.eighth
        if number == 0:
            self.to_core().start()
        elif number == 1:
            self.to_core().wait_recv()
            self.own[...] = self.own[...] + self.from_core[...]
            for copy in self.to_first():
                copy.start()
        elif number == 2:
            for way, start in ((0, q * s.x), (1, 2 * q + q * s.y)):
                self.to_first()[way].wait_recv()
                at = s.rows(start, q)
                self.own[at, :] = self.own[at, :] + self.first[way]
            for copy in self.to_second():
                copy.start()
        elif number == 3:
            for way, start in ((0, q * s.x + e * s.y), (1, 2 * q + q * s.y + e * s.x)):
                self.to_second()[way].wait_recv()
                self.line[s.z, way * e : (way + 1) * e, :] = self.own[s.rows(start, e), :] + self.second[way]
            for ahead in (2, 1, 3):
                self.along_line(lax.rem(s.z + ahead, 4)).start()
        elif number == 4:
            for ahead in (1, 2, 3):
                self.from_line(lax.rem(s.z + ahead, 4)).wait_recv()
            for copy in self.back() + self.keep():
                copy.start()
        elif number == 5:
            for copy in self.keep():
                copy.wait()
            for copy in self.back():
                copy.wait_recv()
            for copy in self.wide():
                copy.start()
        elif number == 6:
            for copy in self.wide():
                copy.wait_recv()
            self.to_twin().start()
        else:
            self.to_twin().wait_recv()

    def finish(self):
        s = self.sums
        for copy in (self.to_core(), self.to_twin()) + self.to_first() + self.to_second() + self.back() + self.wide():
            copy.wait_send()
        for ahead in (1, 2, 3):
            self.along_line(lax.rem(s.z + ahead, 4)).wait_send()

    @staticmethod
    def scratch(chips, half, lanes):
        dma = pltpu.SemaphoreType.DMA
        quarter, eighth = half // 4, half // 8
        array = [pltpu.VMEM((half, lanes), bf16)]
        return (
            array * 3
            + [
                pltpu.VMEM((2, quarter, lanes), bf16),
                pltpu.VMEM((2, eighth, lanes), bf16),
                pltpu.VMEM((chips, quarter, lanes), bf16),
                dma((2, 1)),
                dma((2, 2)),
                dma((2, 2)),
                dma((chips,)),
                dma((chips,)),
                dma((2, 2)),
                dma((2, 2)),
                dma((2, 1)),
                dma((2,)),
            ]
        )


def backward_kernel(
    first_gain, second_gain, received_in, x_in, up_in, normed_in, qa_in, ka_in, va_in, o_in,
    wq_in, wkv_in, wo_in, we_in, wc_in,
    result_ref, input_grad, final, pair_final, query_final,
    acts, pool, result_acc, second_acc, out, grad_out, received, key_turned, dqt, dvk, send_query, send_pair,
    got_query, got_pair, give,
    load_tiles, load_first, load_output, load_heads, load_late, out_send, out_recv, query_send, query_recv, pair_send, pair_recv,
    save, *sum_refs,
):
    blocks, packed = grad_out.shape[0], grad_out.shape[1]
    rows = 2 * packed // 3
    micro, _, width = input_grad.shape
    heads, _, total = key_turned.shape
    chips = blocks // 2
    tall = acts.shape[1]
    tiles = width // LANES
    dp = lax.axis_index("dp")
    me = lax.axis_index("blk")
    z = me // 2
    core = lax.rem(me, 2)
    lane = lax.broadcasted_iota(jnp.int32, (rows, LANES), 1)
    sums = Sums.gather(final, sum_refs[:26])
    pair_sum = UnitSum(sums, pair_final, sum_refs[26:41])
    query_sum = UnitSum(sums, query_final, sum_refs[41:])
    count = sums.count
    parts = (count // 2 - 1) // 2
    low, up, attended, branch = 2 * parts, 2 * parts + 1, 2 * parts + 2, 2 * parts + 3
    arrived = greet(dp, me, blocks, (sums.along_x, sums.along_y))

    at_query, at_key, at_value, at_grad, at_right = (number * heads * total for number in range(5))

    def in_pool(base, head, start, size):
        return pl.ds(pl.multiple_of(base + head * total + start, LANES), size)

    def fetch(number):
        part = number % parts
        copies = []
        for tile in range(tiles):
            if number < parts:
                src = we_in.at[:, pl.ds(part * width + tile * LANES, LANES)]
            else:
                src = wc_in.at[pl.ds(part * width, width), pl.ds(tile * LANES, LANES)]
            place = number * tiles + tile
            copies.append(
                pltpu.make_async_copy(src, pool.at[pl.ds(place * width, width)], load_tiles.at[place])
            )
        return copies

    def weight(number):
        return jnp.concatenate(
            [pool[pl.ds(pl.multiple_of((number * tiles + tile) * width, LANES), width), :] for tile in range(tiles)], 1
        )

    def openers():
        copies = [
            pltpu.make_async_copy(received_in, send_query, load_first.at[0]),
        ]
        for tile in range(tiles):
            src = wo_in.at[:, pl.ds(tile * LANES, LANES)]
            copies.append(pltpu.make_async_copy(src, send_pair.at[tile], load_output.at[tile]))
        for row in range(micro):
            here = pl.ds(row * rows, rows)
            copies.append(pltpu.make_async_copy(x_in.at[row], acts.at[branch, here], load_first.at[1 + 2 * row]))
            copies.append(pltpu.make_async_copy(up_in.at[row], acts.at[up, here], load_first.at[2 + 2 * row]))
        return copies

    def load_head(number):
        src = (qa_in, ka_in, va_in, o_in)[number]
        base = (at_query, at_key, at_value)
        dst = out if number == 3 else pool.at[pl.ds(base[number], heads * total)]
        return pltpu.make_async_copy(src, dst, load_heads.at[number])

    for copy in openers():
        copy.start()
    for part in range(parts):
        for copy in fetch(part) + fetch(parts + part):
            copy.start()

    kinds = {
        "grad": (grad_out, received, out_send, out_recv),
        "query": (send_query, got_query, query_send, query_recv),
        "pair": (send_pair, got_pair, pair_send, pair_recv),
    }

    def send(kind, block):
        src, dst, send_sem, recv_sem = kinds[kind]
        return pltpu.make_async_remote_copy(
            src_ref=src.at[block],
            dst_ref=dst.at[me],
            send_sem=send_sem.at[block],
            recv_sem=recv_sem.at[me],
            device_id=(dp, block),
            device_id_type=MESH,
        )

    def arrive(kind, block):
        src, dst, send_sem, recv_sem = kinds[kind]
        return pltpu.make_async_remote_copy(
            src_ref=src.at[block],
            dst_ref=dst.at[block],
            send_sem=send_sem.at[block],
            recv_sem=recv_sem.at[block],
            device_id=(dp, block),
            device_id_type=MESH,
        )

    def message(number):
        return 2 * far_order(z, number // 2) + lax.rem(core + number, 2)

    def slot(time):
        for kind, starts in (("pair", PAIR_SLOTS), ("query", QUERY_SLOTS)):
            for number, start in enumerate(starts):
                block = message(jnp.int32(2 * chips - 1 if number == 2 * chips - 2 else number))

                @pl.when(time == start)
                def _():
                    send(kind, block).start()

        sums.tick(BACK, BACK_AT, time - LATE, count)
        sums.tick(OUT, OUT_AT, time, count)

    side = sums.half

    def weigh(piece):
        whole = piece // 2
        left = jnp.where(whole < parts, whole, jnp.where(whole < 2 * parts, low, attended))
        right = jnp.where(whole < parts, up, jnp.where(whole < 2 * parts, whole, branch))
        cols = pl.ds(pl.multiple_of(lax.rem(piece, 2) * side, LANES), side)
        turn = lax.rem(piece, GIVE)

        theirs = pl.ds(pl.multiple_of((1 - core) * side, 16), side)
        ours = pl.ds(pl.multiple_of(core * side, 16), side)

        @pl.when(piece >= GIVE)
        def _():
            sums.to_core(piece - GIVE, give.at[turn, theirs]).wait_send()

        give[turn] = dot_tn(acts[left], acts[right, :, cols]).astype(bf16)
        sums.to_core(piece, give.at[turn, theirs]).start()
        sums.own[piece] = give[turn, ours, :]

    def output():
        return jnp.concatenate([send_pair[tile] for tile in range(tiles)], 1)

    opening = openers()
    gain = second_gain[...].reshape(1, width)
    opening[0].wait()
    for row in range(micro):
        acts[attended, row * rows : (row + 1) * rows, :] = columns_of(send_query, row, rows, blocks)
    for copy in opening[1:]:
        copy.wait()
    for row in range(micro):
        at = slice(row * rows, (row + 1) * rows)
        value = acts[branch, at, :].astype(f32) + dot_nn(acts[attended, at, :], output())
        result_acc[at, :] = value
        acts[low, at, :] = (normal(value)[0] * gain).astype(bf16)
    second_acc[...] = jnp.zeros_like(second_acc)

    def through(part, row):
        at = slice(row * rows, (row + 1) * rows)
        widen, narrow = weight(part), weight(parts + part)
        hidden = dot_nn(acts[low, at, :], widen)
        active_grad = dot_nt(acts[up, at, :], narrow)
        square = hidden * hidden
        c = 0.7978845608028654
        bend = jnp.tanh(hidden * (c + 0.044715 * c * square))
        gate = 0.5 + 0.5 * bend
        slope = gate + 0.5 * hidden * (1.0 - bend * bend) * (c + 3.0 * 0.044715 * c * square)
        active = (hidden * gate).astype(bf16)
        grad = (active_grad * slope).astype(bf16)
        acts[part, at, :] = active
        acts[parts + part, at, :] = grad
        result_acc[at, :] += dot_nn(active, narrow)
        second_acc[at, :] += dot_nt(grad, widen)

    def turn_back(row):
        at = slice(row * rows, (row + 1) * rows)
        result_ref[row] = result_acc[at, :].astype(bf16)
        project = output()
        value = acts[branch, at, :].astype(f32) + dot_nn(acts[attended, at, :], project)
        unit_, scale = normal(value)
        grad = acts[up, at, :].astype(f32) + normal_pull(second_acc[at, :] * gain, unit_, scale)
        second_acc[at, :] = grad
        acts[branch, at, :] = grad.astype(bf16)
        back = dot_nt(acts[branch, at, :], project).astype(bf16)
        for chip in range(chips):
            start = chip * heads * HEAD
            wide, narrow = pack_heads(
                [back[:, start + h * HEAD : start + (h + 1) * HEAD] for h in range(heads)]
            )
            grad_out[2 * chip + row, :rows, :] = wide
            grad_out[2 * chip + row, rows:, :] = narrow
        for step in range(chips):
            block = 2 * far_order(z, jnp.int32(step)) + row

            @pl.when(block != me)
            def _():
                send("grad", block).start()

    for part in range(parts):
        for copy in fetch(part) + fetch(parts + part):
            copy.wait()
        through(part, 0)
    arrived()
    turn_back(0)

    @pl.loop(0, parts)
    def _(part):
        through(part, 1)
        for turn in range(2):
            weigh(2 * part + turn)

            @pl.when(part > 0)
            def _():
                slot(2 * part - 2 + turn)

    turn_back(1)
    received[me] = grad_out[me]
    for number in range(4):
        load_head(number).start()

    for number in range(2 * parts - 2, 2 * parts):
        slot(jnp.int32(number))

    @pl.loop(2 * parts, count)
    def _(piece):
        weigh(piece)

        @pl.when((lax.rem(piece, 2) == 1) & (piece > 2 * parts + 1))
        def _():
            slot(2 * parts + (piece - 2 * parts - 3) // 2)

    squares = [(wq_in, 0), (wkv_in, 0), (wkv_in, width)]

    def late():
        copies = [
            pltpu.make_async_copy(normed_in.at[chip], acts.at[chip], load_late.at[chip]) for chip in range(chips)
        ]
        for number, (src, start) in enumerate(squares):
            cols = pl.ds(start, width)
            copies.append(
                pltpu.make_async_copy(
                    src.at[pl.ds(0, tall), cols], acts.at[chips + 2 * number], load_late.at[chips + 2 * number]
                )
            )
            copies.append(
                pltpu.make_async_copy(
                    src.at[pl.ds(tall, width - tall), cols],
                    acts.at[chips + 2 * number + 1, pl.ds(0, width - tall)],
                    load_late.at[chips + 2 * number + 1],
                )
            )
        for row in range(micro):
            copies.append(
                pltpu.make_async_copy(
                    x_in.at[row],
                    acts.at[chips + 6, pl.ds(row * rows, rows)],
                    load_late.at[chips + 6 + row],
                )
            )
        return copies

    for copy in late():
        copy.start()

    dqt[...] = jnp.zeros_like(dqt)
    for number in range(4):
        load_head(number).wait()

    @pl.loop(0, blocks)
    def _(block):
        here = pl.ds(pl.multiple_of(block * rows, rows), rows)
        for head in range(heads):
            key = pool[in_pool(at_key, head, block * rows, rows), :][:, :HEAD].astype(f32)
            key_turned[head, :, here] = jnp.transpose(key).astype(bf16)
            query = pool[in_pool(at_query, head, block * rows, rows), :][:, :HEAD]
            pool[in_pool(at_right, head, block * rows, rows), :] = jnp.concatenate([jnp.zeros_like(query), query], 1)

    @pl.loop(0, blocks)
    def _(step):
        block = 2 * chip_order(z, step // 2) + lax.rem(core + step, 2)

        @pl.when(block != me)
        def _():
            arrive("grad", block).wait_recv()

        wide = received[block, :rows, :].astype(f32)
        narrow = received[block, rows:, :].astype(f32)
        shares = heads_of(wide * out[block, :rows, :].astype(f32), narrow * out[block, rows:, :].astype(f32))
        gap = jnp.zeros((rows, LANES - HEAD), f32)
        for head, piece in enumerate(heads_of(wide, narrow)):
            delta = jnp.sum(shares[head], -1, keepdims=True)
            value = jnp.concatenate([piece, gap], 1)
            pool[in_pool(at_grad, head, block * rows, rows), :] = (value + spread(delta, HEAD, lane)).astype(bf16)

    wide_rows = 2 * rows
    eye = lax.broadcasted_iota(jnp.int32, (wide_rows, wide_rows), 0) == lax.broadcasted_iota(
        jnp.int32, (wide_rows, wide_rows), 1
    )
    half = LANES

    def pull(keys, queries, diagonal=False):
        found = []
        for head in range(heads):
            k = pool[in_pool(at_key, head, *keys), :]
            q = pool[in_pool(at_query, head, *queries), :]
            g = pool[in_pool(at_grad, head, *queries), :]
            at = lax.broadcasted_iota(jnp.int32, k.shape, 1)
            s = dot_nt(k, q)
            if diagonal:
                bare = (at < HEAD) | (at > HEAD + CODES)
                s = jnp.where(eye, dot_nt(jnp.where(bare, k, 0.0).astype(bf16), q), s)
            p = jnp.exp(s)
            ds = (p * dot_nt(pool[in_pool(at_value, head, *keys), :], g)).astype(bf16)
            left = jnp.concatenate([p.astype(bf16), ds], 1)
            at = lax.broadcasted_iota(jnp.int32, g.shape, 1)
            value = jnp.where(at < HEAD, g, 0.0).astype(bf16)
            right = jnp.concatenate([value, pool[in_pool(at_right, head, *queries), :]], 0)
            turned = key_turned[head, :, pl.ds(pl.multiple_of(keys[0], LANES), keys[1])]
            found.append((dot_nn(left, right), dot_nn(turned, ds)))
        return found

    @pl.loop(0, chips)
    def _(step):
        chip = far_order(z, step)
        span = (chip * wide_rows, wide_rows)
        here = pl.ds(pl.multiple_of(chip * wide_rows, wide_rows), wide_rows)
        for head, (pair, query) in enumerate(pull(span, span, True)):
            dvk[head] = pair
            dqt[head, :, here] += query
        time = EARLY
        for earlier in range(chips - 1):
            done = far_order(z, earlier)
            bodies = chips - done + jnp.where(done > 0, 1, 0)
            time = time + jnp.where(earlier < step, bodies, 0)
        slot(time)

        @pl.loop(chip + 1, chips)
        def _(other):
            there = pl.ds(pl.multiple_of(other * wide_rows, wide_rows), wide_rows)
            for head, (pair, query) in enumerate(pull(span, (other * wide_rows, wide_rows))):
                dvk[head] += pair
                dqt[head, :, there] += query
            slot(time + other - chip)

        @pl.when(chip > 0)
        def _():
            edge = chip * wide_rows
            queries = pl.ds(pl.multiple_of(edge - half, half), half)
            for head, (pair, query) in enumerate(pull((edge, half), (edge - half, half))):
                dvk[head, :half] += pair
                dqt[head, :, queries] += query
            slot(time + chips - chip)

        for turn in range(2):
            block = 2 * chip + turn
            for head in range(heads):
                send_pair[block, head * rows : (head + 1) * rows, :] = dvk[
                    head, turn * rows : (turn + 1) * rows
                ].astype(bf16)

            @pl.when(block == me)
            def _():
                got_pair[me] = send_pair[me]

    for copy in late():
        copy.wait()

    def columns(tile):
        right = jnp.concatenate([jnp.concatenate(tile(block), 1) for block in range(blocks)], 0)
        for unit, which in (("give", 1 - core), ("own", core)):
            cols = pl.ds(pl.multiple_of(which * side, LANES), side)
            left = acts[:chips, :, cols].reshape(total, side)
            yield unit, dot_tn(left, right).astype(bf16)

    for unit, value in columns(
        lambda block: [send_pair[block, head * rows : (head + 1) * rows, :] for head in range(heads)]
    ):
        getattr(pair_sum, unit)[...] = value
        if unit == "give":
            pair_sum.step(0)
    slot(jnp.int32(EARLY + 13))

    @pl.loop(0, blocks)
    def _(block):
        here = pl.ds(pl.multiple_of(block * rows, rows), rows)
        wide, narrow = pack_heads(
            [(jnp.transpose(dqt[h, :, here]) * (HEAD**-0.5)).astype(bf16) for h in range(heads)]
        )
        send_query[block, :rows, :] = wide
        send_query[block, rows:, :] = narrow

        @pl.when(block == me)
        def _():
            got_query[me] = send_query[me]

    gap = jnp.zeros((rows, LANES - HEAD), bf16)
    for unit, value in columns(
        lambda block: heads_of(send_query[block, :rows, :], send_query[block, rows:, :]) + [gap]
    ):
        getattr(query_sum, unit)[...] = value
        if unit == "give":
            query_sum.step(0)
    slot(jnp.int32(EARLY + 14))

    ready = EARLY + 15
    end = LATE + count + BACK_AT[-1]

    def normed_part(row, operands, first):
        grad = []
        for part in range(2):
            height = tall if part == 0 else width - tall
            total_ = jnp.zeros((rows, height), f32)
            for number, operand in enumerate(operands):
                total_ = total_ + dot_nt(operand, acts[chips + 2 * (first + number) + part, :height])
            grad.append(total_)
        return jnp.concatenate(grad, 1)

    def pair_part(row):
        keys, values = [], []
        for chip in range(chips):
            for head in range(heads):
                both = got_pair[2 * chip + row, head * rows : (head + 1) * rows, :]
                keys.append(both[:, HEAD:])
                values.append(both[:, :HEAD])
        operands = [jnp.concatenate(keys, 1), jnp.concatenate(values, 1)]
        result_acc[row * rows : (row + 1) * rows, :] = normed_part(row, operands, 1)

    def last(row):
        at = slice(row * rows, (row + 1) * rows)
        grad = result_acc[at, :] + normed_part(row, [columns_of(got_query, row, rows, blocks)], 0)
        unit_, scale = normal(acts[chips + 6, at, :].astype(f32))
        pulled = normal_pull(grad * first_gain[...].reshape(1, width), unit_, scale)
        acts[chips + 7, at, :] = (second_acc[at, :] + pulled).astype(bf16)
        return pltpu.make_async_copy(acts.at[chips + 7, pl.ds(row * rows, rows)], input_grad.at[row], save.at[row])

    def wait_for(kind):
        @pl.loop(0, blocks)
        def _(block):
            @pl.when(block != me)
            def _():
                arrive(kind, block).wait_recv()

    @pl.loop(ready, max(end, ready + max(PAIR_SUM_SLOTS + QUERY_SUM_SLOTS) + 1))
    def _(time):
        for unit, places in ((pair_sum, PAIR_SUM_SLOTS), (query_sum, QUERY_SUM_SLOTS)):
            for number, place in enumerate(places):

                @pl.when(time == ready + place)
                def _():
                    unit.step(number + 1)

        slot(time)

        @pl.when(time == PAIR_DONE)
        def _():
            wait_for("pair")
            for row in range(micro):
                pair_part(row)

    wait_for("query")
    saves = [last(row) for row in range(micro)]
    for copy in saves:
        copy.start()

    @pl.loop(0, blocks)
    def _(block):
        @pl.when(block != me)
        def _():
            send("grad", block).wait_send()
            send("query", block).wait_send()
            send("pair", block).wait_send()

    theirs = pl.ds(pl.multiple_of((1 - core) * side, 16), side)
    for piece in range(count - GIVE, count):
        sums.to_core(piece, give.at[piece % GIVE, theirs]).wait_send()

    @pl.loop(0, count)
    def _(piece):
        sums.finish(piece)

    pair_sum.finish()
    query_sum.finish()
    for copy in saves:
        copy.wait()


def final_kernel(
    final, we_ref, first_gain, second_gain, pair_in, query_in, wq_in, wkv_in, result_in, grad_in,
    first_ref, query_ref, pair_ref, output_ref, second_ref, expand_ref, contract_ref, result_out, grad_out,
    first_acc, second_acc, pair_unit, query_unit, wq_ref, wkv_ref, fetch,
):
    step = pl.program_id(0)
    width = wq_ref.shape[0]
    chips = pair_in.shape[0]
    heads = width // HEAD // chips
    parts = (pl.num_programs(0) - 4) // 2

    def fold(array):
        return sum(array[:, i : i + LANES] for i in range(0, width, LANES))

    def loads():
        pairs = ((pair_in, pair_unit), (query_in, query_unit), (wq_in, wq_ref), (wkv_in, wkv_ref))
        return [pltpu.make_async_copy(src, dst, fetch.at[i]) for i, (src, dst) in enumerate(pairs)]

    @pl.when(step == 0)
    def _():
        for copy in loads():
            copy.start()
        first_acc[...] = jnp.zeros_like(first_acc)
        second_acc[...] = jnp.zeros_like(second_acc)

    @pl.when(step == 1)
    def _():
        result_out[...] = result_in[...]
        grad_out[...] = grad_in[...]

    @pl.when(step < parts)
    def _():
        contract_ref[...] = final[0].astype(f32)

    @pl.when((step >= parts) & (step < 2 * parts))
    def _():
        value = final[0].astype(f32)
        expand_ref[...] = value
        second_acc[...] += fold(value * we_ref[...].astype(f32))

    @pl.when(step == 2 * parts)
    def _():
        output_ref[...] = final[0].astype(f32)

    def columns(unit, place):
        return jnp.concatenate(
            [unit[chip][:, place(head) : place(head) + HEAD] for chip in range(chips) for head in range(heads)], 1
        ).astype(f32)

    @pl.when(step == 2 * parts + 1)
    def _():
        for copy in loads():
            copy.wait()
        value = columns(query_unit, lambda head: head * HEAD)
        query_ref[...] = value
        first_acc[...] += fold(value * wq_ref[...].astype(f32))

    for side in range(2):

        @pl.when(step == 2 * parts + 2 + side)
        def _():
            value = columns(pair_unit, lambda head: head * LANES + (HEAD if side == 0 else 0))
            pair_ref[...] = value
            first_acc[...] += fold(value * wkv_ref[:, side * width : (side + 1) * width].astype(f32))

    @pl.when(step == pl.num_programs(0) - 1)
    def _():
        first_ref[...] = jnp.sum(jnp.transpose(first_acc[...]), 0) / first_gain[...]
        second_ref[...] = jnp.sum(jnp.transpose(second_acc[...]), 0) / second_gain[...]


VMEM = pl.BlockSpec(memory_space=pltpu.VMEM)
SMEM = pl.BlockSpec(memory_space=pltpu.SMEM)
ANY = pl.BlockSpec(memory_space=pl.ANY)


def attention_forward(inputs, gain, lengths, views, padding, query_weight, pair_weight, blocks):
    micro, rows, width = inputs.shape
    total = rows * blocks
    heads = width // HEAD // (blocks // micro)
    packed = rows * heads // 2
    shape = jax.ShapeDtypeStruct
    dma = pltpu.SemaphoreType.DMA
    unit = (heads, total, LANES)
    return pl.pallas_call(
        forward_kernel,
        out_shape=(
            shape((blocks // 2, 2 * rows, width), bf16),
            shape(unit, bf16),
            shape(unit, bf16),
            shape(unit, bf16),
            shape((blocks, packed, LANES), bf16),
            shape((blocks, packed, LANES), bf16),
        ),
        in_specs=[SMEM, SMEM] + [VMEM] * 3 + [ANY] * 2,
        out_specs=(ANY,) * 5 + (VMEM,),
        scratch_shapes=[
            pltpu.VMEM((blocks, rows, width), bf16),
            pltpu.VMEM(unit, bf16),
            pltpu.VMEM(unit, bf16),
            pltpu.VMEM(unit, bf16),
            pltpu.VMEM(unit, f32),
            pltpu.VMEM((width, heads * 3 * LANES), bf16),
            pltpu.VMEM(query_weight.shape, bf16),
            pltpu.VMEM(pair_weight.shape, bf16),
            pltpu.VMEM((rows, width), bf16),
            pltpu.VMEM(unit, f32),
            pltpu.VMEM((blocks, packed, LANES), bf16),
            dma((2,)),
            dma,
            dma,
            dma((blocks, 2)),
            dma((blocks,)),
            dma((blocks,)),
            dma((blocks,)),
            dma((blocks, 5)),
        ],
        compiler_params=pltpu.CompilerParams(
            collective_id=0, has_side_effects=True, vmem_limit_bytes=63 << 20
        ),
        name="attention_forward",
    )(lengths, views, inputs, gain, padding, query_weight, pair_weight)


def attention_backward(
    first_gain, second_gain, received, inputs, cotangent, normed, qa, ka, va, out,
    query_weight, pair_weight, output_weight, expand_weight, contract_weight,
):
    micro, rows, width = inputs.shape
    blocks, packed, _ = received.shape
    heads, total, _ = qa.shape
    chips = blocks // 2
    tokens = micro * rows
    parts = expand_weight.shape[1] // width
    pieces = 2 * parts + 1
    count = 2 * pieces
    side = width // 2
    flat = (heads * total, LANES)
    shape = jax.ShapeDtypeStruct
    dma = pltpu.SemaphoreType.DMA
    message = pltpu.VMEM((blocks, packed, LANES), bf16)
    return pl.pallas_call(
        backward_kernel,
        out_shape=(
            shape(inputs.shape, bf16),
            shape(inputs.shape, bf16),
            shape((pieces, width, width), bf16),
            shape((chips, width, heads * LANES), bf16),
            shape((chips, width, 2 * LANES), bf16),
        ),
        in_specs=[VMEM] * 2 + [ANY] * 13,
        out_specs=(VMEM, ANY, ANY, ANY, ANY),
        scratch_shapes=[
            pltpu.VMEM((2 * parts + 4, tokens, width), bf16),
            pltpu.VMEM((2 * parts * width // LANES * width, LANES), bf16),
            pltpu.VMEM((tokens, width), f32),
            pltpu.VMEM((tokens, width), f32),
            message,
            message,
            message,
            pltpu.VMEM((heads, HEAD, total), bf16),
            pltpu.VMEM((heads, HEAD, total), f32),
            pltpu.VMEM((heads, 2 * rows, LANES), f32),
            message,
            pltpu.VMEM((blocks, heads * rows, LANES), bf16),
            message,
            pltpu.VMEM((blocks, heads * rows, LANES), bf16),
            pltpu.VMEM((GIVE, width, side), bf16),
            dma((2 * parts * width // LANES,)),
            dma((1 + 2 * micro,)),
            dma((width // LANES,)),
            dma((4,)),
            dma((chips + 6 + micro,)),
        ]
        + [dma((blocks,))] * 6
        + [dma((micro,))]
        + Sums.scratch(count, side, side)
        + UnitSum.scratch(chips, side, heads * LANES)
        + UnitSum.scratch(chips, side, 2 * LANES),
        compiler_params=pltpu.CompilerParams(
            collective_id=1, has_side_effects=True, vmem_limit_bytes=63 << 20
        ),
        name="backward",
    )(
        first_gain, second_gain, received, inputs, cotangent, normed,
        qa.reshape(flat), ka.reshape(flat), va.reshape(flat), out,
        query_weight, pair_weight, output_weight, expand_weight, contract_weight,
    )


def finish(final, pair_final, query_final, first_gain, second_gain, query_weight, pair_weight, expand_weight, result, input_grad):
    pieces, width, _ = final.shape
    steps = pieces + 3
    parts = (pieces - 1) // 2
    shape = jax.ShapeDtypeStruct
    square = (width, width)

    def whole(array):
        return pl.BlockSpec(array.shape, lambda p: (0,) * array.ndim)

    def clip(p, start, count):
        return jnp.clip(p - start, 0, count - 1)

    fixed = (first_gain, second_gain)
    later = (pair_final, query_final, query_weight, pair_weight)
    through = (result, input_grad)
    row = pl.BlockSpec((width,), lambda p: (0,))
    return pl.pallas_call(
        final_kernel,
        grid=(steps,),
        out_shape=(
            shape((width,), f32),
            shape(square, f32),
            shape((width, 2 * width), f32),
            shape(square, f32),
            shape((width,), f32),
            shape((width, parts * width), f32),
            shape((parts * width, width), f32),
            shape(result.shape, bf16),
            shape(result.shape, bf16),
        ),
        in_specs=[
            pl.BlockSpec((1,) + square, lambda p: (clip(p, 0, pieces), 0, 0)),
            pl.BlockSpec(square, lambda p: (0, clip(p, parts, parts))),
        ]
        + [whole(array) for array in fixed]
        + [ANY] * 4
        + [whole(array) for array in through],
        out_specs=(
            row,
            pl.BlockSpec(square, lambda p: (0, 0)),
            pl.BlockSpec(square, lambda p: (0, clip(p, 2 * parts + 2, 2))),
            pl.BlockSpec(square, lambda p: (0, 0)),
            row,
            pl.BlockSpec(square, lambda p: (0, clip(p, parts, parts))),
            pl.BlockSpec(square, lambda p: (clip(p, 0, parts), 0)),
            whole(result),
            whole(result),
        ),
        scratch_shapes=[pltpu.VMEM((width, LANES), f32), pltpu.VMEM((width, LANES), f32)]
        + [pltpu.VMEM(array.shape, bf16) for array in later]
        + [pltpu.SemaphoreType.DMA((4,))],
        compiler_params=pltpu.CompilerParams(vmem_limit_bytes=63 << 20),
        name="finish",
    )(final, expand_weight, *fixed, *later, *through)


def layer_norm(value, gain):
    mean = jnp.mean(value, -1, keepdims=True)
    centred = value - mean
    spread = jnp.mean(centred * centred, -1, keepdims=True)
    return centred * lax.rsqrt(spread + epsilon) * gain


def token_info(lengths, views, positions):
    ends = jnp.cumsum(lengths)
    starts = ends - lengths
    inside = (positions[:, None] >= starts[None, :]) & (positions[:, None] < ends[None, :])
    number = jnp.arange(lengths.shape[0], dtype=jnp.int32)
    item = jnp.sum(jnp.where(inside, number[None, :], 0), 1)
    first = jnp.sum(jnp.where(inside, starts[None, :], 0), 1)
    span = jnp.sum(jnp.where(inside, views[None, :], 0), 1) * PATCHES
    frame = (positions - first) // span
    return (item, frame)


def visible(query_pos, query_item, query_frame, key_pos, key_item, key_frame, key_pad):
    same = query_item[:, None] == key_item[None, :]
    order = key_frame[None, :] <= query_frame[:, None]
    usable = (key_pad[None, :] == 1) | (query_pos[:, None] == key_pos[None, :])
    return same & order & usable


def in_blocks(update, carry, piece, block_rows):
    count = piece[0].shape[0]

    def advance(number, inner):
        begin = number * block_rows
        part = (
            lax.dynamic_slice_in_dim(piece[0], begin, block_rows),
            lax.dynamic_slice_in_dim(piece[1], begin, block_rows),
        )
        return update(inner, part, begin)

    return lax.fori_loop(0, count // block_rows, advance, carry)


def score_parts(query_heads, grad_heads, total, shift, key_heads, value_heads, mask, scale):
    scores = (
        jnp.einsum("qhd,khd->hqk", query_heads, key_heads, preferred_element_type=jnp.float32)
        * scale
    )
    chance = jnp.where(mask[None], jnp.exp(scores - total[..., None]), 0.0)
    chance_grad = jnp.einsum(
        "qhd,khd->hqk", grad_heads, value_heads, preferred_element_type=jnp.float32
    )
    score_grad = (chance * (chance_grad - shift[..., None])).astype(jnp.bfloat16)
    return (chance, score_grad)


def on_device(
    inputs,
    cotangent,
    lengths,
    view_counts,
    padding,
    first_gain,
    query_weight,
    key_value_weight,
    output_weight,
    second_gain,
    expand_weight,
    contract_weight,
):
    micro_count, row_count, width = inputs.shape
    head_count = width // HEAD
    scale = HEAD ** (-0.5)
    cycle_size = lax.axis_size("blk")
    own_start = lax.axis_index("blk") * row_count
    query_positions = own_start + jnp.arange(row_count, dtype=jnp.int32)
    gelu = partial(jax.nn.gelu, approximate=True)
    grads = tuple(
        (
            jnp.zeros(array.shape, jnp.float32)
            for array in (
                first_gain,
                query_weight,
                key_value_weight,
                output_weight,
                second_gain,
                expand_weight,
                contract_weight,
            )
        )
    )
    outputs = []
    input_grads = []
    for micro in range(micro_count):
        row_lengths = lengths[micro]
        row_views = view_counts[micro]
        row_pad = padding[micro]
        query_item, query_frame = token_info(row_lengths, row_views, query_positions)
        flat = inputs[micro].astype(jnp.float32)
        normed, first_pull = jax.vjp(layer_norm, flat, first_gain)
        normed_low = normed.astype(jnp.bfloat16)
        query = jnp.dot(normed_low, query_weight, preferred_element_type=jnp.float32).astype(
            jnp.bfloat16
        )
        pair = jnp.dot(normed_low, key_value_weight, preferred_element_type=jnp.float32).astype(
            jnp.bfloat16
        )
        keys = pair[:, :width]
        values = pair[:, width:]
        query_heads = query.reshape(row_count, head_count, HEAD)

        def mask_for(start, count):
            key_positions = start + jnp.arange(count, dtype=jnp.int32)
            key_item, key_frame = token_info(row_lengths, row_views, key_positions)
            key_pad = lax.dynamic_slice_in_dim(row_pad, start, count)
            return visible(
                query_positions,
                query_item,
                query_frame,
                key_positions,
                key_item,
                key_frame,
                key_pad,
            )

        def forward_block(carry, piece, start):
            count = piece[0].shape[0]
            mask = mask_for(start, count)

            def forward_work(state):
                peak, denominator, weighted = state
                key_heads = piece[0].reshape(count, head_count, HEAD)
                value_heads = piece[1].reshape(count, head_count, HEAD)
                scores = (
                    jnp.einsum(
                        "qhd,khd->hqk", query_heads, key_heads, preferred_element_type=jnp.float32
                    )
                    * scale
                )
                scores = jnp.where(mask[None], scores, lowest)
                new_peak = jnp.maximum(peak, jnp.max(scores, -1))
                raised = jnp.where(mask[None], jnp.exp(scores - new_peak[..., None]), 0.0)
                shrink = jnp.exp(peak - new_peak)
                denominator = denominator * shrink + jnp.sum(raised, -1)
                weighted = weighted * shrink[..., None] + jnp.einsum(
                    "hqk,khd->hqd",
                    raised.astype(jnp.bfloat16),
                    value_heads,
                    preferred_element_type=jnp.float32,
                )
                return (new_peak, denominator, weighted)

            return lax.cond(jnp.any(mask), forward_work, lambda state: state, carry)

        initial = (
            jnp.full((head_count, row_count), lowest, jnp.float32),
            jnp.zeros((head_count, row_count), jnp.float32),
            jnp.zeros((head_count, row_count, HEAD), jnp.float32),
        )
        peak, denominator, weighted = in_blocks(
            forward_block,
            initial,
            (
                lax.all_gather(keys, "blk", axis=0, tiled=True),
                lax.all_gather(values, "blk", axis=0, tiled=True),
            ),
            row_count,
        )
        attended_heads = weighted / denominator[..., None]
        log_total = peak + jnp.log(denominator)
        attended_low = (
            jnp.transpose(attended_heads, (1, 0, 2)).reshape(row_count, width).astype(jnp.bfloat16)
        )
        mixed = flat + jnp.dot(attended_low, output_weight, preferred_element_type=jnp.float32)
        second, second_pull = jax.vjp(layer_norm, mixed, second_gain)
        second_low = second.astype(jnp.bfloat16)
        hidden = jnp.dot(second_low, expand_weight, preferred_element_type=jnp.float32)
        activated, gelu_pull = jax.vjp(gelu, hidden)
        activated_low = activated.astype(jnp.bfloat16)
        output = mixed + jnp.dot(activated_low, contract_weight, preferred_element_type=jnp.float32)
        outputs.append(output.astype(jnp.bfloat16))
        upstream = cotangent[micro]
        grad_contract = jnp.einsum(
            "rf,rd->fd", activated_low, upstream, preferred_element_type=jnp.float32
        )
        activated_grad = jnp.einsum(
            "rd,fd->rf", upstream, contract_weight, preferred_element_type=jnp.float32
        )
        hidden_grad = gelu_pull(activated_grad)[0].astype(jnp.bfloat16)
        grad_expand = jnp.einsum(
            "rd,rf->df", second_low, hidden_grad, preferred_element_type=jnp.float32
        )
        second_grad = jnp.einsum(
            "rf,df->rd", hidden_grad, expand_weight, preferred_element_type=jnp.float32
        )
        mixed_part, grad_second = second_pull(second_grad)
        mixed_grad = upstream.astype(jnp.float32) + mixed_part
        branch_grad = mixed_grad.astype(jnp.bfloat16)
        grad_output = jnp.einsum(
            "rd,re->de", attended_low, branch_grad, preferred_element_type=jnp.float32
        )
        attended_grad = jnp.einsum(
            "re,de->rd", branch_grad, output_weight, preferred_element_type=jnp.float32
        ).astype(jnp.bfloat16)
        grad_heads = attended_grad.reshape(row_count, head_count, HEAD)
        delta = jnp.sum(
            jnp.transpose(grad_heads, (1, 0, 2)).astype(jnp.float32) * attended_heads, -1
        )

        def backward_block(carry, piece, start):
            count = piece[0].shape[0]
            mask = mask_for(start, count)

            def backward_work(state):
                query_sum, pair_terms = state
                key_heads = piece[0].reshape(count, head_count, HEAD)
                value_heads = piece[1].reshape(count, head_count, HEAD)
                chance, score_grad = score_parts(
                    query_heads, grad_heads, log_total, delta, key_heads, value_heads, mask, scale
                )
                value_term = jnp.einsum(
                    "hqk,qhd->khd",
                    chance.astype(jnp.bfloat16),
                    grad_heads,
                    preferred_element_type=jnp.float32,
                )
                query_sum = (
                    query_sum
                    + jnp.einsum(
                        "hqk,khd->qhd", score_grad, key_heads, preferred_element_type=jnp.float32
                    )
                    * scale
                )
                key_term = (
                    jnp.einsum(
                        "hqk,qhd->khd", score_grad, query_heads, preferred_element_type=jnp.float32
                    )
                    * scale
                )
                term = jnp.concatenate(
                    [key_term.reshape(count, width), value_term.reshape(count, width)], 1
                )
                previous = lax.dynamic_slice_in_dim(pair_terms, start, count)
                pair_terms = lax.dynamic_update_slice_in_dim(pair_terms, previous + term, start, 0)
                return (query_sum, pair_terms)

            return lax.cond(jnp.any(mask), backward_work, lambda state: state, carry)

        start_back = (
            jnp.zeros((row_count, head_count, HEAD), jnp.float32),
            jnp.zeros((row_count * cycle_size, 2 * width), jnp.float32),
        )
        back_state = in_blocks(
            backward_block,
            start_back,
            (
                lax.all_gather(keys, "blk", axis=0, tiled=True),
                lax.all_gather(values, "blk", axis=0, tiled=True),
            ),
            row_count,
        )
        query_sum, pair_terms = back_state
        pair_grad = lax.psum_scatter(
            pair_terms.astype(jnp.bfloat16), "blk", scatter_dimension=0, tiled=True
        )
        query_grad = query_sum.reshape(row_count, width).astype(jnp.bfloat16)
        grad_query = jnp.einsum(
            "rd,re->de", normed_low, query_grad, preferred_element_type=jnp.float32
        )
        grad_pair = jnp.einsum(
            "rd,re->de", normed_low, pair_grad, preferred_element_type=jnp.float32
        )
        normed_grad = jnp.einsum(
            "re,de->rd", query_grad, query_weight, preferred_element_type=jnp.float32
        )
        normed_grad = normed_grad + jnp.einsum(
            "re,de->rd", pair_grad, key_value_weight, preferred_element_type=jnp.float32
        )
        input_part, grad_first = first_pull(normed_grad)
        input_grads.append((mixed_grad + input_part).astype(jnp.bfloat16))
        terms = (
            grad_first,
            grad_query,
            grad_pair,
            grad_output,
            grad_second,
            grad_expand,
            grad_contract,
        )
        grads = tuple((total + term for total, term in zip(grads, terms)))
    summed = lax.psum(
        (grads[0], grads[1], grads[2], grads[3], grads[4], grads[5], grads[6]), ("dp", "blk")
    )
    return (
        jnp.stack(outputs),
        jnp.stack(input_grads),
        summed[0],
        summed[1],
        summed[2],
        summed[3],
        summed[4],
        summed[5],
        summed[6],
    )


def fast_on_device(
    inputs, cotangent, lengths, view_counts, padding, first_gain, query_weight, key_value_weight,
    output_weight, second_gain, expand_weight, contract_weight,
):
    normed, qa, ka, va, out, received = attention_forward(
        inputs, first_gain, lengths, view_counts, padding, query_weight, key_value_weight, lax.axis_size("blk")
    )
    result, input_grad, final, pair_final, query_final = attention_backward(
        first_gain, second_gain, received, inputs, cotangent, normed, qa, ka, va, out,
        query_weight, key_value_weight, output_weight, expand_weight, contract_weight,
    )
    first, query, pair, output, second, expand, contract, result, input_grad = finish(
        final, pair_final, query_final, first_gain, second_gain, query_weight, key_value_weight, expand_weight,
        result, input_grad,
    )
    return result, input_grad, first, query, pair, output, second, expand, contract


def solution(mesh):
    placed = (
        P("dp", "blk", None),
        P("dp", "blk", None),
        P("dp", None),
        P("dp", None),
        P("dp", None),
    ) + (P(),) * 7

    def program(*arrays):
        inputs, lengths = arrays[0], arrays[2]
        dp, blk = mesh.shape["dp"], mesh.shape["blk"]
        rows, total, width = inputs.shape
        items = lengths.shape[1]
        chips = blk // 2
        fits = (
            (dp, blk) == (4, 8)
            and rows == 2 * dp
            and total % (blk * 2 * LANES) == 0
            and width % (LANES * HEAD // 64) == 0
            and width // HEAD == 3 * chips
            and total // PATCHES + items <= CODES
        )
        return jax.shard_map(
            fast_on_device if fits else on_device,
            mesh=mesh,
            in_specs=placed,
            out_specs=(P("dp", "blk", None), P("dp", "blk", None)) + (P(),) * 7,
            check_vma=False,
        )(*arrays)

    return program
```
